32 devices in a mesh: seq: 8 (over y, x, core), hid: 4 (over z).
Axes of the slice: x: 2, y: 2, z: 4, core: 2. Of those that a mesh axis runs over, the one named last changes fastest.
Arguments:
- tokens_in: bfloat16 [32, 1024, 768], P('hid', 'seq'), may hold values from -6 to 6
- image_lengths: int32 [32, 64], P('hid'), may hold values from 0 to 1024, as said below
- attn_weight: float32 [3072, 768], P('hid')
- attn_moment: float32 [3072, 768], P('hid'), may hold values from -512 to 512
- attn_average: float32 [3072, 768], P('hid')
- mlp_weight: float32 [2, 3072, 768], P(None, 'hid'), may hold values from -0.21875 to 0.21875
- mlp_moment: float32 [2, 3072, 768], P(None, 'hid'), may hold values from -512 to 512
- mlp_average: float32 [2, 3072, 768], P(None, 'hid'), may hold values from -0.21875 to 0.21875
- vector_params: float32 [12, 768], replicated
- vector_moment: float32 [12, 768], replicated, may hold values from -512 to 512
- vector_average: float32 [12, 768], replicated
- out_grad: bfloat16 [32, 1024, 768], P('hid', 'seq'), may hold values from -6 to 6
Outputs:
- block_out: float32 [32, 1024, 768], P('hid', 'seq')
- input_grad: float32 [32, 1024, 768], P('hid', 'seq')
- attn_grad: float32 [3072, 768], P('hid')
- attn_moment_new: float32 [3072, 768], P('hid')
- attn_weight_new: float32 [3072, 768], P('hid')
- attn_average_new: float32 [3072, 768], P('hid')
- mlp_grad: float32 [2, 3072, 768], P(None, 'hid')
- mlp_moment_new: float32 [2, 3072, 768], P(None, 'hid')
- mlp_weight_new: float32 [2, 3072, 768], P(None, 'hid')
- mlp_average_new: float32 [2, 3072, 768], P(None, 'hid')
- vector_grad: float32 [12, 768], replicated
- vector_moment_new: float32 [12, 768], replicated
- vector_params_new: float32 [12, 768], replicated
- vector_average_new: float32 [12, 768], replicated
The draws below stay inside these ranges and needn't reach their ends.
Inputs may be any that keep to these rules, and one draw needn't show every extreme that they name: `image_lengths`: the nonzero entries of a row come first; a row sums to between 897 and 1024, and the positions after its sum are padding. Among the 8 rows of each index of hid, one holds a single image of 1024 patches.
All inputs are finite; a program needn't handle non-finite values.
Results may differ from the reference program's by a relative error of at most 0.019.
Values may be sent and summed in bfloat16 or wider, within the bound.
No kernel may reach another device: no remote copies, remote signals or barrier semaphores. Data moves between devices by JAX's collectives and lax.ppermute only.
A program may use at most 320 MiB of HBM per device.

```python
import math
import jax
import jax.numpy as jnp
from jax import lax

D = 768
HEADS = 12
HEAD_DIM = 64
FF = 3072
LEN = 1024
SLOTS = 64
PACKS = 8
POS_DEV = 128
HPACK = 32
TOKENS = 32768
VROWS = 12
N_HID = 4


def projection_scale():
    row_number = jnp.arange(4 * D)
    return jnp.where(row_number < 3 * D, 1.0, 4.0)[:, None] * (1.0 / math.sqrt(D))


def vector_rows(base):
    row_number = jnp.arange(VROWS)[:, None]
    gain_rows = (row_number == 0) | (row_number == 5)
    return jnp.where(gain_rows, 1.0 + 0.2 * base, 0.3 * base)


def draw_image_lengths(key, part):
    key = jax.random.fold_in(key, 11)
    subkeys = jax.random.split(key, 5)
    first_factor = jax.random.randint(subkeys[0], (HPACK,), 0, SLOTS)
    second_factor = jax.random.randint(subkeys[1], (HPACK,), 0, SLOTS)
    image_count = jnp.minimum(1 + first_factor * second_factor // SLOTS, 60)
    padding = jax.random.randint(subkeys[2], (HPACK,), 0, POS_DEV)
    chosen = jax.random.randint(subkeys[3], (N_HID,), 0, PACKS)
    pack_ids = jnp.arange(HPACK)
    owner = pack_ids // PACKS
    spanning = pack_ids == owner * PACKS + chosen[owner]
    image_count = jnp.where(spanning, 1, image_count)
    padding = jnp.where(spanning, 0, padding)
    used_total = LEN - padding
    image_count = jnp.minimum(image_count, used_total)
    cut_points = jnp.arange(1, LEN)
    ranking = jax.random.randint(subkeys[4], (HPACK, LEN - 1), 0, 1 << 20) * LEN + cut_points[None, :]
    ranking = jnp.where(cut_points[None, :] < used_total[:, None], ranking, 2147483647)
    ordered = jnp.sort(ranking, axis=1)[:, :SLOTS - 1] % LEN
    taken = jnp.arange(SLOTS - 1)[None, :] < (image_count - 1)[:, None]
    cuts = jnp.sort(jnp.where(taken, ordered, used_total[:, None]), axis=1)
    bounds = jnp.concatenate([jnp.zeros((HPACK, 1), jnp.int32), cuts.astype(jnp.int32), used_total[:, None].astype(jnp.int32)], axis=1)
    return (bounds[:, 1:] - bounds[:, :-1]).astype(jnp.int32)


def draw_attn_weight(key, part):
    key = jax.random.fold_in(key, 21)
    base = jax.random.normal(key, (4 * D, D), jnp.float32)
    return base * projection_scale()


def draw_attn_average(key, part):
    key = jax.random.fold_in(key, 22)
    base = jax.random.normal(key, (4 * D, D), jnp.float32)
    return base * projection_scale()


def draw_vector_params(key, part):
    key = jax.random.fold_in(key, 31)
    base = jnp.clip(jax.random.normal(key, (VROWS, D), jnp.float32), -3.0, 3.0)
    return vector_rows(base)


def draw_vector_average(key, part):
    key = jax.random.fold_in(key, 32)
    base = jnp.clip(jax.random.normal(key, (VROWS, D), jnp.float32), -3.0, 3.0)
    return vector_rows(base)


def levels(rng, shape, cuts, least, high):
    loudness = 1.0
    for axis_at, shards_of in cuts:
        steps = jax.random.uniform(jax.random.fold_in(jax.random.fold_in(rng, 6), axis_at), (shards_of,), jnp.float32, least / len(cuts), high / len(cuts))
        loudness = loudness * jnp.repeat(jnp.exp(steps), shape[axis_at] // shards_of).reshape((-1,) + (1,) * (len(shape) - 1 - axis_at))
    return loudness


def normal_values(rng, dims, scale, reach, cuts=(), kind=jnp.bfloat16):
    level = levels(rng, dims, cuts, -0.22, 0.18) if cuts else 1.0
    entries = jax.random.normal(rng, dims, jnp.float32) * scale * level
    return jnp.minimum(jnp.maximum(entries, -reach), reach).astype(kind)


def setup_inputs(seed: int = 0) -> dict:
    splits = jax.random.split(jax.random.key(seed), 13)
    return {
        "tokens_in": normal_values(splits[0], (HPACK, LEN, D), 1.0, 6.0, ((0, 4), (1, 8))),
        "image_lengths": draw_image_lengths(jax.random.fold_in(splits[12], 71), 0),
        "attn_weight": draw_attn_weight(jax.random.fold_in(splits[12], 71), 0),
        "attn_moment": normal_values(splits[3], (4 * D, D), (0.5 * TOKENS ** 0.5), 512.0, ((0, 4),), jnp.float32),
        "attn_average": draw_attn_average(jax.random.fold_in(splits[12], 71), 0),
        "mlp_weight": normal_values(splits[5], (2, FF, D), D ** -0.5, 0.21875, ((1, 4),), jnp.float32),
        "mlp_moment": normal_values(splits[6], (2, FF, D), (0.5 * TOKENS ** 0.5), 512.0, ((1, 4),), jnp.float32),
        "mlp_average": normal_values(splits[7], (2, FF, D), D ** -0.5, 0.21875, ((1, 4),), jnp.float32),
        "vector_params": draw_vector_params(jax.random.fold_in(splits[12], 71), 0),
        "vector_moment": normal_values(splits[9], (VROWS, D), (0.5 * TOKENS ** 0.5), 512.0, (), jnp.float32),
        "vector_average": draw_vector_average(jax.random.fold_in(splits[12], 71), 0),
        "out_grad": normal_values(splits[11], (HPACK, LEN, D), 1.0, 6.0, ((0, 4), (1, 8))),
    }


@jax.custom_vjp
def low(v):
    return lax.optimization_barrier(v.astype(jnp.bfloat16)).astype(jnp.float32)

@jax.custom_vjp
def low_back(v):
    return v

def low_keep(v):
    return (low(v), None)

def low_pass(kept, grad):
    return (grad,)

def back_keep(v):
    return (v, None)

def back_low(kept, grad):
    return (low(grad),)
low.defvjp(low_keep, low_pass)
low_back.defvjp(back_keep, back_low)
score_scale = 0.125
norm_eps = 1e-06
big_negative = -1e+30
matrix_rate = 0.0001
vector_rate = 0.001
momentum_decay = 0.9
weight_decay = 0.0001
average_decay = 0.9

def normalize(inputs, gain_row, offset):
    center = inputs - lax.optimization_barrier(jnp.mean(inputs, axis=-1, keepdims=True))
    spread = lax.optimization_barrier(jnp.mean(center * center, axis=-1, keepdims=True))
    return center * lax.rsqrt(spread + norm_eps) * gain_row + offset

def renew(weight, moment, average, gradient, decay_rate, step_rate):
    step_grad = gradient + decay_rate * weight
    moment_new = momentum_decay * moment + step_grad
    weight_new = weight - step_rate * (step_grad + momentum_decay * moment_new)
    average_new = average_decay * average + (1.0 - average_decay) * weight_new
    return (gradient, moment_new, weight_new, average_new)

def reference(tokens_in, image_lengths, attn_weight, attn_moment, attn_average, mlp_weight, mlp_moment, mlp_average, vector_params, vector_moment, vector_average, out_grad):
    highest = lax.Precision.HIGHEST
    total_packs, seq_length, model_width = tokens_in.shape
    group_size = math.gcd(total_packs, max(1, 2048 // seq_length))
    positions = jnp.arange(seq_length, dtype=jnp.int32)
    image_ends = jnp.cumsum(image_lengths, axis=1)
    segments = lax.optimization_barrier(jnp.sum((image_ends[:, None, :] <= positions[None, :, None]).astype(jnp.int32), axis=2))
    valid_rows = (positions[None, :] < image_ends[:, -1:]).astype(jnp.float32)

    def forward(inputs, attn_params, mlp_params, table):
        wide_low = low(attn_params)
        mlp_low = low(mlp_params)
        w_qkv = wide_low[:3 * model_width]
        w_out = wide_low[3 * model_width:]
        hidden_bias = table[8:].reshape(-1)

        def one_group(items):
            group_in, group_seg, group_valid = items
            head_shape = group_in.shape[:2] + (HEADS, HEAD_DIM)
            first_low = low(normalize(group_in, table[0], table[1]))
            projected = jnp.einsum('gtd,ed->gte', first_low, w_qkv, precision=highest)
            queries = low(low_back(projected[..., :model_width] + table[2]))
            keys_low = low(low_back(projected[..., model_width:2 * model_width]))
            values_low = low(low_back(projected[..., 2 * model_width:] + table[3]))
            scores = jnp.einsum('gqhd,gkhd->gqhk', queries.reshape(head_shape), keys_low.reshape(head_shape), precision=highest)
            scores = low_back(scores * score_scale)
            same_image = group_seg[:, :, None, None] == group_seg[:, None, None, :]
            scores = jnp.where(same_image, scores, big_negative)
            shifted = scores - lax.optimization_barrier(jnp.max(scores, axis=-1, keepdims=True))
            weights = jnp.exp(shifted)
            probs = low(weights / lax.optimization_barrier(jnp.sum(weights, axis=-1, keepdims=True)))
            mixed = jnp.einsum('gqhk,gkhd->gqhd', probs, values_low.reshape(head_shape), precision=highest)
            mixed = low(low_back(mixed.reshape(group_in.shape) * group_valid[..., None]))
            branch = low_back(jnp.einsum('gtd,ed->gte', mixed, w_out, precision=highest) + table[4])
            residual = group_in + branch
            second_low = low(normalize(residual, table[5], table[6]))
            before = low_back(jnp.einsum('gtd,fd->gtf', second_low, mlp_low[0], precision=highest) + hidden_bias)
            active = low(jax.nn.gelu(before, approximate=False))
            mlp_out = jnp.einsum('gtf,fd->gtd', active, mlp_low[1], precision=highest) + table[7]
            return residual + mlp_out

        def shaped(array):
            return array.reshape((total_packs // group_size, group_size) + array.shape[1:])
        outputs = lax.map(jax.checkpoint(one_group), (shaped(inputs), shaped(segments), shaped(valid_rows)))
        return outputs.reshape(inputs.shape)
    block_out, pullback = jax.vjp(forward, tokens_in.astype(jnp.float32), attn_weight, mlp_weight, vector_params)
    input_grad, attn_grad, mlp_grad, vector_grad = pullback(out_grad.astype(jnp.float32))
    attn_new = renew(attn_weight, attn_moment, attn_average, attn_grad, weight_decay, matrix_rate)
    mlp_new = renew(mlp_weight, mlp_moment, mlp_average, mlp_grad, weight_decay, matrix_rate)
    vector_new = renew(vector_params, vector_moment, vector_average, vector_grad, 0.0, vector_rate)
    return (block_out, input_grad, attn_new[0], attn_new[1], attn_new[2], attn_new[3], mlp_new[0], mlp_new[1], mlp_new[2], mlp_new[3], vector_new[0], vector_new[1], vector_new[2], vector_new[3])
```

```python
import functools

import jax
import jax.numpy as jnp
from jax import lax
from jax.experimental import pallas as pl
from jax.experimental.pallas import tpu as pltpu
from jax.sharding import PartitionSpec as P

HEADS = 12
HEAD_DIM = 64

score_scale = 0.125
norm_eps = 1e-06
big_negative = -1e30
matrix_rate = 0.0001
vector_rate = 0.001
momentum_decay = 0.9
weight_decay = 0.0001
average_decay = 0.9

low = jnp.bfloat16
wide = jnp.float32
kernel_vmem = 56 * 1024 * 1024


def rows_by_rows(a, b):
    return lax.dot_general(a, b, (((1,), (1,)), ((), ())), preferred_element_type=wide)


def rows_by_cols(a, b):
    return lax.dot_general(a, b, (((1,), (0,)), ((), ())), preferred_element_type=wide)


def cols_by_cols(a, b):
    return lax.dot_general(a, b, (((0,), (0,)), ((), ())), preferred_element_type=wide)


def normalize(inputs, gain_row, offset):
    center = inputs - jnp.mean(inputs, axis=-1, keepdims=True)
    spread = jnp.mean(center * center, axis=-1, keepdims=True)
    return center * lax.rsqrt(spread + norm_eps) * gain_row + offset


def renew(weight, moment, average, gradient, decay_rate, step_rate):
    step_grad = gradient + decay_rate * weight
    moment_new = momentum_decay * moment + step_grad
    weight_new = weight - step_rate * (step_grad + momentum_decay * moment_new)
    average_new = average_decay * average + (1.0 - average_decay) * weight_new
    return (gradient, moment_new, weight_new, average_new)


def params(**kwargs):
    return pltpu.CompilerParams(vmem_limit_bytes=kernel_vmem, **kwargs)


def smem():
    return pl.BlockSpec(memory_space=pltpu.SMEM)


def whole_vmem():
    return pl.BlockSpec(memory_space=pltpu.VMEM)


def attention_forward_kernel(
    tile, q_ref, k_ref, v_ref, query_seg, key_seg, valid_ref, o_ref, lse_ref
):
    rows = q_ref.shape[0]
    lane = lax.broadcasted_iota(jnp.int32, (1, 128), 1)
    k = k_ref[...]
    v = v_ref[...]
    v_and_ones = jnp.concatenate([v, jnp.ones_like(v)], axis=1)
    for start in range(0, rows, tile):
        part = pl.ds(start, tile)
        q = q_ref[part, :]
        same = query_seg[part, :] == key_seg[...]
        heads = []
        for head in range(2):
            mine = (lane // HEAD_DIM) == head
            scores = rows_by_rows(jnp.where(mine, q, jnp.zeros_like(q)), k)
            scores = jnp.where(same, scores, big_negative)
            top = jnp.max(scores, axis=1, keepdims=True)
            weights = jnp.exp(scores - top).astype(low)
            sums = rows_by_cols(weights, v_and_ones)
            total = sums[:, 128:]
            heads.append(sums[:, :128] / total)
            lse_ref[0, head : head + 1, part] = jnp.transpose(top + jnp.log(total))[:1, :]
        joined = jnp.where(lane < HEAD_DIM, heads[0], heads[1]) * valid_ref[part, :]
        o_ref[part, :] = joined.astype(low)


def attention_forward(q, k, v, query_seg, key_seg, valid):
    rows, width = q.shape
    keys = k.shape[0]
    pairs = width // 128
    column = lambda n: pl.BlockSpec((n, 128), lambda g: (0, g))
    whole = lambda a: pl.BlockSpec(a.shape, lambda g: (0, 0))
    return pl.pallas_call(
        functools.partial(attention_forward_kernel, min(128, rows)),
        grid=(pairs,),
        in_specs=[
            column(rows),
            column(keys),
            column(keys),
            whole(query_seg),
            whole(key_seg),
            whole(valid),
        ],
        out_specs=[column(rows), pl.BlockSpec((1, 2, rows), lambda g: (g, 0, 0))],
        out_shape=[
            jax.ShapeDtypeStruct((rows, width), low),
            jax.ShapeDtypeStruct((pairs, 2, rows), wide),
        ],
        compiler_params=params(),
        cost_estimate=pl.CostEstimate(
            flops=20 * rows * keys * width,
            bytes_accessed=8 * rows * width,
            transcendentals=rows * keys * pairs * 2,
        ),
        name="attention_forward",
    )(q, k, v, query_seg, key_seg, valid)


def attention_backward_kernel(
    tile,
    q_ref,
    k_ref,
    v_ref,
    do_ref,
    lse_ref,
    delta_ref,
    query_seg,
    key_seg,
    dq_ref,
    dk_ref,
    dv_ref,
    dk_sum,
    dv_sum,
):
    rows = q_ref.shape[0]
    lane = lax.broadcasted_iota(jnp.int32, (1, 128), 1)
    k = k_ref[...]
    v = v_ref[...]
    for start in range(0, rows, tile):
        part = pl.ds(start, tile)
        q = q_ref[part, :]
        do = do_ref[part, :]
        same = key_seg[...] == query_seg[:, part]
        heads = []
        dk = 0.0
        dv = 0.0
        for head in range(2):
            mine = (lane // HEAD_DIM) == head
            q_head = jnp.where(mine, q, jnp.zeros_like(q))
            do_head = jnp.where(mine, do, jnp.zeros_like(do))
            scores = jnp.where(same, rows_by_rows(k, q_head), big_negative)
            probs = jnp.exp(scores - lse_ref[0, head : head + 1, part])
            grads = rows_by_rows(v, do_head)
            grads = (probs * (grads - delta_ref[0, head : head + 1, part])).astype(low)
            dv = dv + rows_by_cols(probs.astype(low), do_head)
            dk = dk + rows_by_cols(grads, q_head)
            heads.append(cols_by_cols(grads, k))
        joined = jnp.where(lane < HEAD_DIM, heads[0], heads[1])
        dq_ref[part, :] = (score_scale * joined).astype(low)
        if start == 0:
            dk_sum[...] = dk
            dv_sum[...] = dv
        else:
            dk_sum[...] += dk
            dv_sum[...] += dv
    dk_ref[...] = dk_sum[...].astype(low)
    dv_ref[...] = dv_sum[...].astype(low)


def attention_backward(q, k, v, do, lse, delta, query_seg, key_seg):
    rows, width = q.shape
    keys = k.shape[0]
    pairs = width // 128
    column = lambda n: pl.BlockSpec((n, 128), lambda g: (0, g))
    whole = lambda a: pl.BlockSpec(a.shape, lambda g: (0, 0))
    stat = pl.BlockSpec((1, 2, rows), lambda g: (g, 0, 0))
    return pl.pallas_call(
        functools.partial(attention_backward_kernel, min(256, rows)),
        grid=(pairs,),
        in_specs=[
            column(rows),
            column(keys),
            column(keys),
            column(rows),
            stat,
            stat,
            whole(query_seg),
            whole(key_seg),
        ],
        out_specs=[column(rows), column(keys), column(keys)],
        out_shape=[
            jax.ShapeDtypeStruct((rows, width), low),
            jax.ShapeDtypeStruct((keys, width), low),
            jax.ShapeDtypeStruct((keys, width), low),
        ],
        scratch_shapes=[pltpu.VMEM((keys, 128), wide), pltpu.VMEM((keys, 128), wide)],
        compiler_params=params(),
        cost_estimate=pl.CostEstimate(
            flops=40 * rows * keys * width,
            bytes_accessed=14 * rows * width,
            transcendentals=rows * keys * pairs * 2,
        ),
        name="attention_backward",
    )(q, k, v, do, lse, delta, query_seg, key_seg)


def mlp_step(a, dy, up, down, bias):
    before = rows_by_rows(a, up) + bias
    grad_active = rows_by_rows(dy, down)
    density = 0.3989422804014327 * jnp.exp(-0.5 * before * before)
    below = 0.5 * (1.0 + lax.erf(before * 0.7071067811865476))
    active = (before * below).astype(low)
    grad_before = ((below + before * density) * grad_active).astype(low)
    bias_grad = jnp.sum(grad_before.astype(wide), axis=0, keepdims=True)
    up_grad = cols_by_cols(grad_before, a)
    down_grad = cols_by_cols(active, dy)
    return (
        rows_by_cols(active, down),
        rows_by_cols(grad_before, up),
        up_grad,
        down_grad,
        bias_grad,
    )


def add_up(step, steps, out_ref, da_ref, out_sum, da_sum, out_term, da_term):
    @pl.when(step == 0)
    def _():
        out_sum[...] = out_term
        da_sum[...] = da_term

    @pl.when(step > 0)
    def _():
        out_sum[...] += out_term
        da_sum[...] += da_term

    @pl.when(step == steps - 1)
    def _():
        out_ref[...] = out_sum[...]
        da_ref[...] = da_sum[...]


def mlp_plain_kernel(
    a_ref, dy_ref, up_ref, dn_ref, hb_ref, out_ref, da_ref, gup, gdn, ghb, out_sum, da_sum
):
    out_term, da_term, up_grad, down_grad, bias_grad = mlp_step(
        a_ref[...], dy_ref[...], up_ref[...], dn_ref[...], hb_ref[0]
    )
    gup[...] = up_grad.astype(low)
    gdn[...] = down_grad.astype(low)
    ghb[0] = bias_grad
    add_up(
        pl.program_id(0), pl.num_programs(0), out_ref, da_ref, out_sum, da_sum, out_term, da_term
    )


def mlp_plain(a, dy, up, down, bias, step_width=768):
    rows, width = a.shape
    hidden = up.shape[0]
    steps = hidden // step_width
    whole = pl.BlockSpec((rows, width), lambda i: (0, 0))
    chunk = pl.BlockSpec((step_width, width), lambda i: (i, 0))
    strip = pl.BlockSpec((1, 1, step_width), lambda i: (i, 0, 0))
    return pl.pallas_call(
        mlp_plain_kernel,
        grid=(steps,),
        in_specs=[whole, whole, chunk, chunk, strip],
        out_specs=[whole, whole, chunk, chunk, strip],
        out_shape=[jax.ShapeDtypeStruct((rows, width), wide)] * 2
        + [jax.ShapeDtypeStruct((hidden, width), low)] * 2
        + [jax.ShapeDtypeStruct((steps, 1, step_width), wide)],
        scratch_shapes=[pltpu.VMEM((rows, width), wide)] * 2,
        compiler_params=params(),
        name="mlp_both_ways",
    )(a, dy, up, down, bias.reshape(steps, 1, step_width))


def mlp_pieces_kernel(
    halves,
    place,
    a_ref,
    dy_ref,
    local_ref,
    *refs,
):
    even_refs = refs[:halves]
    odd_ref, hb_ref, out_ref, da_ref, even_grad, odd_grad, ghb, out_sum, da_sum, up, down = refs[
        halves:
    ]
    step = pl.program_id(0)
    seq_index = place[1]
    count = 2 * halves
    piece = even_refs[0].shape[2]

    @pl.when(step == 0)
    def _():
        for other in range(count):
            source = pl.ds(pl.multiple_of((seq_index ^ other) * piece, 16), piece)
            target = pl.ds(other * piece, piece)
            up[target, :] = local_ref[0, source, :]
            down[target, :] = local_ref[1, source, :]

    @pl.when(step > 0)
    def _():
        for other in range(count):
            target = pl.ds(other * piece, piece)
            if other % 2 == 0:
                up[target, :] = even_refs[other // 2][0, 0]
                down[target, :] = even_refs[other // 2][0, 1]
            else:
                up[target, :] = odd_ref[other // 2, 0, 0]
                down[target, :] = odd_ref[other // 2, 0, 1]

    out_term, da_term, up_grad, down_grad, bias_grad = mlp_step(
        a_ref[...], dy_ref[...], up[...], down[...], hb_ref[0]
    )
    up_grad = up_grad.astype(low)
    down_grad = down_grad.astype(low)
    for other in range(count):
        target = even_grad if other % 2 == 0 else odd_grad
        target[other // 2, 0, 0] = up_grad[other * piece : (other + 1) * piece, :]
        target[other // 2, 0, 1] = down_grad[other * piece : (other + 1) * piece, :]
    ghb[0] = bias_grad
    add_up(step, pl.num_programs(0), out_ref, da_ref, out_sum, da_sum, out_term, da_term)


def mlp_pieces(place, a, dy, local, evens, odds, bias):
    rows, width = a.shape
    halves = len(evens)
    steps, _, piece, _ = evens[0].shape
    steps += 1
    step_width = 2 * halves * piece
    whole = pl.BlockSpec((rows, width), lambda i, p: (0, 0))
    strip = pl.BlockSpec((1, 1, step_width), lambda i, p: (i, 0, 0))
    grads = pl.BlockSpec((halves, 1, 2, piece, width), lambda i, p: (0, i, 0, 0, 0))
    before = lambda i: jnp.maximum(i - 1, 0)
    return pl.pallas_call(
        functools.partial(mlp_pieces_kernel, halves),
        grid_spec=pltpu.PrefetchScalarGridSpec(
            num_scalar_prefetch=1,
            grid=(steps,),
            in_specs=[whole, whole, pl.BlockSpec(local.shape, lambda i, p: (0, 0, 0))]
            + [pl.BlockSpec((1, 2, piece, width), lambda i, p: (before(i), 0, 0, 0))] * halves
            + [
                pl.BlockSpec(
                    (halves, 1, 2, piece, width), lambda i, p: (0, before(i), 0, 0, 0)
                ),
                strip,
            ],
            out_specs=[whole, whole, grads, grads, strip],
            scratch_shapes=[pltpu.VMEM((rows, width), wide)] * 2
            + [pltpu.VMEM((step_width, width), low)] * 2,
        ),
        out_shape=[jax.ShapeDtypeStruct((rows, width), wide)] * 2
        + [jax.ShapeDtypeStruct((halves, steps, 2, piece, width), low)] * 2
        + [jax.ShapeDtypeStruct((steps, 1, step_width), wide)],
        compiler_params=params(),
        cost_estimate=pl.CostEstimate(
            flops=12 * rows * steps * step_width * width,
            bytes_accessed=24 * rows * width,
            transcendentals=rows * steps * step_width * 2,
        ),
        name="mlp_both_ways",
    )(place, a, dy, local, *evens, odds, bias)


def assemble_kernel(halves, place, local_ref, *refs):
    even_refs = refs[:halves]
    odd_ref, out_ref = refs[halves:]
    hid_index, seq_index = place[0], place[1]
    quarter = local_ref.shape[0]
    others, piece, _ = even_refs[0].shape
    out_ref[pl.ds(pl.multiple_of(hid_index * quarter, 16), quarter), :] = local_ref[...]
    for step in range(others):
        for other in range(2 * halves):
            start = (hid_index ^ (step + 1)) * quarter + (seq_index ^ other) * piece
            target = pl.ds(pl.multiple_of(start, 16), piece)
            if other % 2 == 0:
                out_ref[target, :] = even_refs[other // 2][step]
            else:
                out_ref[target, :] = odd_ref[other // 2, step]


def assemble(place, local, evens, odds):
    quarter, width = local.shape
    halves = len(evens)
    groups = evens[0].shape[0] + 1
    return pl.pallas_call(
        functools.partial(assemble_kernel, halves),
        in_specs=[smem()] + [whole_vmem()] * (halves + 2),
        out_specs=whole_vmem(),
        out_shape=jax.ShapeDtypeStruct((groups * quarter, width), low),
        compiler_params=params(),
        name="assemble_rows",
    )(place, local, *evens, odds)


def place_packs_kernel(place, own_ref, *refs):
    out_ref = refs[-1]
    packs = out_ref.shape[0]
    seq_index = place[1]
    out_ref[seq_index % packs] = own_ref[...]
    for other in range(1, packs):
        out_ref[(seq_index ^ other) % packs] = refs[other - 1][...].astype(wide)


def place_packs(place, own, others):
    rows, width = own.shape
    packs = len(others) + 1
    return pl.pallas_call(
        place_packs_kernel,
        in_specs=[smem()] + [whole_vmem()] * packs,
        out_specs=whole_vmem(),
        out_shape=jax.ShapeDtypeStruct((packs, rows, width), wide),
        compiler_params=params(),
        name="place_packs",
    )(place, own, *others)


def matrix_grads_kernel(seqs, place, dq, dk, dv, dt, a_ref, o_ref, out_ref):
    hid_index, seq_index = place[0], place[1]
    _, _, piece, width = out_ref.shape
    for matrix, (rows, other) in enumerate(((dq, a_ref), (dk, a_ref), (dv, a_ref), (dt, o_ref))):
        grad = cols_by_cols(rows[...], other[...]).astype(low)
        for chunk in range(width // piece):
            number = matrix * (width // piece) + chunk
            step = (number // seqs) ^ hid_index
            away = (number % seqs) ^ seq_index
            slot = (away % 2) * (seqs // 2) + away // 2
            out_ref[slot, step] = grad[chunk * piece : (chunk + 1) * piece, :]


def matrix_grads(place, seqs, hids, dq, dk, dv, dt, a, o):
    width = a.shape[1]
    piece = 4 * width // (seqs * hids)
    return pl.pallas_call(
        functools.partial(matrix_grads_kernel, seqs),
        in_specs=[smem()] + [whole_vmem()] * 6,
        out_specs=whole_vmem(),
        out_shape=jax.ShapeDtypeStruct((seqs, hids, piece, width), low),
        compiler_params=params(),
        cost_estimate=pl.CostEstimate(
            flops=8 * a.shape[0] * width * width,
            bytes_accessed=12 * a.shape[0] * width,
            transcendentals=0,
        ),
        name="matrix_grads",
    )(place, dq, dk, dv, dt, a, o)


def renew_kernel(place, grads, weight, moment, average, *outs):
    source = place[1] ^ pl.program_id(0)
    gradient = grads[source].astype(wide)
    results = renew(
        weight[...], moment[...], average[...], gradient, weight_decay, matrix_rate
    )
    for out, value in zip(outs, results):
        out[...] = value


def renew_pieces(place, grads, weight, moment, average):
    seqs, matrices, piece, width = grads.shape
    block = pl.BlockSpec((matrices, piece, width), lambda i, p: (0, i, 0))
    return pl.pallas_call(
        renew_kernel,
        grid_spec=pltpu.PrefetchScalarGridSpec(
            num_scalar_prefetch=1,
            grid=(seqs,),
            in_specs=[pl.BlockSpec(grads.shape, lambda i, p: (0, 0, 0, 0))] + [block] * 3,
            out_specs=[block] * 4,
        ),
        out_shape=[jax.ShapeDtypeStruct(weight.shape, wide)] * 4,
        compiler_params=params(),
        cost_estimate=pl.CostEstimate(
            flops=10 * weight.size, bytes_accessed=30 * weight.size, transcendentals=0
        ),
        name="renew_matrices",
    )(place, grads, weight, moment, average)


def solution(mesh):
    seqs = mesh.shape["seq"]
    hids = mesh.shape["hid"]

    def swap(value, axis, step):
        count = mesh.shape[axis]
        return lax.ppermute(value, axis, [(i, i ^ step) for i in range(count)])

    def gather_pieces(local):
        piece = local.shape[1] // seqs
        own = lax.dynamic_slice_in_dim(local, lax.axis_index("seq") * piece, piece, 1)
        remote = jnp.stack([swap(own, "hid", step) for step in range(1, hids)])
        evens = [remote] + [swap(remote, "seq", other) for other in range(2, seqs, 2)]
        return evens, swap(jnp.stack(evens), "seq", 1)

    def tree_sum(values):
        while len(values) > 1:
            values = [values[i] + values[i + 1] for i in range(0, len(values), 2)]
        return values[0]

    def reduce_pieces(evens, odds):
        added = (evens.astype(wide) + swap(odds, "seq", 1).astype(wide)).astype(low)
        terms = [added[0]] + [swap(added[i], "seq", 2 * i) for i in range(1, seqs // 2)]
        added = tree_sum([term.astype(wide) for term in terms]).astype(low)
        terms = [added[0]] + [swap(added[i], "hid", i) for i in range(1, hids)]
        added = tree_sum([term.astype(wide) for term in terms]).astype(low)
        evens = jnp.stack([added] + [swap(added, "seq", other) for other in range(2, seqs, 2)])
        odds = swap(evens, "seq", 1)
        return jnp.stack([evens, odds], axis=1).reshape((seqs,) + added.shape)

    def reduce_small(value):
        value = tree_sum([value] + [swap(value, "hid", step) for step in range(1, hids)])
        return tree_sum([value] + [swap(value, "seq", step) for step in range(1, seqs)])

    def shards(
        tokens_in,
        image_lengths,
        attn_weight,
        attn_moment,
        attn_average,
        mlp_weight,
        mlp_moment,
        mlp_average,
        vector_params,
        vector_moment,
        vector_average,
        out_grad,
    ):
        packs, rows, width = tokens_in.shape
        share = seqs // packs
        hidden = hids * mlp_weight.shape[1]
        seq_index = lax.axis_index("seq")
        hid_index = lax.axis_index("hid")
        place = jnp.stack([hid_index, seq_index]).astype(jnp.int32)
        attn_piece = attn_weight.shape[0] // seqs
        mlp_piece = mlp_weight.shape[1] // seqs
        aligned = attn_piece % 16 == 0 and mlp_piece % 16 == 0

        def to_packs(array):
            pieces = []
            for other in range(packs):
                piece = lax.dynamic_index_in_dim(
                    array, (seq_index ^ other) % packs, 0, keepdims=False
                )
                pieces.append(swap(piece, "seq", other) if other else piece)
            return jnp.concatenate(pieces, axis=0)

        def to_positions(array):
            own = array[:rows]
            moved = array.astype(low)
            others = [
                swap(moved[other * rows : (other + 1) * rows], "seq", other)
                for other in range(1, packs)
            ]
            return place_packs(place, own, others)

        def across_share(array):
            return [array] + [swap(array, "seq", packs * m) for m in range(1, share)]

        tokens = to_packs(tokens_in)
        order = (seq_index ^ jnp.arange(packs, dtype=jnp.int32)) * rows
        positions = (order[:, None] + jnp.arange(rows, dtype=jnp.int32)[None, :]).reshape(-1)
        lengths = lax.dynamic_index_in_dim(image_lengths, seq_index % packs, 0, keepdims=False)
        ends = jnp.cumsum(lengths)
        query_seg = jnp.sum((ends[None, :] <= positions[:, None]).astype(jnp.int32), axis=1)
        valid = (positions < ends[-1]).astype(wide)[:, None]
        key_seg = jnp.concatenate(across_share(query_seg))

        attn_low = attn_weight.astype(low)
        mlp_low = mlp_weight.astype(low)
        if aligned:
            evens, odds = gather_pieces(attn_low[None])
            whole_attn = assemble(place, attn_low, [e[:, 0] for e in evens], odds[:, :, 0])
        else:
            whole_attn = lax.all_gather(attn_low, "hid", axis=0, tiled=True)
        w_qkv = whole_attn[: 3 * width]
        w_out = whole_attn[3 * width :]

        gain_one, shift_one, bias_query, bias_value, bias_out, gain_two, shift_two, bias_down = [
            vector_params[row_index] for row_index in range(8)
        ]
        hidden_bias = vector_params[8:].reshape(-1)

        tokens_wide = tokens.astype(wide)
        first_norm, first_back = jax.vjp(normalize, tokens_wide, gain_one, shift_one)
        first_low = first_norm.astype(low)
        projected = rows_by_rows(first_low, w_qkv)
        queries = ((projected[:, :width] + bias_query).astype(low) * score_scale).astype(low)
        keys_own = projected[:, width : 2 * width].astype(low)
        values_own = (projected[:, 2 * width :] + bias_value).astype(low)
        keys = jnp.concatenate(across_share(keys_own))
        values = jnp.concatenate(across_share(values_own))
        mixed, log_total = attention_forward(
            queries, keys, values, query_seg[:, None], key_seg[None, :], valid
        )
        residual = tokens_wide + rows_by_rows(mixed, w_out) + bias_out
        second_norm, second_back = jax.vjp(normalize, residual, gain_two, shift_two)
        second_low = second_norm.astype(low)

        grad_low = to_packs(out_grad)
        grad_wide = grad_low.astype(wide)
        if aligned:
            evens, odds = gather_pieces(mlp_low)
            apart = seq_index ^ jnp.arange(seqs)
            away = hid_index ^ jnp.arange(hids)
            bias_pieces = hidden_bias.reshape(hids, seqs, mlp_piece)[away][:, apart]
            mlp_out, second_grad, even_grad, odd_grad, bias_grad = mlp_pieces(
                place,
                second_low,
                grad_low,
                mlp_low,
                evens,
                odds,
                bias_pieces.reshape(hids, 1, seqs * mlp_piece),
            )
            mlp_grad = reduce_pieces(even_grad, odd_grad)
            mlp_new = renew_pieces(place, mlp_grad, mlp_weight, mlp_moment, mlp_average)
            bias_grad = bias_grad.reshape(hids, seqs, mlp_piece)[away][:, apart]
        else:
            whole_mlp = lax.all_gather(mlp_low, "hid", axis=1, tiled=True)
            mlp_out, second_grad, up_grad, down_grad, bias_grad = mlp_plain(
                second_low, grad_low, whole_mlp[0], whole_mlp[1], hidden_bias
            )
            mlp_grad = lax.psum_scatter(
                jnp.stack([up_grad, down_grad]), "hid", scatter_dimension=1, tiled=True
            )
            mlp_grad = lax.psum(mlp_grad, "seq").astype(wide)
            mlp_new = renew(
                mlp_weight, mlp_moment, mlp_average, mlp_grad, weight_decay, matrix_rate
            )
        block_out = to_positions(residual + mlp_out + bias_down)

        residual_part, grad_gain_two, grad_shift_two = second_back(second_grad)
        residual_grad = grad_wide + residual_part
        branch_grad = residual_grad.astype(low)
        mixed_grad = (rows_by_cols(branch_grad, w_out) * valid).astype(low)
        delta = jnp.sum(
            (mixed_grad.astype(wide) * mixed.astype(wide)).reshape(-1, HEADS, HEAD_DIM), axis=2
        )
        delta = jnp.transpose(delta).reshape(HEADS // 2, 2, -1)
        query_grad, key_grad, value_grad = attention_backward(
            queries,
            keys,
            values,
            mixed_grad,
            log_total,
            delta,
            query_seg[None, :],
            key_seg[:, None],
        )
        if share > 1:
            count = queries.shape[0]

            def own_share(array):
                terms = [array[:count].astype(wide)]
                for m in range(1, share):
                    part = array[m * count : (m + 1) * count]
                    terms.append(swap(part, "seq", packs * m).astype(wide))
                return tree_sum(terms).astype(low)

            key_grad = own_share(key_grad)
            value_grad = own_share(value_grad)
        if aligned:
            attn_grad = matrix_grads(
                place,
                seqs,
                hids,
                query_grad,
                key_grad,
                value_grad,
                branch_grad,
                first_low,
                mixed,
            )[:, :, None]
            attn_grad = reduce_pieces(attn_grad[: seqs // 2], attn_grad[seqs // 2 :])
            attn_new = renew_pieces(
                place, attn_grad, attn_weight[None], attn_moment[None], attn_average[None]
            )
            attn_new = [array[0] for array in attn_new]
        else:
            attn_grad = [
                cols_by_cols(query_grad, first_low),
                cols_by_cols(key_grad, first_low),
                cols_by_cols(value_grad, first_low),
                cols_by_cols(branch_grad, mixed),
            ]
            attn_grad = lax.psum_scatter(
                jnp.concatenate(attn_grad).astype(low), "hid", scatter_dimension=0, tiled=True
            )
            attn_grad = lax.psum(attn_grad, "seq").astype(wide)
            attn_new = renew(
                attn_weight, attn_moment, attn_average, attn_grad, weight_decay, matrix_rate
            )
        joined_grad = jnp.concatenate([query_grad, key_grad, value_grad], axis=1)
        first_grad = rows_by_cols(joined_grad, w_qkv)
        input_part, grad_gain_one, grad_shift_one = first_back(first_grad)
        input_grad = to_positions(residual_grad + input_part)

        vector_grad = jnp.concatenate(
            [
                jnp.stack(
                    [
                        grad_gain_one,
                        grad_shift_one,
                        jnp.sum(query_grad.astype(wide), axis=0),
                        jnp.sum(value_grad.astype(wide), axis=0),
                        jnp.sum(branch_grad.astype(wide), axis=0),
                        grad_gain_two,
                        grad_shift_two,
                        jnp.sum(grad_wide, axis=0),
                    ]
                ),
                bias_grad.reshape(-1, width),
            ]
        )
        vector_grad = reduce_small(vector_grad)
        vector_new = renew(
            vector_params, vector_moment, vector_average, vector_grad, 0.0, vector_rate
        )
        return (block_out, input_grad, *attn_new, *mlp_new, *vector_new)

    return jax.shard_map(
        shards,
        mesh=mesh,
        in_specs=(
            P("hid", "seq", None),
            P("hid", None),
            P("hid", None),
            P("hid", None),
            P("hid", None),
            P(None, "hid", None),
            P(None, "hid", None),
            P(None, "hid", None),
            P(),
            P(),
            P(),
            P("hid", "seq", None),
        ),
        out_specs=(
            P("hid", "seq", None),
            P("hid", "seq", None),
            P("hid", None),
            P("hid", None),
            P("hid", None),
            P("hid", None),
            P(None, "hid", None),
            P(None, "hid", None),
            P(None, "hid", None),
            P(None, "hid", None),
            P(),
            P(),
            P(),
            P(),
        ),
        check_vma=False,
    )
```

```python
import functools

import jax
import jax.numpy as jnp
from jax import lax
from jax.experimental import pallas as pl
from jax.experimental.pallas import tpu as pltpu
from jax.sharding import PartitionSpec as P

HEADS = 12
HEAD_DIM = 64

score_scale = 0.125
norm_eps = 1e-06
big_negative = -1e30
matrix_rate = 0.0001
vector_rate = 0.001
momentum_decay = 0.9
weight_decay = 0.0001
average_decay = 0.9

low = jnp.bfloat16
wide = jnp.float32
kernel_vmem = 56 * 1024 * 1024


def rows_by_rows(a, b):
    return lax.dot_general(a, b, (((1,), (1,)), ((), ())), preferred_element_type=wide)


def rows_by_cols(a, b):
    return lax.dot_general(a, b, (((1,), (0,)), ((), ())), preferred_element_type=wide)


def cols_by_cols(a, b):
    return lax.dot_general(a, b, (((0,), (0,)), ((), ())), preferred_element_type=wide)


def normalize(inputs, gain_row, offset):
    center = inputs - jnp.mean(inputs, axis=-1, keepdims=True)
    spread = jnp.mean(center * center, axis=-1, keepdims=True)
    return center * lax.rsqrt(spread + norm_eps) * gain_row + offset


def renew(weight, moment, average, gradient, decay_rate, step_rate):
    step_grad = gradient + decay_rate * weight
    moment_new = momentum_decay * moment + step_grad
    weight_new = weight - step_rate * (step_grad + momentum_decay * moment_new)
    average_new = average_decay * average + (1.0 - average_decay) * weight_new
    return (gradient, moment_new, weight_new, average_new)


def params(**kwargs):
    return pltpu.CompilerParams(vmem_limit_bytes=kernel_vmem, **kwargs)


def smem():
    return pl.BlockSpec(memory_space=pltpu.SMEM)


def whole_vmem():
    return pl.BlockSpec(memory_space=pltpu.VMEM)


def unused():
    return pl.BlockSpec(memory_space=pl.ANY)


def attention_forward_kernel(tile, q_ref, k_ref, v_ref, query_seg, key_seg, valid_ref, *refs):
    o_ref, lse_ref = refs[-2:]
    rows = q_ref.shape[0]
    lane = lax.broadcasted_iota(jnp.int32, (1, 128), 1)
    k = k_ref[...]
    v = v_ref[...]
    v_and_ones = jnp.concatenate([v, jnp.ones_like(v)], axis=1)
    for start in range(0, rows, tile):
        part = pl.ds(start, tile)
        q = q_ref[part, :]
        same = query_seg[part, :] == key_seg[...]
        heads = []
        for head in range(2):
            mine = (lane // HEAD_DIM) == head
            scores = rows_by_rows(jnp.where(mine, q, jnp.zeros_like(q)), k)
            scores = jnp.where(same, scores, big_negative)
            top = jnp.max(scores, axis=1, keepdims=True)
            weights = jnp.exp(scores - top).astype(low)
            sums = rows_by_cols(weights, v_and_ones)
            total = sums[:, 128:]
            heads.append(sums[:, :128] / total)
            lse_ref[0, head : head + 1, part] = jnp.transpose(top + jnp.log(total))[:1, :]
        joined = jnp.where(lane < HEAD_DIM, heads[0], heads[1]) * valid_ref[part, :]
        o_ref[part, :] = joined.astype(low)


def attention_forward(q, k, v, query_seg, key_seg, valid, pairs, earlier=(), after=()):
    rows, width = q.shape
    keys = k.shape[0]
    column = lambda n: pl.BlockSpec((n, 128), lambda g: (0, pairs[0] + g))
    whole = lambda a: pl.BlockSpec(a.shape, lambda g: (0, 0))
    return pl.pallas_call(
        functools.partial(attention_forward_kernel, min(128, rows)),
        grid=(len(pairs),),
        in_specs=[
            column(rows),
            column(keys),
            column(keys),
            whole(query_seg),
            whole(key_seg),
            whole(valid),
        ]
        + [unused()] * (len(earlier) + len(after)),
        out_specs=[
            column(rows),
            pl.BlockSpec((1, 2, rows), lambda g: (pairs[0] + g, 0, 0)),
        ],
        out_shape=[
            jax.ShapeDtypeStruct((rows, width), low),
            jax.ShapeDtypeStruct((width // 128, 2, rows), wide),
        ],
        input_output_aliases={6 + i: i for i in range(len(earlier))},
        compiler_params=params(),
        cost_estimate=pl.CostEstimate(
            flops=16 * rows * keys * 128 * len(pairs),
            bytes_accessed=8 * rows * 128 * len(pairs),
            transcendentals=rows * keys * len(pairs) * 2,
        ),
        name="attention_forward",
    )(q, k, v, query_seg, key_seg, valid, *earlier, *after)


def attention_backward_kernel(
    tile,
    q_ref,
    k_ref,
    v_ref,
    do_ref,
    lse_ref,
    delta_ref,
    query_seg,
    key_seg,
    *refs,
):
    dq_ref, dk_ref, dv_ref, dk_sum, dv_sum = refs[-5:]
    rows = q_ref.shape[0]
    lane = lax.broadcasted_iota(jnp.int32, (1, 128), 1)
    k = k_ref[...]
    v = v_ref[...]
    for start in range(0, rows, tile):
        part = pl.ds(start, tile)
        q = q_ref[part, :]
        do = do_ref[part, :]
        same = key_seg[...] == query_seg[:, part]
        heads = []
        dk = 0.0
        dv = 0.0
        for head in range(2):
            mine = (lane // HEAD_DIM) == head
            q_head = jnp.where(mine, q, jnp.zeros_like(q))
            do_head = jnp.where(mine, do, jnp.zeros_like(do))
            scores = jnp.where(same, rows_by_rows(k, q_head), big_negative)
            probs = jnp.exp(scores - lse_ref[0, head : head + 1, part])
            grads = rows_by_rows(v, do_head)
            grads = (probs * (grads - delta_ref[0, head : head + 1, part])).astype(low)
            dv = dv + rows_by_cols(probs.astype(low), do_head)
            dk = dk + rows_by_cols(grads, q_head)
            heads.append(cols_by_cols(grads, k))
        joined = jnp.where(lane < HEAD_DIM, heads[0], heads[1])
        dq_ref[part, :] = (score_scale * joined).astype(low)
        if start == 0:
            dk_sum[...] = dk
            dv_sum[...] = dv
        else:
            dk_sum[...] += dk
            dv_sum[...] += dv
    dk_ref[...] = dk_sum[...].astype(low)
    dv_ref[...] = dv_sum[...].astype(low)


def attention_backward(
    q, k, v, do, lse, delta, query_seg, key_seg, pairs, earlier=(), after=()
):
    rows, width = q.shape
    keys = k.shape[0]
    column = lambda n: pl.BlockSpec((n, 128), lambda g: (0, pairs[0] + g))
    whole = lambda a: pl.BlockSpec(a.shape, lambda g: (0, 0))
    stat = pl.BlockSpec((1, 2, rows), lambda g: (pairs[0] + g, 0, 0))
    return pl.pallas_call(
        functools.partial(attention_backward_kernel, min(256, rows)),
        grid=(len(pairs),),
        in_specs=[
            column(rows),
            column(keys),
            column(keys),
            column(rows),
            stat,
            stat,
            whole(query_seg),
            whole(key_seg),
        ]
        + [unused()] * (len(earlier) + len(after)),
        out_specs=[column(rows), column(keys), column(keys)],
        out_shape=[
            jax.ShapeDtypeStruct((rows, width), low),
            jax.ShapeDtypeStruct((keys, width), low),
            jax.ShapeDtypeStruct((keys, width), low),
        ],
        input_output_aliases={8 + i: i for i in range(len(earlier))},
        scratch_shapes=[pltpu.VMEM((keys, 128), wide), pltpu.VMEM((keys, 128), wide)],
        compiler_params=params(),
        cost_estimate=pl.CostEstimate(
            flops=40 * rows * keys * 128 * len(pairs),
            bytes_accessed=14 * rows * 128 * len(pairs),
            transcendentals=rows * keys * len(pairs) * 2,
        ),
        name="attention_backward",
    )(q, k, v, do, lse, delta, query_seg, key_seg, *earlier, *after)


def mlp_step(a, dy, up, down, bias):
    before = rows_by_rows(a, up) + bias
    grad_active = rows_by_rows(dy, down)
    density = 0.3989422804014327 * jnp.exp(-0.5 * before * before)
    below = 0.5 * (1.0 + lax.erf(before * 0.7071067811865476))
    active = (before * below).astype(low)
    grad_before = ((below + before * density) * grad_active).astype(low)
    bias_grad = jnp.sum(grad_before.astype(wide), axis=0, keepdims=True)
    up_grad = cols_by_cols(grad_before, a)
    down_grad = cols_by_cols(active, dy)
    return (
        rows_by_cols(active, down),
        rows_by_cols(grad_before, up),
        up_grad,
        down_grad,
        bias_grad,
    )


def add_up(step, steps, h_ref, vec_ref, out_ref, da_ref, out_sum, da_sum, out_term, da_term):
    @pl.when(step == 0)
    def _():
        out_sum[...] = out_term
        da_sum[...] = da_term

    @pl.when(step > 0)
    def _():
        out_sum[...] += out_term
        da_sum[...] += da_term

    @pl.when(step == steps - 1)
    def _():
        out_ref[...] = (h_ref[...] + out_sum[...] + vec_ref[7:8, :]).astype(low)
        da_ref[...] = da_sum[...]


def mlp_plain_kernel(
    a_ref,
    dy_ref,
    h_ref,
    vec_ref,
    up_ref,
    dn_ref,
    hb_ref,
    out_ref,
    da_ref,
    gup,
    gdn,
    ghb,
    out_sum,
    da_sum,
):
    out_term, da_term, up_grad, down_grad, bias_grad = mlp_step(
        a_ref[...], dy_ref[...], up_ref[...], dn_ref[...], hb_ref[0]
    )
    gup[...] = up_grad.astype(low)
    gdn[...] = down_grad.astype(low)
    ghb[0] = bias_grad
    step, steps = pl.program_id(0), pl.num_programs(0)
    add_up(step, steps, h_ref, vec_ref, out_ref, da_ref, out_sum, da_sum, out_term, da_term)


def mlp_plain(a, dy, h, vec, up, down, bias, step_width=768):
    rows, width = a.shape
    hidden = up.shape[0]
    steps = hidden // step_width
    whole = pl.BlockSpec((rows, width), lambda i: (0, 0))
    chunk = pl.BlockSpec((step_width, width), lambda i: (i, 0))
    strip = pl.BlockSpec((1, 1, step_width), lambda i: (i, 0, 0))
    return pl.pallas_call(
        mlp_plain_kernel,
        grid=(steps,),
        in_specs=[whole, whole, whole, pl.BlockSpec(vec.shape, lambda i: (0, 0))]
        + [chunk, chunk, strip],
        out_specs=[whole, whole, chunk, chunk, strip],
        out_shape=[
            jax.ShapeDtypeStruct((rows, width), low),
            jax.ShapeDtypeStruct((rows, width), wide),
        ]
        + [jax.ShapeDtypeStruct((hidden, width), low)] * 2
        + [jax.ShapeDtypeStruct((steps, 1, step_width), wide)],
        scratch_shapes=[pltpu.VMEM((rows, width), wide)] * 2,
        compiler_params=params(),
        name="mlp_both_ways",
    )(a, dy, h, vec, up, down, bias.reshape(steps, 1, step_width))


def mlp_pieces_kernel(sources, place, a_ref, dy_ref, h_ref, vec_ref, local_ref, *refs):
    count = len(sources)
    piece_refs = refs[:count]
    hb_ref, out_ref, da_ref, even_grad, odd_grad, ghb, out_sum, da_sum, up, down = refs[count:]
    step = pl.program_id(0)
    seq_index = place[1]
    piece = piece_refs[0].shape[2]

    @pl.when(step == 0)
    def _():
        for other in range(count):
            source = pl.ds(pl.multiple_of((seq_index ^ other) * piece, 16), piece)
            target = pl.ds(other * piece, piece)
            up[target, :] = local_ref[0, source, :]
            down[target, :] = local_ref[1, source, :]

    @pl.when(step > 0)
    def _():
        for other, ((up_from, up_at), (down_from, down_at)) in enumerate(sources):
            target = pl.ds(other * piece, piece)
            up[target, :] = piece_refs[up_from][0, up_at]
            down[target, :] = piece_refs[down_from][0, down_at]

    out_term, da_term, up_grad, down_grad, bias_grad = mlp_step(
        a_ref[...], dy_ref[...], up[...], down[...], hb_ref[0]
    )
    up_grad = up_grad.astype(low)
    down_grad = down_grad.astype(low)
    for other in range(count):
        target = even_grad if other % 2 == 0 else odd_grad
        target[other // 2, 0, 0] = up_grad[other * piece : (other + 1) * piece, :]
        target[other // 2, 0, 1] = down_grad[other * piece : (other + 1) * piece, :]
    ghb[0] = bias_grad
    steps = pl.num_programs(0)
    add_up(step, steps, h_ref, vec_ref, out_ref, da_ref, out_sum, da_sum, out_term, da_term)


def mlp_pieces(place, a, dy, h, vec, local, pieces, sources, bias):
    rows, width = a.shape
    steps, _, piece, _ = pieces[0].shape
    steps += 1
    count = len(sources)
    halves = count // 2
    step_width = count * piece
    whole = pl.BlockSpec((rows, width), lambda i, p: (0, 0))
    strip = pl.BlockSpec((1, 1, step_width), lambda i, p: (i, 0, 0))
    grads = pl.BlockSpec((halves, 1, 2, piece, width), lambda i, p: (0, i, 0, 0, 0))
    before = lambda i: jnp.maximum(i - 1, 0)
    return pl.pallas_call(
        functools.partial(mlp_pieces_kernel, sources),
        grid_spec=pltpu.PrefetchScalarGridSpec(
            num_scalar_prefetch=1,
            grid=(steps,),
            in_specs=[
                whole,
                whole,
                whole,
                pl.BlockSpec(vec.shape, lambda i, p: (0, 0)),
                pl.BlockSpec(local.shape, lambda i, p: (0, 0, 0)),
            ]
            + [pl.BlockSpec((1, 2, piece, width), lambda i, p: (before(i), 0, 0, 0))] * count
            + [strip],
            out_specs=[whole, whole, grads, grads, strip],
            scratch_shapes=[pltpu.VMEM((rows, width), wide)] * 2
            + [pltpu.VMEM((step_width, width), low)] * 2,
        ),
        out_shape=[
            jax.ShapeDtypeStruct((rows, width), low),
            jax.ShapeDtypeStruct((rows, width), wide),
        ]
        + [jax.ShapeDtypeStruct((halves, steps, 2, piece, width), low)] * 2
        + [jax.ShapeDtypeStruct((steps, 1, step_width), wide)],
        compiler_params=params(),
        cost_estimate=pl.CostEstimate(
            flops=12 * rows * steps * step_width * width,
            bytes_accessed=24 * rows * width,
            transcendentals=rows * steps * step_width * 2,
        ),
        name="mlp_both_ways",
    )(place, a, dy, h, vec, local, *pieces, bias)


def norm_parts(rows):
    center = rows - jnp.mean(rows, axis=-1, keepdims=True)
    scale = lax.rsqrt(jnp.mean(center * center, axis=-1, keepdims=True) + norm_eps)
    return center * scale, scale


def norm_back(unit, scale, gain, grad):
    inner = grad * gain
    return scale * (
        inner
        - jnp.mean(inner, axis=-1, keepdims=True)
        - unit * jnp.mean(inner * unit, axis=-1, keepdims=True)
    )


def add_rows(ref, rows):
    total = [jnp.sum(row, axis=0, keepdims=True) for row in rows]
    total = jnp.concatenate(total + [jnp.zeros_like(total[0])] * (8 - len(total)), axis=0)

    @pl.when(pl.program_id(0) == 0)
    def _():
        ref[...] = total

    @pl.when(pl.program_id(0) > 0)
    def _():
        ref[...] += total


def gather_rows(place, local_ref, piece_refs, out_ref):
    hid_index, seq_index = place[0], place[1]
    quarter = local_ref.shape[0]
    others, piece, _ = piece_refs[0].shape
    out_ref[pl.ds(pl.multiple_of(hid_index * quarter, 16), quarter), :] = local_ref[...]
    for step in range(others):
        for other, piece_ref in enumerate(piece_refs):
            start = (hid_index ^ (step + 1)) * quarter + (seq_index ^ other) * piece
            out_ref[pl.ds(pl.multiple_of(start, 16), piece), :] = piece_ref[step]


def project_kernel(pieces, place, x_ref, vec_ref, *refs):
    if pieces:
        w_ref, a_ref, q_ref, k_ref, v_ref = refs[pieces:]

        @pl.when(pl.program_id(0) == 0)
        def _():
            gather_rows(place, refs[0], refs[1:pieces], w_ref)

    else:
        w_ref, a_ref, q_ref, k_ref, v_ref = refs
    width = x_ref.shape[1]
    unit, _ = norm_parts(x_ref[...].astype(wide))
    first = (unit * vec_ref[0:1, :] + vec_ref[1:2, :]).astype(low)
    a_ref[...] = first
    q = (rows_by_rows(first, w_ref[0:width, :]) + vec_ref[2:3, :]).astype(low)
    q_ref[...] = (q.astype(wide) * score_scale).astype(low)
    k_ref[...] = rows_by_rows(first, w_ref[width : 2 * width, :]).astype(low)
    v = rows_by_rows(first, w_ref[2 * width : 3 * width, :]) + vec_ref[3:4, :]
    v_ref[...] = v.astype(low)


def row_tile(rows):
    return min(256, rows)


def project(place, x, vec, pieces, whole):
    rows, width = x.shape
    tile = row_tile(rows)
    strip = pl.BlockSpec((tile, width), lambda i, p: (i, 0))
    fixed = lambda a: pl.BlockSpec(a.shape, lambda i, p: (0,) * len(a.shape))
    arrays = pieces if whole is None else [whole]
    matrix = jax.ShapeDtypeStruct((4 * width, width), low)
    strips = [jax.ShapeDtypeStruct((rows, width), low)] * 4
    results = pl.pallas_call(
        functools.partial(project_kernel, len(pieces)),
        grid_spec=pltpu.PrefetchScalarGridSpec(
            num_scalar_prefetch=1,
            grid=(rows // tile,),
            in_specs=[strip, fixed(vec)] + [fixed(a) for a in arrays],
            out_specs=([fixed(matrix)] if whole is None else []) + [strip] * 4,
        ),
        out_shape=([matrix] if whole is None else []) + strips,
        compiler_params=params(),
        cost_estimate=pl.CostEstimate(
            flops=6 * rows * width * width, bytes_accessed=26 * rows * width, transcendentals=0
        ),
        name="norm_and_project",
    )(place, x, vec, *arrays)
    return results if whole is None else [whole] + list(results)


def join_kernel(o_ref, x_ref, w_ref, vec_ref, h_ref, a_ref):
    joined = x_ref[...].astype(wide) + rows_by_rows(o_ref[...], w_ref[...]) + vec_ref[4:5, :]
    h_ref[...] = joined
    unit, _ = norm_parts(joined)
    a_ref[...] = (unit * vec_ref[5:6, :] + vec_ref[6:7, :]).astype(low)


def join(o, x, w, vec):
    rows, width = x.shape
    tile = row_tile(rows)
    strip = pl.BlockSpec((tile, width), lambda i: (i, 0))
    return pl.pallas_call(
        join_kernel,
        grid=(rows // tile,),
        in_specs=[
            strip,
            strip,
            pl.BlockSpec((width, width), lambda i: (3, 0)),
            pl.BlockSpec(vec.shape, lambda i: (0, 0)),
        ],
        out_specs=[strip, strip],
        out_shape=[
            jax.ShapeDtypeStruct((rows, width), wide),
            jax.ShapeDtypeStruct((rows, width), low),
        ],
        compiler_params=params(),
        cost_estimate=pl.CostEstimate(
            flops=2 * rows * width * width, bytes_accessed=10 * rows * width, transcendentals=0
        ),
        name="join_and_norm",
    )(o, x, w, vec)


def branch_back_kernel(
    da_ref, h_ref, dy_ref, o_ref, valid_ref, w_ref, vec_ref, dh_ref, dt_ref, do_ref, delta_ref, sums
):
    unit, scale = norm_parts(h_ref[...])
    da = da_ref[...]
    dy = dy_ref[...].astype(wide)
    dh = dy + norm_back(unit, scale, vec_ref[5:6, :], da)
    dh_ref[...] = dh
    dt = dh.astype(low)
    dt_ref[...] = dt
    do = (rows_by_cols(dt, w_ref[...]) * valid_ref[...]).astype(low)
    do_ref[...] = do
    product = do.astype(wide) * o_ref[...].astype(wide)
    width = product.shape[1]
    head = lax.broadcasted_iota(jnp.int32, (16, width), 0)
    lane = lax.broadcasted_iota(jnp.int32, (16, width), 1)
    pick = (lane // HEAD_DIM == head).astype(wide)
    delta = lax.dot_general(
        pick,
        product,
        (((1,), (1,)), ((), ())),
        preferred_element_type=wide,
        precision=lax.Precision.HIGHEST,
    )
    for pair in range(delta_ref.shape[0]):
        delta_ref[pair] = delta[2 * pair : 2 * pair + 2, :]
    add_rows(sums, [da * unit, da, dt.astype(wide), dy])


def branch_back(da, h, dy, o, valid, w, vec):
    rows, width = h.shape
    tile = row_tile(rows)
    pairs = width // 128
    strip = pl.BlockSpec((tile, width), lambda i: (i, 0))
    return pl.pallas_call(
        branch_back_kernel,
        grid=(rows // tile,),
        in_specs=[
            strip,
            strip,
            strip,
            strip,
            pl.BlockSpec((tile, 1), lambda i: (i, 0)),
            pl.BlockSpec((width, width), lambda i: (3, 0)),
            pl.BlockSpec(vec.shape, lambda i: (0, 0)),
        ],
        out_specs=[
            strip,
            strip,
            strip,
            pl.BlockSpec((pairs, 2, tile), lambda i: (0, 0, i)),
            pl.BlockSpec((8, width), lambda i: (0, 0)),
        ],
        out_shape=[
            jax.ShapeDtypeStruct((rows, width), wide),
            jax.ShapeDtypeStruct((rows, width), low),
            jax.ShapeDtypeStruct((rows, width), low),
            jax.ShapeDtypeStruct((pairs, 2, rows), wide),
            jax.ShapeDtypeStruct((8, width), wide),
        ],
        compiler_params=params(),
        cost_estimate=pl.CostEstimate(
            flops=2 * rows * width * width, bytes_accessed=20 * rows * width, transcendentals=0
        ),
        name="branch_backward",
    )(da, h, dy, o, valid, w, vec)


def input_back_kernel(dq_ref, dk_ref, dv_ref, w_ref, x_ref, dh_ref, vec_ref, out_ref, sums):
    width = x_ref.shape[1]
    da = rows_by_cols(dq_ref[...], w_ref[0:width, :])
    da += rows_by_cols(dk_ref[...], w_ref[width : 2 * width, :])
    da += rows_by_cols(dv_ref[...], w_ref[2 * width : 3 * width, :])
    unit, scale = norm_parts(x_ref[...].astype(wide))
    grad = dh_ref[...] + norm_back(unit, scale, vec_ref[0:1, :], da)
    out_ref[...] = grad.astype(low)
    add_rows(sums, [da * unit, da, dq_ref[...].astype(wide), dv_ref[...].astype(wide)])


def input_back(dq, dk, dv, w, x, dh, vec):
    rows, width = x.shape
    tile = row_tile(rows)
    strip = pl.BlockSpec((tile, width), lambda i: (i, 0))
    return pl.pallas_call(
        input_back_kernel,
        grid=(rows // tile,),
        in_specs=[
            strip,
            strip,
            strip,
            pl.BlockSpec((3 * width, width), lambda i: (0, 0)),
            strip,
            strip,
            pl.BlockSpec(vec.shape, lambda i: (0, 0)),
        ],
        out_specs=[strip, pl.BlockSpec((8, width), lambda i: (0, 0))],
        out_shape=[
            jax.ShapeDtypeStruct((rows, width), low),
            jax.ShapeDtypeStruct((8, width), wide),
        ],
        compiler_params=params(),
        cost_estimate=pl.CostEstimate(
            flops=6 * rows * width * width, bytes_accessed=18 * rows * width, transcendentals=0
        ),
        name="input_backward",
    )(dq, dk, dv, w, x, dh, vec)


def matrix_grads_kernel(seqs, place, dq, dk, dv, dt, a_ref, o_ref, *refs):
    even_ref, odd_ref = refs[-2:]
    hid_index, seq_index = place[0], place[1]
    _, _, piece, width = even_ref.shape
    for matrix, (rows, other) in enumerate(((dq, a_ref), (dk, a_ref), (dv, a_ref), (dt, o_ref))):
        grad = cols_by_cols(rows[...], other[...]).astype(low)
        for owner in range(seqs):
            away = owner ^ seq_index
            rows_of = grad[owner * piece : (owner + 1) * piece, :]

            @pl.when(away % 2 == 0)
            def _(rows_of=rows_of, away=away, matrix=matrix):
                even_ref[away // 2, matrix ^ hid_index] = rows_of

            @pl.when(away % 2 == 1)
            def _(rows_of=rows_of, away=away, matrix=matrix):
                odd_ref[away // 2, matrix ^ hid_index] = rows_of


def matrix_grads(place, seqs, columns, dq, dk, dv, dt, a, o):
    rows, width = a.shape
    count = len(columns)
    piece = count // seqs
    strip = pl.BlockSpec((rows, count), lambda i, p: (0, columns[0] // count))
    whole = pl.BlockSpec((rows, width), lambda i, p: (0, 0))
    result = jax.ShapeDtypeStruct((seqs // 2, 4, piece, width), low)
    return pl.pallas_call(
        functools.partial(matrix_grads_kernel, seqs),
        grid_spec=pltpu.PrefetchScalarGridSpec(
            num_scalar_prefetch=1,
            grid=(1,),
            in_specs=[strip] * 4 + [whole] * 2,
            out_specs=[pl.BlockSpec(result.shape, lambda i, p: (0, 0, 0, 0))] * 2,
        ),
        out_shape=[result] * 2,
        compiler_params=params(),
        cost_estimate=pl.CostEstimate(
            flops=8 * rows * count * width,
            bytes_accessed=12 * rows * width,
            transcendentals=0,
        ),
        name="matrix_grads",
    )(place, dq, dk, dv, dt, a, o)


def split_kernel(*refs):
    up, down = refs[-2:]
    for step, ref in enumerate(refs[:-2]):
        up[step] = ref[0:2]
        down[step] = ref[2:4]


def split_steps(arrays):
    _, piece, width = arrays[0].shape
    return pl.pallas_call(
        split_kernel,
        in_specs=[whole_vmem()] * len(arrays),
        out_specs=[whole_vmem()] * 2,
        out_shape=[jax.ShapeDtypeStruct((len(arrays), 2, piece, width), low)] * 2,
        compiler_params=params(),
        name="split_steps",
    )(*arrays)


def renew_kernel(count, parts, place, *refs):
    pieces = refs[:count]
    weight, moment, average = refs[count : count + 3]
    outs = refs[count + 3 : count + 7]
    grads = refs[count + 7]
    block = weight.shape[1]

    @pl.when(pl.program_id(0) == 0)
    def _():
        base = 0
        for start, rows in parts:
            for other, piece in enumerate(pieces):
                first = base + (place[1] ^ other) * rows
                target = pl.ds(pl.multiple_of(first, 16), rows)
                grads[:, target, :] = piece[:, start : start + rows, :]
            base += count * rows

    here = pl.ds(pl.multiple_of(pl.program_id(0) * block, 16), block)
    results = renew(
        weight[...],
        moment[...],
        average[...],
        grads[:, here, :].astype(wide),
        weight_decay,
        matrix_rate,
    )
    for out, value in zip(outs, results):
        out[...] = value


def renew_pieces(place, pieces, parts, weight, moment, average):
    matrices, rows, width = weight.shape
    steps = 4
    block = pl.BlockSpec((matrices, rows // steps, width), lambda i, p: (0, i, 0))
    fixed = pl.BlockSpec(pieces[0].shape, lambda i, p: (0, 0, 0))
    return pl.pallas_call(
        functools.partial(renew_kernel, len(pieces), parts),
        grid_spec=pltpu.PrefetchScalarGridSpec(
            num_scalar_prefetch=1,
            grid=(steps,),
            in_specs=[fixed] * len(pieces) + [block] * 3,
            out_specs=[block] * 4,
            scratch_shapes=[pltpu.VMEM(weight.shape, low)],
        ),
        out_shape=[jax.ShapeDtypeStruct(weight.shape, wide)] * 4,
        compiler_params=params(),
        cost_estimate=pl.CostEstimate(
            flops=10 * weight.size, bytes_accessed=30 * weight.size, transcendentals=0
        ),
        name="renew_matrices",
    )(place, *pieces, weight, moment, average)


def add_low(a, b):
    return (a.astype(wide) + b.astype(wide)).astype(low)


def fold_mlp_kernel(even_ref, other_ref, up_keep, up_send, down_keep, down_send):
    for half in range(4):
        up = add_low(even_ref[half, 0, 0], other_ref[half, 0, 0])
        down = add_low(even_ref[half, 0, 1], other_ref[half, 0, 1])
        (up_send if half % 2 else up_keep)[half // 2, 0] = up
        (down_send if half // 2 else down_keep)[half % 2, 0] = down


def fold_mlp(evens, others):
    halves, steps, matrices, piece, width = evens.shape
    block = pl.BlockSpec((halves, 1, matrices, piece, width), lambda i: (0, i, 0, 0, 0))
    part = pl.BlockSpec((2, 1, piece, width), lambda i: (0, i, 0, 0))
    return pl.pallas_call(
        fold_mlp_kernel,
        grid=(steps,),
        in_specs=[block, block],
        out_specs=[part] * 4,
        out_shape=[jax.ShapeDtypeStruct((2, steps, piece, width), low)] * 4,
        compiler_params=params(),
        cost_estimate=pl.CostEstimate(
            flops=evens.size, bytes_accessed=6 * evens.size, transcendentals=0
        ),
        name="fold_cores",
    )(evens, others)


def fold_chips_kernel(up, up_other, down, down_other, up_keep, up_send, down_keep, down_send):
    up_keep[...] = add_low(up[0], up_other[0])
    up_send[...] = add_low(up[1], up_other[1])
    down_keep[...] = add_low(down[0], down_other[0])
    down_send[...] = add_low(down[1], down_other[1])


def fold_chips(up, up_other, down, down_other):
    _, steps, piece, width = up.shape
    return pl.pallas_call(
        fold_chips_kernel,
        in_specs=[whole_vmem()] * 4,
        out_specs=[whole_vmem()] * 4,
        out_shape=[jax.ShapeDtypeStruct((steps, piece, width), low)] * 4,
        compiler_params=params(),
        cost_estimate=pl.CostEstimate(
            flops=2 * up.size, bytes_accessed=12 * up.size, transcendentals=0
        ),
        name="fold_chips",
    )(up, up_other, down, down_other)


def fold_last_kernel(up, up_other, down, down_other, *outs):
    for step, out in enumerate(outs):
        out[0] = add_low(up[step], up_other[step])
        out[1] = add_low(down[step], down_other[step])


def fold_last(up, up_other, down, down_other):
    steps, piece, width = up.shape
    return pl.pallas_call(
        fold_last_kernel,
        in_specs=[whole_vmem()] * 4,
        out_specs=[whole_vmem()] * steps,
        out_shape=[jax.ShapeDtypeStruct((2, piece, width), low)] * steps,
        compiler_params=params(),
        cost_estimate=pl.CostEstimate(
            flops=2 * up.size, bytes_accessed=12 * up.size, transcendentals=0
        ),
        name="fold_last",
    )(up, up_other, down, down_other)


def fold_kernel(halves, even_ref, other_ref, *refs):
    steps, piece, _ = even_ref.shape[1:]
    extra = refs[:-halves]
    if extra:
        tail = jnp.concatenate([ref[...] for ref in extra], axis=0).astype(low)
    for half, out in enumerate(refs[-halves:]):
        for step in range(steps):
            rows = pl.ds(step * piece, piece)
            out[rows, :] = add_low(even_ref[half, step], other_ref[half, step])
        if extra:
            out[pl.ds(steps * piece, tail.shape[0]), :] = tail


def fold_pairs(evens, others, *extra):
    halves, steps, piece, width = evens.shape
    rows = steps * piece + sum(array.shape[0] for array in extra)
    return pl.pallas_call(
        functools.partial(fold_kernel, halves),
        in_specs=[whole_vmem()] * (2 + len(extra)),
        out_specs=[whole_vmem()] * halves,
        out_shape=[jax.ShapeDtypeStruct((rows, width), low)] * halves,
        compiler_params=params(),
        cost_estimate=pl.CostEstimate(
            flops=evens.size, bytes_accessed=6 * evens.size, transcendentals=0
        ),
        name="fold_cores",
    )(evens, others, *extra)


def sum_all(values):
    values = [value.astype(wide) for value in values]
    while len(values) > 1:
        values = [values[i] + values[i + 1] for i in range(0, len(values), 2)]
    return values[0].astype(low)


def sum_kernel(terms, *refs):
    refs[terms][...] = sum_all([ref[...] for ref in refs[:terms]])


def sum_terms(terms):
    return pl.pallas_call(
        functools.partial(sum_kernel, len(terms)),
        in_specs=[whole_vmem()] * len(terms),
        out_specs=whole_vmem(),
        out_shape=jax.ShapeDtypeStruct(terms[0].shape, low),
        compiler_params=params(),
        cost_estimate=pl.CostEstimate(
            flops=terms[0].size * len(terms),
            bytes_accessed=10 * terms[0].size,
            transcendentals=0,
        ),
        name="sum_terms",
    )(*terms)


def sum_steps_kernel(terms, extra, done_ref, *refs):
    outs = refs[terms:]
    steps = len(outs)
    rows = outs[0].shape[0]
    first = done_ref.shape[0] // steps
    second = rows - first - extra
    total = sum_all([ref[...] for ref in refs[:terms]])
    for step, out in enumerate(outs):
        out[pl.ds(0, first), :] = done_ref[pl.ds(step * first, first), :]
        out[pl.ds(first, second), :] = total[step * second : (step + 1) * second]
        out[pl.ds(first + second, extra), :] = total[steps * second :]


def sum_steps(done, terms, steps, extra):
    width = done.shape[1]
    rows = done.shape[0] // steps + (terms[0].shape[0] - extra) // steps + extra
    return pl.pallas_call(
        functools.partial(sum_steps_kernel, len(terms), extra),
        in_specs=[whole_vmem()] * (1 + len(terms)),
        out_specs=[whole_vmem()] * steps,
        out_shape=[jax.ShapeDtypeStruct((rows, width), low)] * steps,
        compiler_params=params(),
        cost_estimate=pl.CostEstimate(
            flops=terms[0].size * len(terms),
            bytes_accessed=10 * terms[0].size,
            transcendentals=0,
        ),
        name="sum_steps",
    )(done, *terms)


def solution(mesh):
    seqs = mesh.shape["seq"]
    hids = mesh.shape["hid"]

    def swap(value, axis, step):
        count = mesh.shape[axis]
        return lax.ppermute(value, axis, [(i, i ^ step) for i in range(count)])

    def after(value, *others):
        return lax.optimization_barrier((value, others))[0]

    def spread_chips(array):
        return [array] + [swap(array, "seq", other) for other in range(2, seqs, 2)]

    def spread(array, *others):
        return spread_pairs(spread_chips(array), *others)

    def spread_pairs(evens, *others):
        evens = [after(even, *others) for even in evens] if others else evens
        pieces = []
        for even in evens:
            pieces += [even, swap(even, "seq", 1)]
        return pieces

    def from_hid(own):
        return jnp.stack([swap(own, "hid", step) for step in range(1, hids)])

    def tree_sum(values):
        while len(values) > 1:
            values = [values[i] + values[i + 1] for i in range(0, len(values), 2)]
        return values[0]

    def hid_terms(arrays):
        return [arrays[0]] + [swap(arrays[i], "hid", i) for i in range(1, hids)]

    def reduce_small(value):
        copies = jnp.broadcast_to(value[None], (hids * seqs,) + value.shape)
        return jnp.sum(lax.all_to_all(copies, ("hid", "seq"), 0, 0), axis=0)

    def shards(
        tokens_in,
        image_lengths,
        attn_weight,
        attn_moment,
        attn_average,
        mlp_weight,
        mlp_moment,
        mlp_average,
        vector_params,
        vector_moment,
        vector_average,
        out_grad,
    ):
        packs, rows, width = tokens_in.shape
        share = seqs // packs
        seq_index = lax.axis_index("seq")
        hid_index = lax.axis_index("hid")
        place = jnp.stack([hid_index, seq_index]).astype(jnp.int32)
        attn_piece = attn_weight.shape[0] // seqs
        mlp_piece = mlp_weight.shape[1] // seqs
        aligned = seqs == 8 and attn_piece % 16 == 0 and mlp_piece % 16 == 0
        teams = [[r * packs + b for b in range(packs)] for r in range(share)]

        def exchange(array):
            array = array.reshape(packs, rows, width)
            return lax.all_to_all(array, "seq", 0, 0, axis_index_groups=teams)

        def across_share(array):
            return [array] + [swap(array, "seq", packs * m) for m in range(1, share)]

        tokens = exchange(tokens_in).reshape(packs * rows, width)
        first = (seq_index // packs) * (packs * rows)
        positions = first + jnp.arange(packs * rows, dtype=jnp.int32)
        lengths = lax.dynamic_index_in_dim(image_lengths, seq_index % packs, 0, keepdims=False)
        ends = jnp.cumsum(lengths)
        query_seg = jnp.sum((ends[None, :] <= positions[:, None]).astype(jnp.int32), axis=1)
        valid = (positions < ends[-1]).astype(wide)[:, None]
        key_seg = jnp.concatenate(across_share(query_seg))

        attn_low = attn_weight.astype(low)
        mlp_low = mlp_weight.astype(low)
        if aligned:
            def own_rows(weight, piece):
                return lax.dynamic_slice_in_dim(weight, seq_index * piece, piece, 1).astype(low)

            attn_remote = from_hid(own_rows(attn_weight[None], attn_piece))
            attn_chips = spread_chips(attn_remote)
            whole_attn = None
            def own_row(matrix, other):
                start = (seq_index ^ other) * mlp_piece
                return lax.dynamic_slice_in_dim(matrix, start, mlp_piece, 0).astype(low)

            mlp_own = [(0, 0), (0, 4), (1, 0), (1, 2)]
            mlp_own = jnp.stack([own_row(mlp_weight[m], other) for m, other in mlp_own])
            mlp_steps = [swap(mlp_own, "hid", step) for step in range(1, hids)]
            attn_parts = spread_pairs(attn_chips)
            out_grad = after(out_grad, *attn_chips)
            pieces = [attn_low] + [piece[:, 0] for piece in attn_parts]
        else:
            pieces = []
            ordered = []
            whole_attn = lax.all_gather(attn_low, "hid", axis=0, tiled=True)

        whole_attn, first_low, queries, keys, values = project(
            place, tokens, vector_params, pieces, whole_attn
        )
        keys = jnp.concatenate(across_share(keys))
        values = jnp.concatenate(across_share(values))
        pairs = range(width // 128)
        half = len(pairs) // 2
        first_pairs, last_pairs = pairs[:half], pairs[half:]
        attended = (queries, keys, values, query_seg[:, None], key_seg[None, :], valid)
        attended_first = attention_forward(*attended, first_pairs)
        grad_low = exchange(out_grad).reshape(packs * rows, width)
        if aligned:
            up_here, down_here = split_steps(after(mlp_steps, attended_first[0]))
            up_there = swap(up_here, "seq", 2)
            down_there = swap(down_here, "seq", 4)
            ordered = [up_here, down_here]
            attended_first = after(attended_first, grad_low)
        mixed, log_total = attention_forward(*attended, last_pairs, attended_first, ordered)
        residual, second_low = join(mixed, tokens, whole_attn, vector_params)

        hidden_bias = vector_params[8:].reshape(-1)
        if aligned:
            mlp_weights = [after(up_here, mixed), after(down_here, mixed)]
            mlp_weights += [after(up_there, second_low), after(down_there, second_low)]
            mlp_weights += [swap(array, "seq", 1) for array in mlp_weights]
            even_sources = [((0, 0), (1, 0)), ((2, 0), (1, 1)), ((0, 1), (3, 0)), ((2, 1), (3, 1))]
            sources = []
            for (up_from, up_at), (down_from, down_at) in even_sources:
                sources.append(((up_from, up_at), (down_from, down_at)))
                sources.append(((up_from + 4, up_at), (down_from + 4, down_at)))
            apart = seq_index ^ jnp.arange(seqs)
            away = hid_index ^ jnp.arange(hids)
            bias_pieces = hidden_bias.reshape(hids, seqs, mlp_piece)[away][:, apart]
            mlp_out, second_grad, even_grad, odd_grad, bias_grad = mlp_pieces(
                place,
                second_low,
                grad_low,
                residual,
                vector_params,
                mlp_low,
                mlp_weights,
                sources,
                bias_pieces.reshape(hids, 1, seqs * mlp_piece),
            )
            up_keep, up_send, down_keep, down_send = fold_mlp(
                even_grad, swap(odd_grad, "seq", 1)
            )
            up_other = swap(up_send, "seq", 2)
            down_other = swap(down_send, "seq", 4)
            block_out = exchange(mlp_out)
            ordered = [up_keep]
            bias_grad = bias_grad.reshape(hids, seqs, mlp_piece)[away][:, apart]
        else:
            whole_mlp = lax.all_gather(mlp_low, "hid", axis=1, tiled=True)
            mlp_out, second_grad, up_grad, down_grad, bias_grad = mlp_plain(
                second_low,
                grad_low,
                residual,
                vector_params,
                whole_mlp[0],
                whole_mlp[1],
                hidden_bias,
            )
            mlp_grad = lax.psum_scatter(
                jnp.stack([up_grad, down_grad]), "hid", scatter_dimension=1, tiled=True
            )
            mlp_grad = lax.psum(mlp_grad, "seq").astype(wide)
            block_out = exchange(mlp_out)
            mlp_new = renew(
                mlp_weight, mlp_moment, mlp_average, mlp_grad, weight_decay, matrix_rate
            )

        residual_grad, branch_grad, mixed_grad, delta, branch_sums = branch_back(
            second_grad, residual, grad_low, mixed, valid, whole_attn, vector_params
        )
        attended = (queries, keys, values, mixed_grad, log_total, delta)
        attended += (query_seg[None, :], key_seg[:, None])
        third = len(pairs) // 3
        first_pairs, last_pairs = pairs[: 2 * third], pairs[2 * third :]
        if aligned:
            ordered = [after(ordered[0], block_out)]
        attended_first = attention_backward(*attended, first_pairs, (), ordered)
        if aligned:
            up_keep, up_send, down_keep, down_send = fold_chips(
                up_keep, up_other, down_keep, down_other
            )
            up_other = swap(up_send, "seq", 4)
            down_other = swap(down_send, "seq", 2)
            columns = range(len(first_pairs) * 128)
            even_grad, odd_grad = matrix_grads(
                place, seqs, columns, *attended_first, after(branch_grad, up_keep), first_low, mixed
            )
            mlp_added = fold_last(up_keep, up_other, down_keep, down_other)
            mlp_terms = hid_terms(mlp_added)
            first_folded = fold_pairs(even_grad, swap(odd_grad, "seq", 1))
            first_terms = [first_folded[0]]
            first_terms += [swap(first_folded[i], "seq", 2 * i) for i in range(1, seqs // 2)]
            ordered = []
            attended_first = after(attended_first, mlp_added[0], first_folded[0])
        query_grad, key_grad, value_grad = attention_backward(
            *attended, last_pairs, attended_first, ordered
        )
        if aligned:
            query_grad, key_grad, value_grad = after(
                (query_grad, key_grad, value_grad), *first_terms
            )
        if share > 1:
            count = queries.shape[0]

            def own_share(array):
                terms = [array[:count].astype(wide)]
                for m in range(1, share):
                    part = array[m * count : (m + 1) * count]
                    terms.append(swap(part, "seq", packs * m).astype(wide))
                return tree_sum(terms).astype(low)

            key_grad = own_share(key_grad)
            value_grad = own_share(value_grad)
        if aligned:
            columns = range(len(first_pairs) * 128, width)
            even_grad, odd_grad = matrix_grads(
                place,
                seqs,
                columns,
                query_grad,
                key_grad,
                value_grad,
                branch_grad,
                first_low,
                mixed,
            )
            last_other = swap(odd_grad, "seq", 1)
            residual_grad = after(residual_grad, even_grad)
        else:
            attn_grad = [
                cols_by_cols(query_grad, first_low),
                cols_by_cols(key_grad, first_low),
                cols_by_cols(value_grad, first_low),
                cols_by_cols(branch_grad, mixed),
            ]
            attn_grad = lax.psum_scatter(
                jnp.concatenate(attn_grad).astype(low), "hid", scatter_dimension=0, tiled=True
            )
            attn_grad = lax.psum(attn_grad, "seq").astype(wide)
            attn_new = renew(
                attn_weight, attn_moment, attn_average, attn_grad, weight_decay, matrix_rate
            )
        input_grad, input_sums = input_back(
            query_grad, key_grad, value_grad, whole_attn, tokens, residual_grad, vector_params
        )
        early_rows = jnp.concatenate([branch_sums[:4], bias_grad.reshape(-1, width)])
        if aligned:
            mlp_sums = sum_all([mlp_terms[i] for i in range(hids)])
            mlp_grad = spread(mlp_sums)
            last_folded = fold_pairs(
                even_grad, last_other, after(input_sums, mlp_sums), early_rows
            )
            extra = input_sums.shape[0] + early_rows.shape[0]
            last_terms = [last_folded[0]]
            last_terms += [swap(last_folded[i], "seq", 2 * i) for i in range(1, seqs // 2)]
            first_sum = sum_terms(after(first_terms, last_folded[0]))
            attn_added = sum_steps(first_sum, last_terms, hids, extra)
            input_grad = after(input_grad, *attn_added)
            attn_terms = hid_terms(attn_added)
            mlp_new = renew_pieces(
                place,
                after(mlp_grad, *attn_added),
                [(0, mlp_piece)],
                mlp_weight,
                mlp_moment,
                mlp_average,
            )
            attn_sums = sum_all(after(attn_terms, mlp_new[0]))
            attn_grad = spread(attn_sums)
            first_rows = first_sum.shape[0] // hids
            attn_new = renew_pieces(
                place,
                [piece[None] for piece in attn_grad],
                [(0, first_rows), (first_rows, attn_piece - first_rows)],
                attn_weight[None],
                attn_moment[None],
                attn_average[None],
            )
            attn_new = [array[0] for array in attn_new]
            own = slice(attn_piece, attn_piece + extra)
            small = attn_grad[0][own].astype(wide) + attn_grad[1][own].astype(wide)
        else:
            small = reduce_small(jnp.concatenate([input_sums, early_rows]))
        vector_grad = jnp.concatenate(
            [small[:4], small[10:11], small[8:10], small[11:]], axis=0
        )
        input_grad = exchange(input_grad).astype(wide)
        block_out = block_out.astype(wide)
        vector_new = renew(
            vector_params, vector_moment, vector_average, vector_grad, 0.0, vector_rate
        )
        return (block_out, input_grad, *attn_new, *mlp_new, *vector_new)

    return jax.shard_map(
        shards,
        mesh=mesh,
        in_specs=(
            P("hid", "seq", None),
            P("hid", None),
            P("hid", None),
            P("hid", None),
            P("hid", None),
            P(None, "hid", None),
            P(None, "hid", None),
            P(None, "hid", None),
            P(),
            P(),
            P(),
            P("hid", "seq", None),
        ),
        out_specs=(
            P("hid", "seq", None),
            P("hid", "seq", None),
            P("hid", None),
            P("hid", None),
            P("hid", None),
            P("hid", None),
            P(None, "hid", None),
            P(None, "hid", None),
            P(None, "hid", None),
            P(None, "hid", None),
            P(),
            P(),
            P(),
            P(),
        ),
        check_vma=False,
    )
```

```python
import functools

import jax
import jax.numpy as jnp
from jax import lax
from jax.experimental import pallas as pl
from jax.experimental.pallas import tpu as pltpu
from jax.sharding import PartitionSpec as P

HEADS = 12
HEAD_DIM = 64

score_scale = 0.125
norm_eps = 1e-06
big_negative = -1e30
matrix_rate = 0.0001
vector_rate = 0.001
momentum_decay = 0.9
weight_decay = 0.0001
average_decay = 0.9

low = jnp.bfloat16
wide = jnp.float32
kernel_vmem = 56 * 1024 * 1024


def cost(microseconds):
    return pl.CostEstimate(
        flops=int(4e+08 * microseconds) + 1000, bytes_accessed=1000, transcendentals=0
    )


def rows_by_rows(a, b):
    return lax.dot_general(a, b, (((1,), (1,)), ((), ())), preferred_element_type=wide)


def rows_by_cols(a, b):
    return lax.dot_general(a, b, (((1,), (0,)), ((), ())), preferred_element_type=wide)


def cols_by_cols(a, b):
    return lax.dot_general(a, b, (((0,), (0,)), ((), ())), preferred_element_type=wide)


def normalize(inputs, gain_row, offset):
    center = inputs - jnp.mean(inputs, axis=-1, keepdims=True)
    spread = jnp.mean(center * center, axis=-1, keepdims=True)
    return center * lax.rsqrt(spread + norm_eps) * gain_row + offset


def renew(weight, moment, average, gradient, decay_rate, step_rate):
    step_grad = gradient + decay_rate * weight
    moment_new = momentum_decay * moment + step_grad
    weight_new = weight - step_rate * (step_grad + momentum_decay * moment_new)
    average_new = average_decay * average + (1.0 - average_decay) * weight_new
    return (gradient, moment_new, weight_new, average_new)


def params(**kwargs):
    return pltpu.CompilerParams(vmem_limit_bytes=kernel_vmem, **kwargs)


def smem():
    return pl.BlockSpec(memory_space=pltpu.SMEM)


def whole_vmem():
    return pl.BlockSpec(memory_space=pltpu.VMEM)


def in_place():
    return pl.BlockSpec(memory_space=pl.ANY)


def attention_forward_kernel(tile, q_ref, k_ref, v_ref, query_seg, key_seg, valid_ref, *refs):
    o_ref, lse_ref = refs[-2:]
    rows = q_ref.shape[0]
    lane = lax.broadcasted_iota(jnp.int32, (1, 128), 1)
    k = k_ref[...]
    v = v_ref[...]
    v_and_ones = jnp.concatenate([v, jnp.ones_like(v)], axis=1)
    for start in range(0, rows, tile):
        part = pl.ds(start, tile)
        q = q_ref[part, :]
        same = query_seg[part, :] == key_seg[...]
        heads = []
        for head in range(2):
            mine = (lane // HEAD_DIM) == head
            scores = rows_by_rows(jnp.where(mine, q, jnp.zeros_like(q)), k)
            scores = jnp.where(same, scores, big_negative)
            top = jnp.max(scores, axis=1, keepdims=True)
            weights = jnp.exp(scores - top).astype(low)
            sums = rows_by_cols(weights, v_and_ones)
            total = sums[:, 128:]
            heads.append(sums[:, :128] / total)
            lse_ref[0, head : head + 1, part] = jnp.transpose(top + jnp.log(total))[:1, :]
        joined = jnp.where(lane < HEAD_DIM, heads[0], heads[1]) * valid_ref[part, :]
        o_ref[part, :] = joined.astype(low)


def attention_forward(q, k, v, query_seg, key_seg, valid, pairs, earlier=(), after=()):
    rows, width = q.shape
    keys = k.shape[0]
    column = lambda n: pl.BlockSpec((n, 128), lambda g: (0, pairs[0] + g))
    whole = lambda a: pl.BlockSpec(a.shape, lambda g: (0, 0))
    return pl.pallas_call(
        functools.partial(attention_forward_kernel, min(128, rows)),
        grid=(len(pairs),),
        in_specs=[
            column(rows),
            column(keys),
            column(keys),
            whole(query_seg),
            whole(key_seg),
            whole(valid),
        ]
        + [in_place()] * (len(earlier) + len(after)),
        out_specs=[
            column(rows),
            pl.BlockSpec((1, 2, rows), lambda g: (pairs[0] + g, 0, 0)),
        ],
        out_shape=[
            jax.ShapeDtypeStruct((rows, width), low),
            jax.ShapeDtypeStruct((width // 128, 2, rows), wide),
        ],
        input_output_aliases={6 + i: i for i in range(len(earlier))},
        compiler_params=params(),
        cost_estimate=cost(4 * len(pairs)),
        name="attention_forward",
    )(q, k, v, query_seg, key_seg, valid, *earlier, *after)


def attention_backward_pair(
    tile, q_ref, k_ref, v_ref, do_ref, lse_ref, delta_ref, query_seg, key_seg, sums
):
    dq, dk, dv = sums
    rows = q_ref.shape[0]
    lane = lax.broadcasted_iota(jnp.int32, (1, 128), 1)
    k = k_ref[...]
    v = v_ref[...]
    k_turned = jnp.transpose(k)
    q_turned = jnp.transpose(q_ref[...])
    do_turned = jnp.transpose(do_ref[...])
    for start in range(0, rows, tile):
        part = pl.ds(start, tile)
        q = q_ref[part, :]
        do = do_ref[part, :]
        same = key_seg[...] == query_seg[:, part]
        for head in range(2):
            mine = (lane // HEAD_DIM) == head
            features = slice(head * HEAD_DIM, (head + 1) * HEAD_DIM)
            scores = rows_by_rows(k, jnp.where(mine, q, jnp.zeros_like(q)))
            scores = jnp.where(same, scores, big_negative)
            probs = jnp.exp(scores - lse_ref[0, head : head + 1, part])
            grads = rows_by_rows(v, jnp.where(mine, do, jnp.zeros_like(do)))
            grads = (probs * (grads - delta_ref[0, head : head + 1, part])).astype(low)
            here = slice(start, start + tile)
            dv_term = rows_by_rows(do_turned[features, here], probs.astype(low))
            dk_term = rows_by_rows(q_turned[features, here], grads)
            dq[features, part] = score_scale * rows_by_cols(k_turned[features, :], grads)
            if start == 0:
                dk[features, :] = dk_term
                dv[features, :] = dv_term
            else:
                dk[features, :] += dk_term
                dv[features, :] += dv_term


def attention_backward_kernel(tile, *refs):
    dq_ref, dk_ref, dv_ref, dq, dk, dv = refs[-6:]
    attention_backward_pair(tile, *refs[:8], (dq, dk, dv))
    for out, total in zip((dq_ref, dk_ref, dv_ref), (dq, dk, dv)):
        out[...] = jnp.transpose(total[...].astype(low))


def attention_backward(q, k, v, do, lse, delta, query_seg, key_seg):
    rows, width = q.shape
    keys = k.shape[0]
    pairs = width // 128
    column = lambda n: pl.BlockSpec((n, 128), lambda g: (0, g))
    whole = lambda a: pl.BlockSpec(a.shape, lambda g: (0, 0))
    stat = pl.BlockSpec((1, 2, rows), lambda g: (g, 0, 0))
    return pl.pallas_call(
        functools.partial(attention_backward_kernel, min(256, rows)),
        grid=(pairs,),
        in_specs=[
            column(rows),
            column(keys),
            column(keys),
            column(rows),
            stat,
            stat,
            whole(query_seg),
            whole(key_seg),
        ],
        out_specs=[column(rows), column(keys), column(keys)],
        out_shape=[
            jax.ShapeDtypeStruct((rows, width), low),
            jax.ShapeDtypeStruct((keys, width), low),
            jax.ShapeDtypeStruct((keys, width), low),
        ],
        scratch_shapes=[
            pltpu.VMEM((128, rows), wide),
            pltpu.VMEM((128, keys), wide),
            pltpu.VMEM((128, keys), wide),
        ],
        compiler_params=params(),
        cost_estimate=cost(6 * pairs),
        name="attention_backward",
    )(q, k, v, do, lse, delta, query_seg, key_seg)


def attention_grads_kernel(tile, seqs, place, *refs):
    dt_ref, a_ref, o_ref = refs[8:11]
    dq_ref, dk_ref, dv_ref, even_ref, odd_ref, dq, dk, dv, dq_all, dk_all, dv_all, grads = refs[-12:]
    attention_backward_pair(tile, *refs[:8], (dq, dk, dv))
    pair = pl.program_id(0)
    band = pl.ds(pl.multiple_of(pair * 128, 128), 128)
    for out, total, group in zip(
        (dq_ref, dk_ref, dv_ref), (dq, dk, dv), (dq_all, dk_all, dv_all)
    ):
        rounded = total[...].astype(low)
        out[...] = jnp.transpose(rounded)
        group[band, :] = rounded

    @pl.when(pair == pl.num_programs(0) - 1)
    def _():
        grads[0] = rows_by_cols(dq_all[...], a_ref[...]).astype(low)
        grads[1] = rows_by_cols(dk_all[...], a_ref[...]).astype(low)
        grads[2] = rows_by_cols(dv_all[...], a_ref[...]).astype(low)
        grads[3] = cols_by_cols(dt_ref[...], o_ref[...]).astype(low)
        piece = even_ref.shape[2]
        for other in range(seqs):
            source = pl.ds(pl.multiple_of((place[1] ^ other) * piece, 16), piece)
            target = odd_ref if other % 2 else even_ref
            for matrix in range(4):
                target[other // 2, matrix ^ place[0]] = grads[matrix, source, :]


def attention_grads(
    place, seqs, q, k, v, do, lse, delta, query_seg, key_seg, dt, a, o, pairs, earlier=()
):
    rows, width = q.shape
    count = len(pairs)
    piece = count * 128 // seqs
    group = pairs[0] // count
    column = pl.BlockSpec((rows, 128), lambda g, p: (0, pairs[0] + g))
    fixed = lambda a: pl.BlockSpec(a.shape, lambda g, p: (0,) * len(a.shape))
    stat = pl.BlockSpec((1, 2, rows), lambda g, p: (pairs[0] + g, 0, 0))
    grad = jax.ShapeDtypeStruct((rows, width), low)
    result = jax.ShapeDtypeStruct((seqs // 2, 4, piece, width), low)
    return pl.pallas_call(
        functools.partial(attention_grads_kernel, min(256, rows), seqs),
        grid_spec=pltpu.PrefetchScalarGridSpec(
            num_scalar_prefetch=1,
            grid=(count,),
            in_specs=[column] * 4
            + [
                stat,
                stat,
                fixed(query_seg),
                fixed(key_seg),
                pl.BlockSpec((rows, count * 128), lambda g, p: (0, group)),
                fixed(a),
                fixed(o),
            ]
            + [in_place()] * len(earlier),
            out_specs=[column] * 3 + [fixed(result)] * 2,
            scratch_shapes=[pltpu.VMEM((128, rows), wide)] * 3
            + [pltpu.VMEM((count * 128, rows), low)] * 3
            + [pltpu.VMEM((4, count * 128, width), low)],
        ),
        out_shape=[grad] * 3 + [result] * 2,
        input_output_aliases={12 + i: i for i in range(len(earlier))},
        compiler_params=params(),
        cost_estimate=cost(7 * count),
        name="attention_backward",
    )(place, q, k, v, do, lse, delta, query_seg, key_seg, dt, a, o, *earlier)


def mlp_step(a, dy, up, down, bias):
    before = rows_by_rows(a, up) + bias
    grad_active = rows_by_rows(dy, down)
    density = 0.3989422804014327 * jnp.exp(-0.5 * before * before)
    below = 0.5 * (1.0 + lax.erf(before * 0.7071067811865476))
    active = (before * below).astype(low)
    grad_before = ((below + before * density) * grad_active).astype(low)
    bias_grad = jnp.sum(grad_before.astype(wide), axis=0, keepdims=True)
    up_grad = cols_by_cols(grad_before, a)
    down_grad = cols_by_cols(active, dy)
    return (
        rows_by_cols(active, down),
        rows_by_cols(grad_before, up),
        up_grad,
        down_grad,
        bias_grad,
    )


def add_up(step, steps, h_ref, vec_ref, out_ref, da_ref, out_sum, da_sum, out_term, da_term):
    @pl.when(step == 0)
    def _():
        out_sum[...] = out_term
        da_sum[...] = da_term

    @pl.when(step > 0)
    def _():
        out_sum[...] += out_term
        da_sum[...] += da_term

    @pl.when(step == steps - 1)
    def _():
        out_ref[...] = (h_ref[...] + out_sum[...] + vec_ref[7:8, :]).astype(low)
        da_ref[...] = da_sum[...]


def mlp_plain_kernel(
    a_ref,
    dy_ref,
    h_ref,
    vec_ref,
    up_ref,
    dn_ref,
    hb_ref,
    out_ref,
    da_ref,
    gup,
    gdn,
    ghb,
    out_sum,
    da_sum,
):
    out_term, da_term, up_grad, down_grad, bias_grad = mlp_step(
        a_ref[...], dy_ref[...], up_ref[...], dn_ref[...], hb_ref[0]
    )
    gup[...] = up_grad.astype(low)
    gdn[...] = down_grad.astype(low)
    ghb[0] = bias_grad
    step, steps = pl.program_id(0), pl.num_programs(0)
    add_up(step, steps, h_ref, vec_ref, out_ref, da_ref, out_sum, da_sum, out_term, da_term)


def mlp_plain(a, dy, h, vec, up, down, bias, step_width=768):
    rows, width = a.shape
    hidden = up.shape[0]
    steps = hidden // step_width
    whole = pl.BlockSpec((rows, width), lambda i: (0, 0))
    chunk = pl.BlockSpec((step_width, width), lambda i: (i, 0))
    strip = pl.BlockSpec((1, 1, step_width), lambda i: (i, 0, 0))
    return pl.pallas_call(
        mlp_plain_kernel,
        grid=(steps,),
        in_specs=[whole, whole, whole, pl.BlockSpec(vec.shape, lambda i: (0, 0))]
        + [chunk, chunk, strip],
        out_specs=[whole, whole, chunk, chunk, strip],
        out_shape=[
            jax.ShapeDtypeStruct((rows, width), low),
            jax.ShapeDtypeStruct((rows, width), wide),
        ]
        + [jax.ShapeDtypeStruct((hidden, width), low)] * 2
        + [jax.ShapeDtypeStruct((steps, 1, step_width), wide)],
        scratch_shapes=[pltpu.VMEM((rows, width), wide)] * 2,
        compiler_params=params(),
        name="mlp_both_ways",
    )(a, dy, h, vec, up, down, bias.reshape(steps, 1, step_width))


def norm_parts(rows):
    center = rows - jnp.mean(rows, axis=-1, keepdims=True)
    scale = lax.rsqrt(jnp.mean(center * center, axis=-1, keepdims=True) + norm_eps)
    return center * scale, scale


def norm_back(unit, scale, gain, grad):
    inner = grad * gain
    return scale * (
        inner
        - jnp.mean(inner, axis=-1, keepdims=True)
        - unit * jnp.mean(inner * unit, axis=-1, keepdims=True)
    )


def add_rows(ref, rows, first):
    total = [jnp.sum(row, axis=0, keepdims=True) for row in rows]
    total = jnp.concatenate(total + [jnp.zeros_like(total[0])] * (8 - len(total)), axis=0)

    @pl.when(first)
    def _():
        ref[...] = total

    @pl.when(jnp.logical_not(first))
    def _():
        ref[...] += total


def gather_rows(place, local_ref, piece_refs, out_ref):
    hid_index, seq_index = place[0], place[1]
    quarter = local_ref.shape[0]
    steps, _, rows, _ = piece_refs[0].shape
    out_ref[pl.ds(pl.multiple_of(hid_index * quarter, 16), quarter), :] = local_ref[...]
    for step in range(steps):
        for number, piece_ref in enumerate(piece_refs):
            for chunk, away in enumerate(((0, 4), (2, 6), (0, 2), (4, 6))[number // 2]):
                away += number % 2
                start = (hid_index ^ (step + 1)) * quarter + (seq_index ^ away) * (2 * rows)
                start += (number // 4) * rows
                target = pl.ds(pl.multiple_of(start, 16), rows)
                out_ref[target, :] = piece_ref[step, chunk]


def project_kernel(pieces, place, x_ref, vec_ref, *refs):
    if pieces:
        w_ref, a_ref, q_ref, k_ref, v_ref = refs[pieces:]

        @pl.when(pl.program_id(0) == 0)
        def _():
            gather_rows(place, refs[0], refs[1:pieces], w_ref)

    else:
        w_ref, a_ref, q_ref, k_ref, v_ref = refs
    width = x_ref.shape[1]
    unit, _ = norm_parts(x_ref[...].astype(wide))
    first = (unit * vec_ref[0:1, :] + vec_ref[1:2, :]).astype(low)
    a_ref[...] = first
    q = (rows_by_rows(first, w_ref[0:width, :]) + vec_ref[2:3, :]).astype(low)
    q_ref[...] = (q.astype(wide) * score_scale).astype(low)
    k_ref[...] = rows_by_rows(first, w_ref[width : 2 * width, :]).astype(low)
    v = rows_by_rows(first, w_ref[2 * width : 3 * width, :]) + vec_ref[3:4, :]
    v_ref[...] = v.astype(low)


def row_tile(rows):
    return min(256, rows)


def project(place, x, vec, pieces, whole):
    rows, width = x.shape
    tile = row_tile(rows)
    strip = pl.BlockSpec((tile, width), lambda i, p: (i, 0))
    fixed = lambda a: pl.BlockSpec(a.shape, lambda i, p: (0,) * len(a.shape))
    arrays = pieces if whole is None else [whole]
    matrix = jax.ShapeDtypeStruct((4 * width, width), low)
    strips = [jax.ShapeDtypeStruct((rows, width), low)] * 4
    results = pl.pallas_call(
        functools.partial(project_kernel, len(pieces)),
        grid_spec=pltpu.PrefetchScalarGridSpec(
            num_scalar_prefetch=1,
            grid=(rows // tile,),
            in_specs=[strip, fixed(vec)] + [fixed(a) for a in arrays],
            out_specs=([fixed(matrix)] if whole is None else []) + [strip] * 4,
        ),
        out_shape=([matrix] if whole is None else []) + strips,
        compiler_params=params(),
        cost_estimate=cost(10),
        name="norm_and_project",
    )(place, x, vec, *arrays)
    return results if whole is None else [whole] + list(results)


def join_kernel(o_ref, x_ref, w_ref, vec_ref, h_ref, a_ref):
    joined = x_ref[...].astype(wide) + rows_by_rows(o_ref[...], w_ref[...]) + vec_ref[4:5, :]
    h_ref[...] = joined
    unit, _ = norm_parts(joined)
    a_ref[...] = (unit * vec_ref[5:6, :] + vec_ref[6:7, :]).astype(low)


def join(o, x, w, vec):
    rows, width = x.shape
    tile = row_tile(rows)
    strip = pl.BlockSpec((tile, width), lambda i: (i, 0))
    return pl.pallas_call(
        join_kernel,
        grid=(rows // tile,),
        in_specs=[
            strip,
            strip,
            pl.BlockSpec((width, width), lambda i: (3, 0)),
            pl.BlockSpec(vec.shape, lambda i: (0, 0)),
        ],
        out_specs=[strip, strip],
        out_shape=[
            jax.ShapeDtypeStruct((rows, width), wide),
            jax.ShapeDtypeStruct((rows, width), low),
        ],
        compiler_params=params(),
        cost_estimate=cost(6),
        name="join_and_norm",
    )(o, x, w, vec)


def branch_back_rows(da, h, dy, o, valid, w, vec_ref):
    unit, scale = norm_parts(h)
    dy = dy.astype(wide)
    dh = dy + norm_back(unit, scale, vec_ref[5:6, :], da)
    dt = dh.astype(low)
    do = (rows_by_cols(dt, w) * valid).astype(low)
    product = do.astype(wide) * o.astype(wide)
    width = product.shape[1]
    lane = lax.broadcasted_iota(jnp.int32, (width, 128), 0)
    head = lax.broadcasted_iota(jnp.int32, (width, 128), 1)
    pick = (lane // HEAD_DIM == head).astype(low)
    high = product.astype(low)
    rest = (product - high.astype(wide)).astype(low)
    delta = jnp.transpose(rows_by_cols(high, pick) + rows_by_cols(rest, pick))
    return dh, dt, do, delta, [da * unit, da, dt.astype(wide), dy]


def branch_back_kernel(
    da_ref, h_ref, dy_ref, o_ref, valid_ref, w_ref, vec_ref, dh_ref, dt_ref, do_ref, delta_ref, sums
):
    dh, dt, do, delta, rows = branch_back_rows(
        da_ref[...], h_ref[...], dy_ref[...], o_ref[...], valid_ref[...], w_ref[...], vec_ref
    )
    dh_ref[...] = dh
    dt_ref[...] = dt
    do_ref[...] = do
    for pair in range(delta_ref.shape[0]):
        delta_ref[pair] = delta[2 * pair : 2 * pair + 2, :]
    add_rows(sums, rows, pl.program_id(0) == 0)


def branch_back(da, h, dy, o, valid, w, vec):
    rows, width = h.shape
    tile = row_tile(rows)
    pairs = width // 128
    strip = pl.BlockSpec((tile, width), lambda i: (i, 0))
    return pl.pallas_call(
        branch_back_kernel,
        grid=(rows // tile,),
        in_specs=[
            strip,
            strip,
            strip,
            strip,
            pl.BlockSpec((tile, 1), lambda i: (i, 0)),
            pl.BlockSpec((width, width), lambda i: (3, 0)),
            pl.BlockSpec(vec.shape, lambda i: (0, 0)),
        ],
        out_specs=[
            strip,
            strip,
            strip,
            pl.BlockSpec((pairs, 2, tile), lambda i: (0, 0, i)),
            pl.BlockSpec((8, width), lambda i: (0, 0)),
        ],
        out_shape=[
            jax.ShapeDtypeStruct((rows, width), wide),
            jax.ShapeDtypeStruct((rows, width), low),
            jax.ShapeDtypeStruct((rows, width), low),
            jax.ShapeDtypeStruct((pairs, 2, rows), wide),
            jax.ShapeDtypeStruct((8, width), wide),
        ],
        compiler_params=params(),
        cost_estimate=cost(11),
        name="branch_backward",
    )(da, h, dy, o, valid, w, vec)


def mlp_rows_kernel(count, steps, place, *refs):
    a_ref, dy_ref, h_ref, o_ref, valid_ref, wo_ref, vec_ref, hb_ref, local_ref = refs[:9]
    up_refs, down_refs = refs[9 : 9 + count], refs[9 + count : 9 + 2 * count]
    out_ref, dh_ref, dt_ref, do_ref, delta_ref, sums = refs[9 + 2 * count : 15 + 2 * count]
    even_grad, odd_grad, ghb, active, inner, up, down, a_turned, dy_turned = refs[
        15 + 2 * count : 24 + 2 * count
    ]
    local_done, piece_done = refs[24 + 2 * count :]
    step = pl.program_id(0)
    seq_index = place[1]
    piece = up_refs[0].shape[1]
    units = count * piece
    share = a_turned.shape[0] // count
    tile = h_ref.shape[0]

    def local_copies():
        return [
            pltpu.make_async_copy(
                local_ref.at[matrix], target.at[pl.ds(0, units), :], local_done.at[matrix]
            )
            for matrix, target in enumerate((up, down))
        ]

    def piece_copies(number):
        copies = []
        for other in range(count):
            start = pl.multiple_of(number * units + (seq_index ^ other) * piece, 16)
            for matrix, (sources, target) in enumerate(((up_refs, up), (down_refs, down))):
                copies.append(
                    pltpu.make_async_copy(
                        sources[other].at[number - 1],
                        target.at[pl.ds(start, piece), :],
                        piece_done.at[number - 1, matrix, other],
                    )
                )
        return copies

    @pl.when(step == 0)
    def _():
        for copy in local_copies():
            copy.start()
        for number in range(1, steps):
            for copy in piece_copies(number):
                copy.start()
        for source, target in ((a_ref, a_turned), (dy_ref, dy_turned)):
            turned = jnp.transpose(source[...])
            for owner in range(count):
                start = pl.multiple_of((seq_index ^ owner) * share, 16)
                target[pl.ds(start, share), :] = turned[owner * share : (owner + 1) * share, :]
        for copy in local_copies():
            copy.wait()

    for number in range(1, steps):

        @pl.when(step == number)
        def _(number=number):
            for copy in piece_copies(number):
                copy.wait()

    @pl.when(step < steps)
    def _():
        here = pl.ds(pl.multiple_of(step * units, 128), units)
        before = rows_by_rows(a_ref[...], up[here, :]) + hb_ref[0]
        grad_active = rows_by_rows(dy_ref[...], down[here, :])
        density = 0.3989422804014327 * jnp.exp(-0.5 * before * before)
        below = 0.5 * (1.0 + lax.erf(before * 0.7071067811865476))
        active_now = (before * below).astype(low)
        inner_now = ((below + before * density) * grad_active).astype(low)
        active[:, here] = active_now
        inner[:, here] = inner_now
        ghb[0] = jnp.sum(inner_now.astype(wide), axis=0, keepdims=True)
        up_grad = rows_by_cols(a_turned[...], inner_now).astype(low)
        down_grad = rows_by_cols(dy_turned[...], active_now).astype(low)
        for other in range(count):
            part = slice(other * share, (other + 1) * share)
            target = odd_grad if other % 2 else even_grad
            target[other // 2, 0, 0] = up_grad[part, :]
            target[other // 2, 0, 1] = down_grad[part, :]

    @pl.when(step >= steps)
    def _():
        rows = pl.ds(pl.multiple_of((step - steps) * tile, 16), tile)
        out = h_ref[...] + rows_by_cols(active[rows, :], down[...]) + vec_ref[7:8, :]
        out_ref[...] = out.astype(low)
        da = rows_by_cols(inner[rows, :], up[...])
        dh, dt, do, delta, row_sums = branch_back_rows(
            da, h_ref[...], dy_ref[rows, :], o_ref[...], valid_ref[...], wo_ref[...], vec_ref
        )
        dh_ref[...] = dh
        dt_ref[...] = dt
        do_ref[...] = do
        for pair in range(delta_ref.shape[0]):
            delta_ref[pair] = delta[2 * pair : 2 * pair + 2, :]
        add_rows(sums, row_sums, step == steps)


def mlp_rows(place, a, dy, h, o, valid, w, vec, local, bias, ups, downs):
    rows, width = a.shape
    steps, count, piece = bias.shape[0], len(ups), ups[0].shape[1]
    share = width // count
    tile = row_tile(rows)
    pairs = width // 128
    hidden = steps * count * piece
    once = dict(pipeline_mode=pl.Buffered(1))
    fixed = lambda a: pl.BlockSpec(a.shape, lambda i, p: (0,) * len(a.shape), **once)
    late = lambda i: jnp.maximum(i - steps, 0)
    early = lambda i: jnp.minimum(i, steps - 1)
    strip = pl.BlockSpec((tile, width), lambda i, p: (late(i), 0))
    units = count * piece
    bias_strip = pl.BlockSpec((1, 1, units), lambda i, p: (p[0] ^ early(i), 0, 0))
    grads = pl.BlockSpec((count // 2, 1, 2, share, units), lambda i, p: (0, early(i), 0, 0, 0))
    return pl.pallas_call(
        functools.partial(mlp_rows_kernel, count, steps),
        grid_spec=pltpu.PrefetchScalarGridSpec(
            num_scalar_prefetch=1,
            grid=(steps + rows // tile,),
            in_specs=[
                fixed(a),
                fixed(dy),
                strip,
                strip,
                pl.BlockSpec((tile, 1), lambda i, p: (late(i), 0)),
                pl.BlockSpec((width, width), lambda i, p: (3, 0), **once),
                fixed(vec),
                bias_strip,
            ]
            + [in_place()] * (1 + 2 * count),
            out_specs=[
                strip,
                strip,
                strip,
                strip,
                pl.BlockSpec((pairs, 2, tile), lambda i, p: (0, 0, late(i))),
                pl.BlockSpec((8, width), lambda i, p: (0, 0)),
                grads,
                grads,
                bias_strip,
            ],
            scratch_shapes=[pltpu.VMEM((rows, hidden), low)] * 2
            + [pltpu.VMEM((hidden, width), low)] * 2
            + [pltpu.VMEM((width, rows), low)] * 2
            + [pltpu.SemaphoreType.DMA((2,)), pltpu.SemaphoreType.DMA((steps - 1, 2, count))],
        ),
        out_shape=[
            jax.ShapeDtypeStruct((rows, width), low),
            jax.ShapeDtypeStruct((rows, width), wide),
            jax.ShapeDtypeStruct((rows, width), low),
            jax.ShapeDtypeStruct((rows, width), low),
            jax.ShapeDtypeStruct((pairs, 2, rows), wide),
            jax.ShapeDtypeStruct((8, width), wide),
        ]
        + [jax.ShapeDtypeStruct((count // 2, steps, 2, share, units), low)] * 2
        + [jax.ShapeDtypeStruct(bias.shape, wide)],
        compiler_params=params(),
        cost_estimate=cost(36),
        name="mlp_both_ways",
    )(place, a, dy, h, o, valid, w, vec, bias, local, *ups, *downs)


def input_back_kernel(dq_ref, dk_ref, dv_ref, w_ref, x_ref, dh_ref, vec_ref, out_ref, sums):
    width = x_ref.shape[1]
    da = rows_by_cols(dq_ref[...], w_ref[0:width, :])
    da += rows_by_cols(dk_ref[...], w_ref[width : 2 * width, :])
    da += rows_by_cols(dv_ref[...], w_ref[2 * width : 3 * width, :])
    unit, scale = norm_parts(x_ref[...].astype(wide))
    grad = dh_ref[...] + norm_back(unit, scale, vec_ref[0:1, :], da)
    out_ref[...] = grad.astype(low)
    rows = [da * unit, da, dq_ref[...].astype(wide), dv_ref[...].astype(wide)]
    add_rows(sums, rows, pl.program_id(0) == 0)


def input_back(dq, dk, dv, w, x, dh, vec):
    rows, width = x.shape
    tile = row_tile(rows)
    strip = pl.BlockSpec((tile, width), lambda i: (i, 0))
    return pl.pallas_call(
        input_back_kernel,
        grid=(rows // tile,),
        in_specs=[
            strip,
            strip,
            strip,
            pl.BlockSpec((3 * width, width), lambda i: (0, 0)),
            strip,
            strip,
            pl.BlockSpec(vec.shape, lambda i: (0, 0)),
        ],
        out_specs=[strip, pl.BlockSpec((8, width), lambda i: (0, 0))],
        out_shape=[
            jax.ShapeDtypeStruct((rows, width), low),
            jax.ShapeDtypeStruct((8, width), wide),
        ],
        compiler_params=params(),
        cost_estimate=cost(10),
        name="input_backward",
    )(dq, dk, dv, w, x, dh, vec)


def renew_kernel(count, parts, turned, place, *refs):
    pieces = refs[:count]
    weight, moment, average = refs[count : count + 3]
    outs = refs[count + 3 : count + 7]
    grads = refs[count + 7]
    block = weight.shape[1]

    @pl.when(pl.program_id(0) == 0)
    def _():
        base = 0
        for start, rows in parts:
            for other, piece in enumerate(pieces):
                first = base + (place[1] ^ other) * rows
                target = pl.ds(pl.multiple_of(first, 16), rows)
                grads[:, target, :] = piece[:, start : start + rows, :]
            base += count * rows
        if turned:
            for matrix in range(grads.shape[0]):
                grads[matrix] = jnp.transpose(grads[matrix])

    here = pl.ds(pl.multiple_of(pl.program_id(0) * block, 16), block)
    results = renew(
        weight[...],
        moment[...],
        average[...],
        grads[:, here, :].astype(wide),
        weight_decay,
        matrix_rate,
    )
    for out, value in zip(outs, results):
        out[...] = value


def renew_pieces(place, pieces, parts, weight, moment, average, turned=False):
    matrices, rows, width = weight.shape
    steps = 4
    block = pl.BlockSpec((matrices, rows // steps, width), lambda i, p: (0, i, 0))
    fixed = pl.BlockSpec(pieces[0].shape, lambda i, p: (0, 0, 0))
    return pl.pallas_call(
        functools.partial(renew_kernel, len(pieces), parts, turned),
        grid_spec=pltpu.PrefetchScalarGridSpec(
            num_scalar_prefetch=1,
            grid=(steps,),
            in_specs=[fixed] * len(pieces) + [block] * 3,
            out_specs=[block] * 4,
            scratch_shapes=[pltpu.VMEM(weight.shape, low)],
        ),
        out_shape=[jax.ShapeDtypeStruct(weight.shape, wide)] * 4,
        compiler_params=params(),
        cost_estimate=cost(10),
        name="renew_matrices",
    )(place, *pieces, weight, moment, average)


def add_low(a, b):
    return (a.astype(wide) + b.astype(wide)).astype(low)


def fold_mlp_kernel(even_ref, other_ref, up_keep, up_send, down_keep, down_send):
    for half in range(4):
        up = add_low(even_ref[half, 0, 0], other_ref[half, 0, 0])
        down = add_low(even_ref[half, 0, 1], other_ref[half, 0, 1])
        (up_send if half % 2 else up_keep)[half // 2, 0] = up
        (down_send if half // 2 else down_keep)[half % 2, 0] = down


def fold_mlp(evens, others):
    halves, steps, matrices, piece, width = evens.shape
    block = pl.BlockSpec((halves, 1, matrices, piece, width), lambda i: (0, i, 0, 0, 0))
    part = pl.BlockSpec((2, 1, piece, width), lambda i: (0, i, 0, 0))
    return pl.pallas_call(
        fold_mlp_kernel,
        grid=(steps,),
        in_specs=[block, block],
        out_specs=[part] * 4,
        out_shape=[jax.ShapeDtypeStruct((2, steps, piece, width), low)] * 4,
        compiler_params=params(),
        cost_estimate=cost(4),
        name="fold_cores",
    )(evens, others)


def fold_chips_kernel(up, up_other, down, down_other, up_keep, up_send, down_keep, down_send):
    up_keep[...] = add_low(up[0], up_other[0])
    up_send[...] = add_low(up[1], up_other[1])
    down_keep[...] = add_low(down[0], down_other[0])
    down_send[...] = add_low(down[1], down_other[1])


def fold_chips(up, up_other, down, down_other):
    _, steps, piece, width = up.shape
    return pl.pallas_call(
        fold_chips_kernel,
        in_specs=[whole_vmem()] * 4,
        out_specs=[whole_vmem()] * 4,
        out_shape=[jax.ShapeDtypeStruct((steps, piece, width), low)] * 4,
        compiler_params=params(),
        cost_estimate=cost(4),
        name="fold_chips",
    )(up, up_other, down, down_other)


def fold_last_kernel(up, up_other, down, down_other, *outs):
    for step, out in enumerate(outs):
        out[0] = add_low(up[step], up_other[step])
        out[1] = add_low(down[step], down_other[step])


def fold_last(up, up_other, down, down_other):
    steps, piece, width = up.shape
    return pl.pallas_call(
        fold_last_kernel,
        in_specs=[whole_vmem()] * 4,
        out_specs=[whole_vmem()] * steps,
        out_shape=[jax.ShapeDtypeStruct((2, piece, width), low)] * steps,
        compiler_params=params(),
        cost_estimate=cost(3),
        name="fold_last",
    )(up, up_other, down, down_other)


def fold_kernel(halves, groups, *refs):
    evens, others, outs = refs[:groups], refs[groups : 2 * groups], refs[2 * groups :]
    for half, out in enumerate(outs):
        at = 0
        for step in range(evens[0].shape[1]):
            for even_ref, other_ref in zip(evens, others):
                rows = pl.ds(at, even_ref.shape[2])
                out[rows, :] = add_low(even_ref[half, step], other_ref[half, step])
                at += even_ref.shape[2]


def fold_pairs(evens, others):
    halves, steps, _, width = evens[0].shape
    rows = steps * sum(array.shape[2] for array in evens)
    return pl.pallas_call(
        functools.partial(fold_kernel, halves, len(evens)),
        in_specs=[whole_vmem()] * (2 * len(evens)),
        out_specs=[whole_vmem()] * halves,
        out_shape=[jax.ShapeDtypeStruct((rows, width), low)] * halves,
        compiler_params=params(),
        cost_estimate=cost(4),
        name="fold_cores",
    )(*evens, *others)


def sum_all(values):
    values = [value.astype(wide) for value in values]
    while len(values) > 1:
        values = [values[i] + values[i + 1] for i in range(0, len(values), 2)]
    return values[0].astype(low)


def sum_steps_kernel(terms, *refs):
    extra, outs = refs[terms : terms + 2], refs[terms + 2 :]
    total = sum_all([ref[...] for ref in refs[:terms]])
    tail = jnp.concatenate([ref[...] for ref in extra], axis=0).astype(low)
    rows = total.shape[0] // len(outs)
    for step, out in enumerate(outs):
        out[pl.ds(0, rows), :] = total[step * rows : (step + 1) * rows]
        out[pl.ds(rows, tail.shape[0]), :] = tail


def sum_steps(terms, steps, *extra):
    rows, width = terms[0].shape
    rows = rows // steps + sum(array.shape[0] for array in extra)
    return pl.pallas_call(
        functools.partial(sum_steps_kernel, len(terms)),
        in_specs=[whole_vmem()] * (len(terms) + 2),
        out_specs=[whole_vmem()] * steps,
        out_shape=[jax.ShapeDtypeStruct((rows, width), low)] * steps,
        compiler_params=params(),
        cost_estimate=cost(2),
        name="sum_steps",
    )(*terms, *extra)


def solution(mesh):
    seqs = mesh.shape["seq"]
    hids = mesh.shape["hid"]

    def swap(value, axis, step):
        count = mesh.shape[axis]
        return lax.ppermute(value, axis, [(i, i ^ step) for i in range(count)])

    def after(value, *others):
        return lax.optimization_barrier((value, others))[0]

    def spread_chips(array):
        return [array] + [swap(array, "seq", other) for other in range(2, seqs, 2)]

    def spread_pairs(evens):
        pieces = []
        for even in evens:
            pieces += [even, swap(even, "seq", 1)]
        return pieces

    def tree_sum(values):
        while len(values) > 1:
            values = [values[i] + values[i + 1] for i in range(0, len(values), 2)]
        return values[0]

    def hid_terms(arrays):
        return [arrays[0]] + [swap(arrays[i], "hid", i) for i in range(1, hids)]

    def seq_terms(arrays):
        return [arrays[0]] + [swap(arrays[i], "seq", 2 * i) for i in range(1, seqs // 2)]

    def exchange(array, packs, rows):
        teams = [[r * packs + b for b in range(packs)] for r in range(seqs // packs)]
        array = array.reshape(packs, rows, array.shape[-1])
        return lax.all_to_all(array, "seq", 0, 0, axis_index_groups=teams)

    def image_parts(image_lengths, packs, rows):
        seq_index = lax.axis_index("seq")
        first = (seq_index // packs) * (packs * rows)
        positions = first + jnp.arange(packs * rows, dtype=jnp.int32)
        lengths = lax.dynamic_index_in_dim(image_lengths, seq_index % packs, 0, keepdims=False)
        ends = jnp.cumsum(lengths)
        query_seg = jnp.sum((ends[None, :] <= positions[:, None]).astype(jnp.int32), axis=1)
        return query_seg, (positions < ends[-1]).astype(wide)[:, None]

    def vector_rows(small):
        return jnp.concatenate([small[:4], small[10:11], small[8:10], small[11:16]], axis=0)

    def shards_general(
        tokens_in,
        image_lengths,
        attn_weight,
        attn_moment,
        attn_average,
        mlp_weight,
        mlp_moment,
        mlp_average,
        vector_params,
        vector_moment,
        vector_average,
        out_grad,
    ):
        packs, rows, width = tokens_in.shape
        share = seqs // packs

        def across_share(array):
            return [array] + [swap(array, "seq", packs * m) for m in range(1, share)]

        place = jnp.stack([lax.axis_index("hid"), lax.axis_index("seq")]).astype(jnp.int32)
        tokens = exchange(tokens_in, packs, rows).reshape(packs * rows, width)
        grad_low = exchange(out_grad, packs, rows).reshape(packs * rows, width)
        query_seg, valid = image_parts(image_lengths, packs, rows)
        key_seg = jnp.concatenate(across_share(query_seg))
        whole_attn = lax.all_gather(attn_weight.astype(low), "hid", axis=0, tiled=True)
        whole_mlp = lax.all_gather(mlp_weight.astype(low), "hid", axis=1, tiled=True)
        whole_attn, first_low, queries, keys, values = project(
            place, tokens, vector_params, [], whole_attn
        )
        keys = jnp.concatenate(across_share(keys))
        values = jnp.concatenate(across_share(values))
        pairs = range(width // 128)
        mixed, log_total = attention_forward(
            queries, keys, values, query_seg[:, None], key_seg[None, :], valid, pairs
        )
        residual, second_low = join(mixed, tokens, whole_attn, vector_params)
        hidden_bias = vector_params[8:].reshape(-1)
        mlp_out, second_grad, up_grad, down_grad, bias_grad = mlp_plain(
            second_low,
            grad_low,
            residual,
            vector_params,
            whole_mlp[0],
            whole_mlp[1],
            hidden_bias,
        )
        block_out = exchange(mlp_out, packs, rows).astype(wide)
        mlp_grad = lax.psum_scatter(
            jnp.stack([up_grad, down_grad]), "hid", scatter_dimension=1, tiled=True
        )
        mlp_grad = lax.psum(mlp_grad, "seq").astype(wide)
        residual_grad, branch_grad, mixed_grad, delta, branch_sums = branch_back(
            second_grad, residual, grad_low, mixed, valid, whole_attn, vector_params
        )
        query_grad, key_grad, value_grad = attention_backward(
            queries,
            keys,
            values,
            mixed_grad,
            log_total,
            delta,
            query_seg[None, :],
            key_seg[:, None],
        )
        count = queries.shape[0]

        def own_share(array):
            terms = [array[:count]]
            for m in range(1, share):
                terms.append(swap(array[m * count : (m + 1) * count], "seq", packs * m))
            return sum_all(terms)

        key_grad = own_share(key_grad)
        value_grad = own_share(value_grad)
        input_grad, input_sums = input_back(
            query_grad, key_grad, value_grad, whole_attn, tokens, residual_grad, vector_params
        )
        input_grad = exchange(input_grad, packs, rows).astype(wide)
        attn_grad = [
            cols_by_cols(query_grad, first_low),
            cols_by_cols(key_grad, first_low),
            cols_by_cols(value_grad, first_low),
            cols_by_cols(branch_grad, mixed),
        ]
        attn_grad = lax.psum_scatter(
            jnp.concatenate(attn_grad).astype(low), "hid", scatter_dimension=0, tiled=True
        )
        attn_grad = lax.psum(attn_grad, "seq").astype(wide)
        small = jnp.concatenate([input_sums, branch_sums[:4], bias_grad.reshape(-1, width)])
        copies = jnp.broadcast_to(small[None], (hids * seqs,) + small.shape)
        small = jnp.sum(lax.all_to_all(copies, ("hid", "seq"), 0, 0), axis=0)
        rates = (weight_decay, matrix_rate)
        return (
            block_out,
            input_grad,
            *renew(attn_weight, attn_moment, attn_average, attn_grad, *rates),
            *renew(mlp_weight, mlp_moment, mlp_average, mlp_grad, *rates),
            *renew(
                vector_params, vector_moment, vector_average, vector_rows(small), 0.0, vector_rate
            ),
        )

    def shards(
        tokens_in,
        image_lengths,
        attn_weight,
        attn_moment,
        attn_average,
        mlp_weight,
        mlp_moment,
        mlp_average,
        vector_params,
        vector_moment,
        vector_average,
        out_grad,
    ):
        packs, rows, width = tokens_in.shape
        seq_index = lax.axis_index("seq")
        hid_index = lax.axis_index("hid")
        place = jnp.stack([hid_index, seq_index]).astype(jnp.int32)
        attn_piece = attn_weight.shape[0] // seqs
        mlp_piece = mlp_weight.shape[1] // seqs
        pairs = range(width // 128)

        def own_row(matrix, piece, other=0):
            start = (seq_index ^ other) * piece
            return lax.dynamic_slice_in_dim(matrix, start, piece, 0).astype(low)

        attn_half = attn_piece // 2
        attn_own = [own_row(attn_weight, attn_piece, other)[:attn_half] for other in (0, 4)]
        attn_own += [own_row(attn_weight, attn_piece, other)[attn_half:] for other in (0, 2)]
        attn_steps = hid_terms([jnp.stack(attn_own)] * hids)[1:]
        tokens = exchange(tokens_in, packs, rows).reshape(packs * rows, width)
        attn_low = attn_weight.astype(low)
        up_own, down_own = [own_row(matrix, mlp_piece) for matrix in mlp_weight]
        attn_steps = after(attn_steps, attn_low, up_own, down_own, tokens)
        first_here = jnp.stack([step[:2] for step in attn_steps])
        last_here = jnp.stack([step[2:] for step in attn_steps])
        attn_chips = [first_here, swap(first_here, "seq", 2), last_here, swap(last_here, "seq", 4)]
        up_here = jnp.stack(hid_terms([after(up_own, first_here)] * hids)[1:])
        query_seg, valid = image_parts(image_lengths, packs, rows)
        mlp_low = mlp_weight.astype(low)
        bias_pieces = vector_params[8:].reshape(hids, 1, seqs * mlp_piece)
        query_seg_rows, key_seg_rows = query_seg[:, None], query_seg[None, :]
        ready = (up_here, mlp_low, bias_pieces, query_seg_rows, key_seg_rows, valid)
        attn_chips = after(attn_chips, *ready)
        pieces = [attn_low] + spread_pairs(attn_chips)
        grad_low = exchange(after(out_grad, *attn_chips), packs, rows)
        grad_low = grad_low.reshape(packs * rows, width)
        up_here = after(up_here, *attn_chips)
        up_x, up_y = swap(up_here, "seq", 2), swap(up_here, "seq", 4)
        down_steps = hid_terms([after(down_own, *attn_chips)] * hids)[1:]

        whole_attn, first_low, queries, keys, values = project(
            place, tokens, vector_params, pieces, None
        )
        down_here = jnp.stack(after(down_steps, queries))
        down_x, down_y = swap(down_here, "seq", 2), swap(down_here, "seq", 4)
        queries = after(queries, down_here)
        attended = (queries, keys, values, query_seg_rows, key_seg_rows, valid)
        half = len(pairs) // 2
        part = attention_forward(*attended, pairs[:half])
        mixed, log_total = attention_forward(*attended, pairs[half:], part)
        up_far = swap(after(up_x, mixed), "seq", 4)
        down_far = swap(after(down_y, mixed), "seq", 2)
        residual, second_low = join(mixed, tokens, whole_attn, vector_params)
        ups = [up_here, up_x, up_y, up_far]
        downs = [down_here, down_x, down_y, down_far]
        ups = after(ups[:3], mixed) + after(ups[3:], second_low)
        downs = after(downs[:3], mixed) + after(downs[3:], second_low)
        mlp_out, residual_grad, branch_grad, mixed_grad, delta, branch_sums, *mlp_grads = mlp_rows(
            place,
            second_low,
            grad_low,
            residual,
            mixed,
            valid,
            whole_attn,
            vector_params,
            mlp_low,
            bias_pieces,
            spread_pairs(ups),
            spread_pairs(downs),
        )
        even_grad, odd_grad, bias_grad = mlp_grads

        other_grad = swap(odd_grad, "seq", 1)
        block_out = exchange(mlp_out, packs, rows)
        early_rows = jnp.concatenate([branch_sums[:4], bias_grad.reshape(-1, width)])
        attended = (queries, keys, values, mixed_grad, log_total, delta)
        attended += (key_seg_rows, query_seg_rows)
        attended += (branch_grad, first_low, mixed)
        *part, first_even, first_odd = attention_grads(place, seqs, *attended, pairs[:half])
        even_grad = after(even_grad, first_even, block_out)
        up_keep, up_send, down_keep, down_send = fold_mlp(even_grad, other_grad)
        up_other = swap(up_send, "seq", 2)
        down_other = swap(down_send, "seq", 4)
        first_other = swap(first_odd, "seq", 1)
        part = after(part, up_keep)
        *part, last_even, last_odd = attention_grads(place, seqs, *attended, pairs[half:], part)
        up_keep, up_send, down_keep, down_send = fold_chips(
            after(up_keep, last_even), up_other, down_keep, down_other
        )
        up_other = swap(up_send, "seq", 4)
        down_other = swap(down_send, "seq", 2)
        last_other = swap(last_odd, "seq", 1)
        attn_folded = fold_pairs(
            after([first_even, last_even], up_keep), [first_other, last_other]
        )
        attn_terms = seq_terms(attn_folded)
        query_grad, key_grad, value_grad = after(part, attn_folded[0])
        input_grad, input_sums = input_back(
            query_grad, key_grad, value_grad, whole_attn, tokens, residual_grad, vector_params
        )
        mlp_added = fold_last(after(up_keep, input_sums), up_other, down_keep, down_other)
        mlp_terms = hid_terms(mlp_added)
        extra = input_sums.shape[0] + early_rows.shape[0]
        attn_terms = after(attn_terms, mlp_added[0])
        attn_added = sum_steps(attn_terms, hids, input_sums, early_rows)
        mlp_sums = sum_all(after(mlp_terms, attn_added[0]))
        mlp_chips = spread_chips(mlp_sums)
        attn_terms = hid_terms(attn_added)
        input_grad = exchange(after(input_grad, mlp_sums), packs, rows)
        attn_sums = sum_all(attn_terms)
        attn_grad = spread_chips(attn_sums)
        mlp_grad = spread_pairs(after(mlp_chips, attn_sums))
        mlp_new = renew_pieces(
            place,
            mlp_grad,
            [(0, width // seqs)],
            mlp_weight,
            mlp_moment,
            mlp_average,
            turned=True,
        )
        attn_grad = spread_pairs(after(attn_grad, mlp_new[0]))
        group_rows = attn_piece // 2
        attn_new = renew_pieces(
            place,
            [piece[None] for piece in attn_grad],
            [(group * group_rows, group_rows) for group in range(2)],
            attn_weight[None],
            attn_moment[None],
            attn_average[None],
        )
        own = slice(attn_piece, attn_piece + extra)
        small = tree_sum([piece[own].astype(wide) for piece in attn_grad])
        return (
            block_out.astype(wide),
            input_grad.astype(wide),
            *[array[0] for array in attn_new],
            *mlp_new,
            *renew(
                vector_params, vector_moment, vector_average, vector_rows(small), 0.0, vector_rate
            ),
        )

    def whole(*arrays):
        pieces = [arrays[2].shape[0] // seqs, arrays[5].shape[1] // seqs]
        fits = seqs == 8 and arrays[0].shape[0] == 8 and all(n % 96 == 0 for n in pieces)
        return (shards if fits else shards_general)(*arrays)

    return jax.shard_map(
        whole,
        mesh=mesh,
        in_specs=(
            P("hid", "seq", None),
            P("hid", None),
            P("hid", None),
            P("hid", None),
            P("hid", None),
            P(None, "hid", None),
            P(None, "hid", None),
            P(None, "hid", None),
            P(),
            P(),
            P(),
            P("hid", "seq", None),
        ),
        out_specs=(
            P("hid", "seq", None),
            P("hid", "seq", None),
            P("hid", None),
            P("hid", None),
            P("hid", None),
            P("hid", None),
            P(None, "hid", None),
            P(None, "hid", None),
            P(None, "hid", None),
            P(None, "hid", None),
            P(),
            P(),
            P(),
            P(),
        ),
        check_vma=False,
    )
```

```python
import functools

import jax
import jax.numpy as jnp
from jax import lax
from jax.experimental import pallas as pl
from jax.experimental.pallas import tpu as pltpu
from jax.sharding import PartitionSpec as P

HEADS = 12
HEAD_DIM = 64

score_scale = 0.125
norm_eps = 1e-06
big_negative = -1e30
matrix_rate = 0.0001
vector_rate = 0.001
momentum_decay = 0.9
weight_decay = 0.0001
average_decay = 0.9

low = jnp.bfloat16
wide = jnp.float32
kernel_vmem = 56 * 1024 * 1024


def cost(microseconds):
    return pl.CostEstimate(
        flops=int(4e+08 * microseconds) + 1000, bytes_accessed=1000, transcendentals=0
    )


def rows_by_rows(a, b):
    return lax.dot_general(a, b, (((1,), (1,)), ((), ())), preferred_element_type=wide)


def rows_by_cols(a, b):
    return lax.dot_general(a, b, (((1,), (0,)), ((), ())), preferred_element_type=wide)


def cols_by_cols(a, b):
    return lax.dot_general(a, b, (((0,), (0,)), ((), ())), preferred_element_type=wide)


def normalize(inputs, gain_row, offset):
    center = inputs - jnp.mean(inputs, axis=-1, keepdims=True)
    spread = jnp.mean(center * center, axis=-1, keepdims=True)
    return center * lax.rsqrt(spread + norm_eps) * gain_row + offset


def renew(weight, moment, average, gradient, decay_rate, step_rate):
    step_grad = gradient + decay_rate * weight
    moment_new = momentum_decay * moment + step_grad
    weight_new = weight - step_rate * (step_grad + momentum_decay * moment_new)
    average_new = average_decay * average + (1.0 - average_decay) * weight_new
    return (gradient, moment_new, weight_new, average_new)


def params(**kwargs):
    return pltpu.CompilerParams(vmem_limit_bytes=kernel_vmem, **kwargs)


def smem():
    return pl.BlockSpec(memory_space=pltpu.SMEM)


def whole_vmem():
    return pl.BlockSpec(memory_space=pltpu.VMEM)


def in_place():
    return pl.BlockSpec(memory_space=pl.ANY)


def attention_forward_kernel(tile, q_ref, k_ref, v_ref, query_seg, key_seg, valid_ref, *refs):
    o_ref, lse_ref = refs[-2:]
    rows = q_ref.shape[0]
    lane = lax.broadcasted_iota(jnp.int32, (1, 128), 1)
    k = k_ref[...]
    v = v_ref[...]
    v_and_ones = jnp.concatenate([v, jnp.ones_like(v)], axis=1)
    for start in range(0, rows, tile):
        part = pl.ds(start, tile)
        q = q_ref[part, :]
        same = query_seg[part, :] == key_seg[...]
        heads = []
        for head in range(2):
            mine = (lane // HEAD_DIM) == head
            scores = rows_by_rows(jnp.where(mine, q, jnp.zeros_like(q)), k)
            scores = jnp.where(same, scores, big_negative)
            top = jnp.max(scores, axis=1, keepdims=True)
            weights = jnp.exp(scores - top).astype(low)
            sums = rows_by_cols(weights, v_and_ones)
            total = sums[:, 128:]
            heads.append(sums[:, :128] / total)
            lse_ref[0, head : head + 1, part] = jnp.transpose(top + jnp.log(total))[:1, :]
        joined = jnp.where(lane < HEAD_DIM, heads[0], heads[1]) * valid_ref[part, :]
        o_ref[part, :] = joined.astype(low)


def attention_forward(q, k, v, query_seg, key_seg, valid, pairs, earlier=(), after=()):
    rows, width = q.shape
    keys = k.shape[0]
    column = lambda n: pl.BlockSpec((n, 128), lambda g: (0, pairs[0] + g))
    whole = lambda a: pl.BlockSpec(a.shape, lambda g: (0, 0))
    return pl.pallas_call(
        functools.partial(attention_forward_kernel, min(128, rows)),
        grid=(len(pairs),),
        in_specs=[
            column(rows),
            column(keys),
            column(keys),
            whole(query_seg),
            whole(key_seg),
            whole(valid),
        ]
        + [in_place()] * (len(earlier) + len(after)),
        out_specs=[
            column(rows),
            pl.BlockSpec((1, 2, rows), lambda g: (pairs[0] + g, 0, 0)),
        ],
        out_shape=[
            jax.ShapeDtypeStruct((rows, width), low),
            jax.ShapeDtypeStruct((width // 128, 2, rows), wide),
        ],
        input_output_aliases={6 + i: i for i in range(len(earlier))},
        compiler_params=params(),
        cost_estimate=cost(4 * len(pairs)),
        name="attention_forward",
    )(q, k, v, query_seg, key_seg, valid, *earlier, *after)


def attention_backward_pair(
    tile, q_ref, k_ref, v_ref, do_ref, lse_ref, delta_ref, query_seg, key_seg, sums
):
    dq, dk, dv = sums
    rows = q_ref.shape[0]
    lane = lax.broadcasted_iota(jnp.int32, (1, 128), 1)
    k = k_ref[...]
    v = v_ref[...]
    k_turned = jnp.transpose(k)
    q_turned = jnp.transpose(q_ref[...])
    do_turned = jnp.transpose(do_ref[...])
    for start in range(0, rows, tile):
        part = pl.ds(start, tile)
        q = q_ref[part, :]
        do = do_ref[part, :]
        same = key_seg[...] == query_seg[:, part]
        for head in range(2):
            mine = (lane // HEAD_DIM) == head
            features = slice(head * HEAD_DIM, (head + 1) * HEAD_DIM)
            scores = rows_by_rows(k, jnp.where(mine, q, jnp.zeros_like(q)))
            scores = jnp.where(same, scores, big_negative)
            probs = jnp.exp(scores - lse_ref[0, head : head + 1, part])
            grads = rows_by_rows(v, jnp.where(mine, do, jnp.zeros_like(do)))
            grads = (probs * (grads - delta_ref[0, head : head + 1, part])).astype(low)
            here = slice(start, start + tile)
            dv_term = rows_by_rows(do_turned[features, here], probs.astype(low))
            dk_term = rows_by_rows(q_turned[features, here], grads)
            dq[features, part] = score_scale * rows_by_cols(k_turned[features, :], grads)
            if start == 0:
                dk[features, :] = dk_term
                dv[features, :] = dv_term
            else:
                dk[features, :] += dk_term
                dv[features, :] += dv_term


def attention_backward_kernel(tile, *refs):
    dq_ref, dk_ref, dv_ref, dq, dk, dv = refs[-6:]
    attention_backward_pair(tile, *refs[:8], (dq, dk, dv))
    for out, total in zip((dq_ref, dk_ref, dv_ref), (dq, dk, dv)):
        out[...] = jnp.transpose(total[...].astype(low))


def attention_backward(q, k, v, do, lse, delta, query_seg, key_seg):
    rows, width = q.shape
    keys = k.shape[0]
    pairs = width // 128
    column = lambda n: pl.BlockSpec((n, 128), lambda g: (0, g))
    whole = lambda a: pl.BlockSpec(a.shape, lambda g: (0, 0))
    stat = pl.BlockSpec((1, 2, rows), lambda g: (g, 0, 0))
    return pl.pallas_call(
        functools.partial(attention_backward_kernel, min(256, rows)),
        grid=(pairs,),
        in_specs=[
            column(rows),
            column(keys),
            column(keys),
            column(rows),
            stat,
            stat,
            whole(query_seg),
            whole(key_seg),
        ],
        out_specs=[column(rows), column(keys), column(keys)],
        out_shape=[
            jax.ShapeDtypeStruct((rows, width), low),
            jax.ShapeDtypeStruct((keys, width), low),
            jax.ShapeDtypeStruct((keys, width), low),
        ],
        scratch_shapes=[
            pltpu.VMEM((128, rows), wide),
            pltpu.VMEM((128, keys), wide),
            pltpu.VMEM((128, keys), wide),
        ],
        compiler_params=params(),
        cost_estimate=cost(6 * pairs),
        name="attention_backward",
    )(q, k, v, do, lse, delta, query_seg, key_seg)


def attention_grads_kernel(tile, seqs, place, *refs):
    dt_ref, a_ref, o_ref = refs[8:11]
    dq_ref, dk_ref, dv_ref, even_ref, odd_ref, dq, dk, dv, dq_all, dk_all, dv_all, grads = refs[-12:]
    attention_backward_pair(tile, *refs[:8], (dq, dk, dv))
    pair = pl.program_id(0)
    band = pl.ds(pl.multiple_of(pair * 128, 128), 128)
    for out, total, group in zip(
        (dq_ref, dk_ref, dv_ref), (dq, dk, dv), (dq_all, dk_all, dv_all)
    ):
        rounded = total[...].astype(low)
        out[...] = jnp.transpose(rounded)
        group[band, :] = rounded

    @pl.when(pair == pl.num_programs(0) - 1)
    def _():
        grads[0] = rows_by_cols(dq_all[...], a_ref[...]).astype(low)
        grads[1] = rows_by_cols(dk_all[...], a_ref[...]).astype(low)
        grads[2] = rows_by_cols(dv_all[...], a_ref[...]).astype(low)
        grads[3] = cols_by_cols(dt_ref[...], o_ref[...]).astype(low)
        piece = even_ref.shape[2]
        for other in range(seqs):
            source = pl.ds(pl.multiple_of((place[1] ^ other) * piece, 16), piece)
            target = odd_ref if other % 2 else even_ref
            for matrix in range(4):
                target[other // 2, matrix ^ place[0]] = grads[matrix, source, :]


def attention_grads(
    place, seqs, q, k, v, do, lse, delta, query_seg, key_seg, dt, a, o, pairs, earlier=()
):
    rows, width = q.shape
    count = len(pairs)
    piece = count * 128 // seqs
    group = pairs[0] // count
    column = pl.BlockSpec((rows, 128), lambda g, p: (0, pairs[0] + g))
    fixed = lambda a: pl.BlockSpec(a.shape, lambda g, p: (0,) * len(a.shape))
    stat = pl.BlockSpec((1, 2, rows), lambda g, p: (pairs[0] + g, 0, 0))
    grad = jax.ShapeDtypeStruct((rows, width), low)
    result = jax.ShapeDtypeStruct((seqs // 2, 4, piece, width), low)
    return pl.pallas_call(
        functools.partial(attention_grads_kernel, min(256, rows), seqs),
        grid_spec=pltpu.PrefetchScalarGridSpec(
            num_scalar_prefetch=1,
            grid=(count,),
            in_specs=[column] * 4
            + [
                stat,
                stat,
                fixed(query_seg),
                fixed(key_seg),
                pl.BlockSpec((rows, count * 128), lambda g, p: (0, group)),
                fixed(a),
                fixed(o),
            ]
            + [in_place()] * len(earlier),
            out_specs=[column] * 3 + [fixed(result)] * 2,
            scratch_shapes=[pltpu.VMEM((128, rows), wide)] * 3
            + [pltpu.VMEM((count * 128, rows), low)] * 3
            + [pltpu.VMEM((4, count * 128, width), low)],
        ),
        out_shape=[grad] * 3 + [result] * 2,
        input_output_aliases={12 + i: i for i in range(len(earlier))},
        compiler_params=params(),
        cost_estimate=cost(7 * count),
        name="attention_backward",
    )(place, q, k, v, do, lse, delta, query_seg, key_seg, dt, a, o, *earlier)


def mlp_step(a, dy, up, down, bias):
    before = rows_by_rows(a, up) + bias
    grad_active = rows_by_rows(dy, down)
    density = 0.3989422804014327 * jnp.exp(-0.5 * before * before)
    below = 0.5 * (1.0 + lax.erf(before * 0.7071067811865476))
    active = (before * below).astype(low)
    grad_before = ((below + before * density) * grad_active).astype(low)
    bias_grad = jnp.sum(grad_before.astype(wide), axis=0, keepdims=True)
    up_grad = cols_by_cols(grad_before, a)
    down_grad = cols_by_cols(active, dy)
    return (
        rows_by_cols(active, down),
        rows_by_cols(grad_before, up),
        up_grad,
        down_grad,
        bias_grad,
    )


def add_up(step, steps, h_ref, vec_ref, out_ref, da_ref, out_sum, da_sum, out_term, da_term):
    @pl.when(step == 0)
    def _():
        out_sum[...] = out_term
        da_sum[...] = da_term

    @pl.when(step > 0)
    def _():
        out_sum[...] += out_term
        da_sum[...] += da_term

    @pl.when(step == steps - 1)
    def _():
        out_ref[...] = (h_ref[...] + out_sum[...] + vec_ref[7:8, :]).astype(low)
        da_ref[...] = da_sum[...]


def mlp_plain_kernel(
    a_ref,
    dy_ref,
    h_ref,
    vec_ref,
    up_ref,
    dn_ref,
    hb_ref,
    out_ref,
    da_ref,
    gup,
    gdn,
    ghb,
    out_sum,
    da_sum,
):
    out_term, da_term, up_grad, down_grad, bias_grad = mlp_step(
        a_ref[...], dy_ref[...], up_ref[...], dn_ref[...], hb_ref[0]
    )
    gup[...] = up_grad.astype(low)
    gdn[...] = down_grad.astype(low)
    ghb[0] = bias_grad
    step, steps = pl.program_id(0), pl.num_programs(0)
    add_up(step, steps, h_ref, vec_ref, out_ref, da_ref, out_sum, da_sum, out_term, da_term)


def mlp_plain(a, dy, h, vec, up, down, bias, step_width=768):
    rows, width = a.shape
    hidden = up.shape[0]
    steps = hidden // step_width
    whole = pl.BlockSpec((rows, width), lambda i: (0, 0))
    chunk = pl.BlockSpec((step_width, width), lambda i: (i, 0))
    strip = pl.BlockSpec((1, 1, step_width), lambda i: (i, 0, 0))
    return pl.pallas_call(
        mlp_plain_kernel,
        grid=(steps,),
        in_specs=[whole, whole, whole, pl.BlockSpec(vec.shape, lambda i: (0, 0))]
        + [chunk, chunk, strip],
        out_specs=[whole, whole, chunk, chunk, strip],
        out_shape=[
            jax.ShapeDtypeStruct((rows, width), low),
            jax.ShapeDtypeStruct((rows, width), wide),
        ]
        + [jax.ShapeDtypeStruct((hidden, width), low)] * 2
        + [jax.ShapeDtypeStruct((steps, 1, step_width), wide)],
        scratch_shapes=[pltpu.VMEM((rows, width), wide)] * 2,
        compiler_params=params(),
        name="mlp_both_ways",
    )(a, dy, h, vec, up, down, bias.reshape(steps, 1, step_width))


def norm_parts(rows):
    center = rows - jnp.mean(rows, axis=-1, keepdims=True)
    scale = lax.rsqrt(jnp.mean(center * center, axis=-1, keepdims=True) + norm_eps)
    return center * scale, scale


def norm_back(unit, scale, gain, grad):
    inner = grad * gain
    return scale * (
        inner
        - jnp.mean(inner, axis=-1, keepdims=True)
        - unit * jnp.mean(inner * unit, axis=-1, keepdims=True)
    )


def add_rows(ref, rows, first):
    total = [jnp.sum(row, axis=0, keepdims=True) for row in rows]
    total = jnp.concatenate(total + [jnp.zeros_like(total[0])] * (8 - len(total)), axis=0)

    @pl.when(first)
    def _():
        ref[...] = total

    @pl.when(jnp.logical_not(first))
    def _():
        ref[...] += total


def gather_rows(place, local_ref, piece_refs, out_ref):
    hid_index, seq_index = place[0], place[1]
    quarter = local_ref.shape[0]
    steps, _, rows, _ = piece_refs[0].shape
    out_ref[pl.ds(pl.multiple_of(hid_index * quarter, 16), quarter), :] = local_ref[...]
    for step in range(steps):
        for number, piece_ref in enumerate(piece_refs):
            for chunk, away in enumerate(((0, 4), (2, 6), (0, 2), (4, 6))[number // 2]):
                away += number % 2
                start = (hid_index ^ (step + 1)) * quarter + (seq_index ^ away) * (2 * rows)
                start += (number // 4) * rows
                target = pl.ds(pl.multiple_of(start, 16), rows)
                out_ref[target, :] = piece_ref[step, chunk]


def project_kernel(pieces, place, x_ref, vec_ref, *refs):
    if pieces:
        w_ref, a_ref, q_ref, k_ref, v_ref = refs[pieces:]

        @pl.when(pl.program_id(0) == 0)
        def _():
            gather_rows(place, refs[0], refs[1:pieces], w_ref)

    else:
        w_ref, a_ref, q_ref, k_ref, v_ref = refs
    width = x_ref.shape[1]
    unit, _ = norm_parts(x_ref[...].astype(wide))
    first = (unit * vec_ref[0:1, :] + vec_ref[1:2, :]).astype(low)
    a_ref[...] = first
    q = (rows_by_rows(first, w_ref[0:width, :]) + vec_ref[2:3, :]).astype(low)
    q_ref[...] = (q.astype(wide) * score_scale).astype(low)
    k_ref[...] = rows_by_rows(first, w_ref[width : 2 * width, :]).astype(low)
    v = rows_by_rows(first, w_ref[2 * width : 3 * width, :]) + vec_ref[3:4, :]
    v_ref[...] = v.astype(low)


def row_tile(rows):
    return min(256, rows)


def project(place, x, vec, pieces, whole):
    rows, width = x.shape
    tile = min(512, rows)
    strip = pl.BlockSpec((tile, width), lambda i, p: (i, 0))
    fixed = lambda a: pl.BlockSpec(a.shape, lambda i, p: (0,) * len(a.shape))
    arrays = pieces if whole is None else [whole]
    matrix = jax.ShapeDtypeStruct((4 * width, width), low)
    strips = [jax.ShapeDtypeStruct((rows, width), low)] * 4
    results = pl.pallas_call(
        functools.partial(project_kernel, len(pieces)),
        grid_spec=pltpu.PrefetchScalarGridSpec(
            num_scalar_prefetch=1,
            grid=(rows // tile,),
            in_specs=[strip, fixed(vec)] + [fixed(a) for a in arrays],
            out_specs=([fixed(matrix)] if whole is None else []) + [strip] * 4,
        ),
        out_shape=([matrix] if whole is None else []) + strips,
        compiler_params=params(),
        cost_estimate=cost(10),
        name="norm_and_project",
    )(place, x, vec, *arrays)
    return results if whole is None else [whole] + list(results)


def join_kernel(o_ref, x_ref, w_ref, vec_ref, h_ref, a_ref):
    joined = x_ref[...].astype(wide) + rows_by_rows(o_ref[...], w_ref[...]) + vec_ref[4:5, :]
    h_ref[...] = joined
    unit, _ = norm_parts(joined)
    a_ref[...] = (unit * vec_ref[5:6, :] + vec_ref[6:7, :]).astype(low)


def join(o, x, w, vec):
    rows, width = x.shape
    tile = min(512, rows)
    strip = pl.BlockSpec((tile, width), lambda i: (i, 0))
    return pl.pallas_call(
        join_kernel,
        grid=(rows // tile,),
        in_specs=[
            strip,
            strip,
            pl.BlockSpec((width, width), lambda i: (3, 0)),
            pl.BlockSpec(vec.shape, lambda i: (0, 0)),
        ],
        out_specs=[strip, strip],
        out_shape=[
            jax.ShapeDtypeStruct((rows, width), wide),
            jax.ShapeDtypeStruct((rows, width), low),
        ],
        compiler_params=params(),
        cost_estimate=cost(6),
        name="join_and_norm",
    )(o, x, w, vec)


def branch_back_rows(da, h, dy, o, valid, w, vec_ref):
    unit, scale = norm_parts(h)
    dy = dy.astype(wide)
    dh = dy + norm_back(unit, scale, vec_ref[5:6, :], da)
    dt = dh.astype(low)
    do = (rows_by_cols(dt, w) * valid).astype(low)
    product = do.astype(wide) * o.astype(wide)
    width = product.shape[1]
    lane = lax.broadcasted_iota(jnp.int32, (width, 128), 0)
    head = lax.broadcasted_iota(jnp.int32, (width, 128), 1)
    pick = (lane // HEAD_DIM == head).astype(low)
    high = product.astype(low)
    rest = (product - high.astype(wide)).astype(low)
    delta = jnp.transpose(rows_by_cols(high, pick) + rows_by_cols(rest, pick))
    return dh, dt, do, delta, [da * unit, da, dt.astype(wide), dy]


def branch_back_kernel(
    da_ref, h_ref, dy_ref, o_ref, valid_ref, w_ref, vec_ref, dh_ref, dt_ref, do_ref, delta_ref, sums
):
    dh, dt, do, delta, rows = branch_back_rows(
        da_ref[...], h_ref[...], dy_ref[...], o_ref[...], valid_ref[...], w_ref[...], vec_ref
    )
    dh_ref[...] = dh
    dt_ref[...] = dt
    do_ref[...] = do
    for pair in range(delta_ref.shape[0]):
        delta_ref[pair] = delta[2 * pair : 2 * pair + 2, :]
    add_rows(sums, rows, pl.program_id(0) == 0)


def branch_back(da, h, dy, o, valid, w, vec):
    rows, width = h.shape
    tile = row_tile(rows)
    pairs = width // 128
    strip = pl.BlockSpec((tile, width), lambda i: (i, 0))
    return pl.pallas_call(
        branch_back_kernel,
        grid=(rows // tile,),
        in_specs=[
            strip,
            strip,
            strip,
            strip,
            pl.BlockSpec((tile, 1), lambda i: (i, 0)),
            pl.BlockSpec((width, width), lambda i: (3, 0)),
            pl.BlockSpec(vec.shape, lambda i: (0, 0)),
        ],
        out_specs=[
            strip,
            strip,
            strip,
            pl.BlockSpec((pairs, 2, tile), lambda i: (0, 0, i)),
            pl.BlockSpec((8, width), lambda i: (0, 0)),
        ],
        out_shape=[
            jax.ShapeDtypeStruct((rows, width), wide),
            jax.ShapeDtypeStruct((rows, width), low),
            jax.ShapeDtypeStruct((rows, width), low),
            jax.ShapeDtypeStruct((pairs, 2, rows), wide),
            jax.ShapeDtypeStruct((8, width), wide),
        ],
        compiler_params=params(),
        cost_estimate=cost(11),
        name="branch_backward",
    )(da, h, dy, o, valid, w, vec)


def mlp_rows_kernel(count, steps, place, *refs):
    a_ref, dy_ref, h_ref, o_ref, valid_ref, wo_ref, vec_ref, hb_ref, local_ref = refs[:9]
    up_refs, down_refs = refs[9 : 9 + count], refs[9 + count : 9 + 2 * count]
    out_ref, dh_ref, dt_ref, do_ref, delta_ref, sums = refs[9 + 2 * count : 15 + 2 * count]
    even_grad, odd_grad, ghb, active, inner, up, down, a_turned, dy_turned = refs[
        15 + 2 * count : 24 + 2 * count
    ]
    local_done, piece_done = refs[24 + 2 * count :]
    step = pl.program_id(0)
    seq_index = place[1]
    piece = up_refs[0].shape[1]
    units = count * piece
    share = a_turned.shape[0] // count
    tile = h_ref.shape[0]

    def local_copies():
        return [
            pltpu.make_async_copy(
                local_ref.at[matrix], target.at[pl.ds(0, units), :], local_done.at[matrix]
            )
            for matrix, target in enumerate((up, down))
        ]

    def piece_copies(number):
        copies = []
        for other in range(count):
            start = pl.multiple_of(number * units + (seq_index ^ other) * piece, 16)
            for matrix, (sources, target) in enumerate(((up_refs, up), (down_refs, down))):
                copies.append(
                    pltpu.make_async_copy(
                        sources[other].at[number - 1],
                        target.at[pl.ds(start, piece), :],
                        piece_done.at[number - 1, matrix, other],
                    )
                )
        return copies

    @pl.when(step == 0)
    def _():
        for copy in local_copies():
            copy.start()
        for number in range(1, steps):
            for copy in piece_copies(number):
                copy.start()
        for source, target in ((a_ref, a_turned), (dy_ref, dy_turned)):
            turned = jnp.transpose(source[...])
            for owner in range(count):
                start = pl.multiple_of((seq_index ^ owner) * share, 16)
                target[pl.ds(start, share), :] = turned[owner * share : (owner + 1) * share, :]
        for copy in local_copies():
            copy.wait()

    for number in range(1, steps):

        @pl.when(step == number)
        def _(number=number):
            for copy in piece_copies(number):
                copy.wait()

    @pl.when(step < steps)
    def _():
        here = pl.ds(pl.multiple_of(step * units, 128), units)
        before = rows_by_rows(a_ref[...], up[here, :]) + hb_ref[0]
        grad_active = rows_by_rows(dy_ref[...], down[here, :])
        density = 0.3989422804014327 * jnp.exp(-0.5 * before * before)
        below = 0.5 * (1.0 + lax.erf(before * 0.7071067811865476))
        active_now = (before * below).astype(low)
        inner_now = ((below + before * density) * grad_active).astype(low)
        active[:, here] = active_now
        inner[:, here] = inner_now
        ghb[0] = jnp.sum(inner_now.astype(wide), axis=0, keepdims=True)
        up_grad = rows_by_cols(a_turned[...], inner_now).astype(low)
        down_grad = rows_by_cols(dy_turned[...], active_now).astype(low)
        for other in range(count):
            part = slice(other * share, (other + 1) * share)
            target = odd_grad if other % 2 else even_grad
            target[other // 2, 0, 0] = up_grad[part, :]
            target[other // 2, 0, 1] = down_grad[part, :]

    @pl.when(step >= steps)
    def _():
        rows = pl.ds(pl.multiple_of((step - steps) * tile, 16), tile)
        out = h_ref[...] + rows_by_cols(active[rows, :], down[...]) + vec_ref[7:8, :]
        out_ref[...] = out.astype(low)
        da = rows_by_cols(inner[rows, :], up[...])
        dh, dt, do, delta, row_sums = branch_back_rows(
            da, h_ref[...], dy_ref[rows, :], o_ref[...], valid_ref[...], wo_ref[...], vec_ref
        )
        dh_ref[...] = dh
        dt_ref[...] = dt
        do_ref[...] = do
        for pair in range(delta_ref.shape[0]):
            delta_ref[pair] = delta[2 * pair : 2 * pair + 2, :]
        add_rows(sums, row_sums, step == steps)


def mlp_rows(place, a, dy, h, o, valid, w, vec, local, bias, ups, downs):
    rows, width = a.shape
    steps, count, piece = bias.shape[0], len(ups), ups[0].shape[1]
    share = width // count
    tile = row_tile(rows)
    pairs = width // 128
    hidden = steps * count * piece
    once = dict(pipeline_mode=pl.Buffered(1))
    fixed = lambda a: pl.BlockSpec(a.shape, lambda i, p: (0,) * len(a.shape), **once)
    late = lambda i: jnp.maximum(i - steps, 0)
    early = lambda i: jnp.minimum(i, steps - 1)
    strip = pl.BlockSpec((tile, width), lambda i, p: (late(i), 0))
    units = count * piece
    bias_strip = pl.BlockSpec((1, 1, units), lambda i, p: (p[0] ^ early(i), 0, 0))
    grads = pl.BlockSpec((count // 2, 1, 2, share, units), lambda i, p: (0, early(i), 0, 0, 0))
    return pl.pallas_call(
        functools.partial(mlp_rows_kernel, count, steps),
        grid_spec=pltpu.PrefetchScalarGridSpec(
            num_scalar_prefetch=1,
            grid=(steps + rows // tile,),
            in_specs=[
                fixed(a),
                fixed(dy),
                strip,
                strip,
                pl.BlockSpec((tile, 1), lambda i, p: (late(i), 0)),
                pl.BlockSpec((width, width), lambda i, p: (3, 0), **once),
                fixed(vec),
                bias_strip,
            ]
            + [in_place()] * (1 + 2 * count),
            out_specs=[
                strip,
                strip,
                strip,
                strip,
                pl.BlockSpec((pairs, 2, tile), lambda i, p: (0, 0, late(i))),
                pl.BlockSpec((8, width), lambda i, p: (0, 0)),
                grads,
                grads,
                bias_strip,
            ],
            scratch_shapes=[pltpu.VMEM((rows, hidden), low)] * 2
            + [pltpu.VMEM((hidden, width), low)] * 2
            + [pltpu.VMEM((width, rows), low)] * 2
            + [pltpu.SemaphoreType.DMA((2,)), pltpu.SemaphoreType.DMA((steps - 1, 2, count))],
        ),
        out_shape=[
            jax.ShapeDtypeStruct((rows, width), low),
            jax.ShapeDtypeStruct((rows, width), wide),
            jax.ShapeDtypeStruct((rows, width), low),
            jax.ShapeDtypeStruct((rows, width), low),
            jax.ShapeDtypeStruct((pairs, 2, rows), wide),
            jax.ShapeDtypeStruct((8, width), wide),
        ]
        + [jax.ShapeDtypeStruct((count // 2, steps, 2, share, units), low)] * 2
        + [jax.ShapeDtypeStruct(bias.shape, wide)],
        compiler_params=params(),
        cost_estimate=cost(36),
        name="mlp_both_ways",
    )(place, a, dy, h, o, valid, w, vec, bias, local, *ups, *downs)


def input_back_kernel(dq_ref, dk_ref, dv_ref, w_ref, x_ref, dh_ref, vec_ref, out_ref, sums):
    width = x_ref.shape[1]
    da = rows_by_cols(dq_ref[...], w_ref[0:width, :])
    da += rows_by_cols(dk_ref[...], w_ref[width : 2 * width, :])
    da += rows_by_cols(dv_ref[...], w_ref[2 * width : 3 * width, :])
    unit, scale = norm_parts(x_ref[...].astype(wide))
    grad = dh_ref[...] + norm_back(unit, scale, vec_ref[0:1, :], da)
    out_ref[...] = grad.astype(low)
    rows = [da * unit, da, dq_ref[...].astype(wide), dv_ref[...].astype(wide)]
    add_rows(sums, rows, pl.program_id(0) == 0)


def input_back(dq, dk, dv, w, x, dh, vec):
    rows, width = x.shape
    tile = row_tile(rows)
    strip = pl.BlockSpec((tile, width), lambda i: (i, 0))
    return pl.pallas_call(
        input_back_kernel,
        grid=(rows // tile,),
        in_specs=[
            strip,
            strip,
            strip,
            pl.BlockSpec((3 * width, width), lambda i: (0, 0)),
            strip,
            strip,
            pl.BlockSpec(vec.shape, lambda i: (0, 0)),
        ],
        out_specs=[strip, pl.BlockSpec((8, width), lambda i: (0, 0))],
        out_shape=[
            jax.ShapeDtypeStruct((rows, width), low),
            jax.ShapeDtypeStruct((8, width), wide),
        ],
        compiler_params=params(),
        cost_estimate=cost(10),
        name="input_backward",
    )(dq, dk, dv, w, x, dh, vec)


def renew_kernel(count, parts, turned, place, *refs):
    pieces = refs[:count]
    weight, moment, average = refs[count : count + 3]
    outs, grads = refs[-5:-1], refs[-1]
    block = weight.shape[1]

    @pl.when(pl.program_id(0) == 0)
    def _():
        base = 0
        for start, rows in parts:
            for other, piece in enumerate(pieces):
                first = base + (place[1] ^ other) * rows
                target = pl.ds(pl.multiple_of(first, 16), rows)
                grads[:, target, :] = piece[:, start : start + rows, :]
            base += count * rows
        if turned:
            for matrix in range(grads.shape[0]):
                grads[matrix] = jnp.transpose(grads[matrix])

    here = pl.ds(pl.multiple_of(pl.program_id(0) * block, 16), block)
    results = renew(
        weight[...],
        moment[...],
        average[...],
        grads[:, here, :].astype(wide),
        weight_decay,
        matrix_rate,
    )
    for out, value in zip(outs, results):
        out[...] = value


def renew_pieces(
    place, pieces, parts, weight, moment, average, turned=False, only=None, earlier=()
):
    matrices, rows, width = weight.shape
    count, at = (matrices, 0) if only is None else (1, only)
    steps = 4
    block = pl.BlockSpec((count, rows // steps, width), lambda i, p: (at, i, 0))
    fixed = pl.BlockSpec((count,) + pieces[0].shape[1:], lambda i, p: (at, 0, 0))
    return pl.pallas_call(
        functools.partial(renew_kernel, len(pieces), parts, turned),
        grid_spec=pltpu.PrefetchScalarGridSpec(
            num_scalar_prefetch=1,
            grid=(steps,),
            in_specs=[fixed] * len(pieces) + [block] * 3 + [in_place()] * len(earlier),
            out_specs=[block] * 4,
            scratch_shapes=[pltpu.VMEM((count, rows, width), low)],
        ),
        out_shape=[jax.ShapeDtypeStruct(weight.shape, wide)] * 4,
        input_output_aliases={4 + len(pieces) + i: i for i in range(len(earlier))},
        compiler_params=params(),
        cost_estimate=cost(10),
        name="renew_matrices",
    )(place, *pieces, weight, moment, average, *earlier)


def add_low(a, b):
    return (a.astype(wide) + b.astype(wide)).astype(low)


def fold_mlp_kernel(even_ref, other_ref, up_keep, up_send, down_keep, down_send):
    for half in range(4):
        up = add_low(even_ref[half, 0, 0], other_ref[half, 0, 0])
        down = add_low(even_ref[half, 0, 1], other_ref[half, 0, 1])
        (up_send if half % 2 else up_keep)[half // 2, 0] = up
        (down_send if half // 2 else down_keep)[half % 2, 0] = down


def fold_mlp(evens, others):
    halves, steps, matrices, piece, width = evens.shape
    block = pl.BlockSpec((halves, 1, matrices, piece, width), lambda i: (0, i, 0, 0, 0))
    part = pl.BlockSpec((2, 1, piece, width), lambda i: (0, i, 0, 0))
    return pl.pallas_call(
        fold_mlp_kernel,
        grid=(steps,),
        in_specs=[block, block],
        out_specs=[part] * 4,
        out_shape=[jax.ShapeDtypeStruct((2, steps, piece, width), low)] * 4,
        compiler_params=params(),
        cost_estimate=cost(4),
        name="fold_cores",
    )(evens, others)


def fold_chips_kernel(up, up_other, down, down_other, up_keep, up_send, down_keep, down_send):
    up_keep[...] = add_low(up[0], up_other[0])
    up_send[...] = add_low(up[1], up_other[1])
    down_keep[...] = add_low(down[0], down_other[0])
    down_send[...] = add_low(down[1], down_other[1])


def fold_chips(up, up_other, down, down_other):
    _, steps, piece, width = up.shape
    return pl.pallas_call(
        fold_chips_kernel,
        in_specs=[whole_vmem()] * 4,
        out_specs=[whole_vmem()] * 4,
        out_shape=[jax.ShapeDtypeStruct((steps, piece, width), low)] * 4,
        compiler_params=params(),
        cost_estimate=cost(4),
        name="fold_chips",
    )(up, up_other, down, down_other)


def fold_last_kernel(up, up_other, down, down_other, *outs):
    for step, out in enumerate(outs):
        out[0] = add_low(up[step], up_other[step])
        out[1] = add_low(down[step], down_other[step])


def fold_last(up, up_other, down, down_other):
    steps, piece, width = up.shape
    return pl.pallas_call(
        fold_last_kernel,
        in_specs=[whole_vmem()] * 4,
        out_specs=[whole_vmem()] * steps,
        out_shape=[jax.ShapeDtypeStruct((2, piece, width), low)] * steps,
        compiler_params=params(),
        cost_estimate=cost(3),
        name="fold_last",
    )(up, up_other, down, down_other)


def fold_kernel(halves, groups, *refs):
    evens, others, outs = refs[:groups], refs[groups : 2 * groups], refs[2 * groups :]
    for half, out in enumerate(outs):
        at = 0
        for step in range(evens[0].shape[1]):
            for even_ref, other_ref in zip(evens, others):
                rows = pl.ds(at, even_ref.shape[2])
                out[rows, :] = add_low(even_ref[half, step], other_ref[half, step])
                at += even_ref.shape[2]


def fold_pairs(evens, others):
    halves, steps, _, width = evens[0].shape
    rows = steps * sum(array.shape[2] for array in evens)
    return pl.pallas_call(
        functools.partial(fold_kernel, halves, len(evens)),
        in_specs=[whole_vmem()] * (2 * len(evens)),
        out_specs=[whole_vmem()] * halves,
        out_shape=[jax.ShapeDtypeStruct((rows, width), low)] * halves,
        compiler_params=params(),
        cost_estimate=cost(4),
        name="fold_cores",
    )(*evens, *others)


def sum_all(values):
    values = [value.astype(wide) for value in values]
    while len(values) > 1:
        values = [values[i] + values[i + 1] for i in range(0, len(values), 2)]
    return values[0].astype(low)


def sum_steps_kernel(terms, *refs):
    extra, outs = refs[terms : terms + 2], refs[terms + 2 :]
    total = sum_all([ref[...] for ref in refs[:terms]])
    tail = jnp.concatenate([ref[...] for ref in extra], axis=0).astype(low)
    rows = total.shape[0] // len(outs)
    for step, out in enumerate(outs):
        out[pl.ds(0, rows), :] = total[step * rows : (step + 1) * rows]
        out[pl.ds(rows, tail.shape[0]), :] = tail


def sum_steps(terms, steps, *extra):
    rows, width = terms[0].shape
    rows = rows // steps + sum(array.shape[0] for array in extra)
    return pl.pallas_call(
        functools.partial(sum_steps_kernel, len(terms)),
        in_specs=[whole_vmem()] * (len(terms) + 2),
        out_specs=[whole_vmem()] * steps,
        out_shape=[jax.ShapeDtypeStruct((rows, width), low)] * steps,
        compiler_params=params(),
        cost_estimate=cost(2),
        name="sum_steps",
    )(*terms, *extra)


def solution(mesh):
    seqs = mesh.shape["seq"]
    hids = mesh.shape["hid"]

    def swap(value, axis, step):
        count = mesh.shape[axis]
        return lax.ppermute(value, axis, [(i, i ^ step) for i in range(count)])

    def after(value, *others):
        return lax.optimization_barrier((value, others))[0]

    def spread_chips(array):
        return [array] + [swap(array, "seq", other) for other in range(2, seqs, 2)]

    def spread_pairs(evens):
        pieces = []
        for even in evens:
            pieces += [even, swap(even, "seq", 1)]
        return pieces

    def tree_sum(values):
        while len(values) > 1:
            values = [values[i] + values[i + 1] for i in range(0, len(values), 2)]
        return values[0]

    def hid_terms(arrays):
        return [arrays[0]] + [swap(arrays[i], "hid", i) for i in range(1, hids)]

    def seq_terms(arrays):
        return [arrays[0]] + [swap(arrays[i], "seq", 2 * i) for i in range(1, seqs // 2)]

    def exchange(array, packs, rows):
        teams = [[r * packs + b for b in range(packs)] for r in range(seqs // packs)]
        array = array.reshape(packs, rows, array.shape[-1])
        return lax.all_to_all(array, "seq", 0, 0, axis_index_groups=teams)

    def image_parts(image_lengths, packs, rows):
        seq_index = lax.axis_index("seq")
        first = (seq_index // packs) * (packs * rows)
        positions = first + jnp.arange(packs * rows, dtype=jnp.int32)
        lengths = lax.dynamic_index_in_dim(image_lengths, seq_index % packs, 0, keepdims=False)
        ends = jnp.cumsum(lengths)
        query_seg = jnp.sum((ends[None, :] <= positions[:, None]).astype(jnp.int32), axis=1)
        return query_seg, (positions < ends[-1]).astype(wide)[:, None]

    def vector_rows(small):
        return jnp.concatenate([small[:4], small[10:11], small[8:10], small[11:16]], axis=0)

    def shards_general(
        tokens_in,
        image_lengths,
        attn_weight,
        attn_moment,
        attn_average,
        mlp_weight,
        mlp_moment,
        mlp_average,
        vector_params,
        vector_moment,
        vector_average,
        out_grad,
    ):
        packs, rows, width = tokens_in.shape
        share = seqs // packs

        def across_share(array):
            return [array] + [swap(array, "seq", packs * m) for m in range(1, share)]

        place = jnp.stack([lax.axis_index("hid"), lax.axis_index("seq")]).astype(jnp.int32)
        tokens = exchange(tokens_in, packs, rows).reshape(packs * rows, width)
        grad_low = exchange(out_grad, packs, rows).reshape(packs * rows, width)
        query_seg, valid = image_parts(image_lengths, packs, rows)
        key_seg = jnp.concatenate(across_share(query_seg))
        whole_attn = lax.all_gather(attn_weight.astype(low), "hid", axis=0, tiled=True)
        whole_mlp = lax.all_gather(mlp_weight.astype(low), "hid", axis=1, tiled=True)
        whole_attn, first_low, queries, keys, values = project(
            place, tokens, vector_params, [], whole_attn
        )
        keys = jnp.concatenate(across_share(keys))
        values = jnp.concatenate(across_share(values))
        pairs = range(width // 128)
        mixed, log_total = attention_forward(
            queries, keys, values, query_seg[:, None], key_seg[None, :], valid, pairs
        )
        residual, second_low = join(mixed, tokens, whole_attn, vector_params)
        hidden_bias = vector_params[8:].reshape(-1)
        mlp_out, second_grad, up_grad, down_grad, bias_grad = mlp_plain(
            second_low,
            grad_low,
            residual,
            vector_params,
            whole_mlp[0],
            whole_mlp[1],
            hidden_bias,
        )
        block_out = exchange(mlp_out, packs, rows).astype(wide)
        mlp_grad = lax.psum_scatter(
            jnp.stack([up_grad, down_grad]), "hid", scatter_dimension=1, tiled=True
        )
        mlp_grad = lax.psum(mlp_grad, "seq").astype(wide)
        residual_grad, branch_grad, mixed_grad, delta, branch_sums = branch_back(
            second_grad, residual, grad_low, mixed, valid, whole_attn, vector_params
        )
        query_grad, key_grad, value_grad = attention_backward(
            queries,
            keys,
            values,
            mixed_grad,
            log_total,
            delta,
            query_seg[None, :],
            key_seg[:, None],
        )
        count = queries.shape[0]

        def own_share(array):
            terms = [array[:count]]
            for m in range(1, share):
                terms.append(swap(array[m * count : (m + 1) * count], "seq", packs * m))
            return sum_all(terms)

        key_grad = own_share(key_grad)
        value_grad = own_share(value_grad)
        input_grad, input_sums = input_back(
            query_grad, key_grad, value_grad, whole_attn, tokens, residual_grad, vector_params
        )
        input_grad = exchange(input_grad, packs, rows).astype(wide)
        attn_grad = [
            cols_by_cols(query_grad, first_low),
            cols_by_cols(key_grad, first_low),
            cols_by_cols(value_grad, first_low),
            cols_by_cols(branch_grad, mixed),
        ]
        attn_grad = lax.psum_scatter(
            jnp.concatenate(attn_grad).astype(low), "hid", scatter_dimension=0, tiled=True
        )
        attn_grad = lax.psum(attn_grad, "seq").astype(wide)
        small = jnp.concatenate([input_sums, branch_sums[:4], bias_grad.reshape(-1, width)])
        copies = jnp.broadcast_to(small[None], (hids * seqs,) + small.shape)
        small = jnp.sum(lax.all_to_all(copies, ("hid", "seq"), 0, 0), axis=0)
        rates = (weight_decay, matrix_rate)
        return (
            block_out,
            input_grad,
            *renew(attn_weight, attn_moment, attn_average, attn_grad, *rates),
            *renew(mlp_weight, mlp_moment, mlp_average, mlp_grad, *rates),
            *renew(
                vector_params, vector_moment, vector_average, vector_rows(small), 0.0, vector_rate
            ),
        )

    def shards(
        tokens_in,
        image_lengths,
        attn_weight,
        attn_moment,
        attn_average,
        mlp_weight,
        mlp_moment,
        mlp_average,
        vector_params,
        vector_moment,
        vector_average,
        out_grad,
    ):
        packs, rows, width = tokens_in.shape
        seq_index = lax.axis_index("seq")
        hid_index = lax.axis_index("hid")
        place = jnp.stack([hid_index, seq_index]).astype(jnp.int32)
        attn_piece = attn_weight.shape[0] // seqs
        mlp_piece = mlp_weight.shape[1] // seqs
        pairs = range(width // 128)

        def own_row(matrix, piece, other=0):
            start = (seq_index ^ other) * piece
            return lax.dynamic_slice_in_dim(matrix, start, piece, 0).astype(low)

        attn_half = attn_piece // 2
        attn_own = [own_row(attn_weight, attn_piece, other)[:attn_half] for other in (0, 4)]
        attn_own += [own_row(attn_weight, attn_piece, other)[attn_half:] for other in (0, 2)]
        attn_steps = hid_terms([jnp.stack(attn_own)] * hids)[1:]
        tokens = exchange(tokens_in, packs, rows).reshape(packs * rows, width)
        attn_low = attn_weight.astype(low)
        up_own, down_own = [own_row(matrix, mlp_piece) for matrix in mlp_weight]
        attn_steps = after(attn_steps, attn_low, up_own, down_own, tokens)
        first_here = jnp.stack([step[:2] for step in attn_steps])
        last_here = jnp.stack([step[2:] for step in attn_steps])
        attn_chips = [first_here, swap(first_here, "seq", 2), last_here, swap(last_here, "seq", 4)]
        up_here = jnp.stack(hid_terms([after(up_own, first_here)] * hids)[1:])
        query_seg, valid = image_parts(image_lengths, packs, rows)
        mlp_low = mlp_weight.astype(low)
        bias_pieces = vector_params[8:].reshape(hids, 1, seqs * mlp_piece)
        query_seg_rows, key_seg_rows = query_seg[:, None], query_seg[None, :]
        ready = (up_here, mlp_low, bias_pieces, query_seg_rows, key_seg_rows, valid)
        attn_chips = after(attn_chips, *ready)
        pieces = [attn_low] + spread_pairs(attn_chips)
        grad_low = exchange(after(out_grad, first_here), packs, rows)
        grad_low = grad_low.reshape(packs * rows, width)
        up_here = after(up_here, *attn_chips)
        up_x, up_y = swap(up_here, "seq", 2), swap(up_here, "seq", 4)
        down_steps = hid_terms([after(down_own, *attn_chips)] * hids)[1:]

        whole_attn, first_low, queries, keys, values = project(
            place, tokens, vector_params, pieces, None
        )
        down_here = jnp.stack(after(down_steps, queries))
        down_x, down_y = swap(down_here, "seq", 2), swap(down_here, "seq", 4)
        queries = after(queries, down_here)
        attended = (queries, keys, values, query_seg_rows, key_seg_rows, valid)
        half = len(pairs) // 2
        part = attention_forward(*attended, pairs[:half])
        mixed, log_total = attention_forward(*attended, pairs[half:], part)
        up_far = swap(after(up_x, mixed), "seq", 4)
        down_far = swap(after(down_y, mixed), "seq", 2)
        residual, second_low = join(mixed, tokens, whole_attn, vector_params)
        ups = [up_here, up_x, up_y, up_far]
        downs = [down_here, down_x, down_y, down_far]
        ups = after(ups[:3], mixed) + after(ups[3:], second_low)
        downs = after(downs[:3], mixed) + after(downs[3:], second_low)
        mlp_out, residual_grad, branch_grad, mixed_grad, delta, branch_sums, *mlp_grads = mlp_rows(
            place,
            second_low,
            grad_low,
            residual,
            mixed,
            valid,
            whole_attn,
            vector_params,
            mlp_low,
            bias_pieces,
            spread_pairs(ups),
            spread_pairs(downs),
        )
        even_grad, odd_grad, bias_grad = mlp_grads

        other_grad = swap(odd_grad, "seq", 1)
        block_out = exchange(mlp_out, packs, rows)
        early_rows = jnp.concatenate([branch_sums[:4], bias_grad.reshape(-1, width)])
        attended = (queries, keys, values, mixed_grad, log_total, delta)
        attended += (key_seg_rows, query_seg_rows)
        attended += (branch_grad, first_low, mixed)
        *part, first_even, first_odd = attention_grads(place, seqs, *attended, pairs[:half])
        even_grad = after(even_grad, first_even, block_out)
        up_keep, up_send, down_keep, down_send = fold_mlp(even_grad, other_grad)
        up_other = swap(up_send, "seq", 2)
        down_other = swap(down_send, "seq", 4)
        first_other = swap(first_odd, "seq", 1)
        part = after(part, up_keep)
        *part, last_even, last_odd = attention_grads(place, seqs, *attended, pairs[half:], part)
        up_keep, up_send, down_keep, down_send = fold_chips(
            after(up_keep, last_even), up_other, down_keep, down_other
        )
        up_other = swap(up_send, "seq", 4)
        down_other = swap(down_send, "seq", 2)
        last_other = swap(last_odd, "seq", 1)
        attn_folded = fold_pairs(
            after([first_even, last_even], up_keep), [first_other, last_other]
        )
        attn_terms = seq_terms(attn_folded)
        query_grad, key_grad, value_grad = after(part, attn_folded[0])
        input_grad, input_sums = input_back(
            query_grad, key_grad, value_grad, whole_attn, tokens, residual_grad, vector_params
        )
        mlp_added = fold_last(after(up_keep, input_sums), up_other, down_keep, down_other)
        mlp_terms = hid_terms(mlp_added)
        extra = input_sums.shape[0] + early_rows.shape[0]
        attn_terms = after(attn_terms, *mlp_terms[:3])
        attn_added = sum_steps(attn_terms, hids, input_sums, early_rows)
        mlp_sums = sum_all(after(mlp_terms, attn_added[0]))
        mlp_chips = spread_chips(mlp_sums)
        attn_terms = hid_terms(attn_added)
        block_out = block_out.astype(wide)
        attn_sums = sum_all(after(attn_terms, block_out))
        attn_grad = spread_chips(attn_sums)
        mlp_grad = spread_pairs(after(mlp_chips, attn_sums))
        mlp_rest = ([(0, width // seqs)], mlp_weight, mlp_moment, mlp_average, True)
        mlp_new = renew_pieces(place, mlp_grad, *mlp_rest, 0)
        attn_grad = after(attn_grad, mlp_new[0])
        input_grad = exchange(after(input_grad, *attn_grad), packs, rows)
        mlp_grad = after(mlp_grad, *attn_grad)
        mlp_new = renew_pieces(place, mlp_grad, *mlp_rest, 1, mlp_new)
        attn_grad = after(attn_grad, mlp_new[0])
        attn_grad = spread_pairs(attn_grad)
        group_rows = attn_piece // 2
        attn_new = renew_pieces(
            place,
            [piece[None] for piece in attn_grad],
            [(group * group_rows, group_rows) for group in range(2)],
            attn_weight[None],
            attn_moment[None],
            attn_average[None],
        )
        own = slice(attn_piece, attn_piece + extra)
        small = tree_sum([piece[own].astype(wide) for piece in attn_grad])
        return (
            block_out,
            after(input_grad, attn_new[0]).astype(wide),
            *[array[0] for array in attn_new],
            *mlp_new,
            *renew(
                vector_params, vector_moment, vector_average, vector_rows(small), 0.0, vector_rate
            ),
        )

    def whole(*arrays):
        pieces = [arrays[2].shape[0] // seqs, arrays[5].shape[1] // seqs]
        fits = seqs == 8 and arrays[0].shape[0] == 8 and all(n % 96 == 0 for n in pieces)
        return (shards if fits else shards_general)(*arrays)

    return jax.shard_map(
        whole,
        mesh=mesh,
        in_specs=(
            P("hid", "seq", None),
            P("hid", None),
            P("hid", None),
            P("hid", None),
            P("hid", None),
            P(None, "hid", None),
            P(None, "hid", None),
            P(None, "hid", None),
            P(),
            P(),
            P(),
            P("hid", "seq", None),
        ),
        out_specs=(
            P("hid", "seq", None),
            P("hid", "seq", None),
            P("hid", None),
            P("hid", None),
            P("hid", None),
            P("hid", None),
            P(None, "hid", None),
            P(None, "hid", None),
            P(None, "hid", None),
            P(None, "hid", None),
            P(),
            P(),
            P(),
            P(),
        ),
        check_vma=False,
    )
```

```python
import functools

import jax
import jax.numpy as jnp
from jax import lax
from jax.experimental import pallas as pl
from jax.experimental.pallas import tpu as pltpu
from jax.sharding import PartitionSpec as P

HEADS = 12
HEAD_DIM = 64

score_scale = 0.125
norm_eps = 1e-06
big_negative = -1e30
matrix_rate = 0.0001
vector_rate = 0.001
momentum_decay = 0.9
weight_decay = 0.0001
average_decay = 0.9

low = jnp.bfloat16
wide = jnp.float32
kernel_vmem = 56 * 1024 * 1024


def cost(microseconds):
    return pl.CostEstimate(
        flops=int(4e+08 * microseconds) + 1000, bytes_accessed=1000, transcendentals=0
    )


def rows_by_rows(a, b):
    return lax.dot_general(a, b, (((1,), (1,)), ((), ())), preferred_element_type=wide)


def rows_by_cols(a, b):
    return lax.dot_general(a, b, (((1,), (0,)), ((), ())), preferred_element_type=wide)


def cols_by_cols(a, b):
    return lax.dot_general(a, b, (((0,), (0,)), ((), ())), preferred_element_type=wide)


def normalize(inputs, gain_row, offset):
    center = inputs - jnp.mean(inputs, axis=-1, keepdims=True)
    spread = jnp.mean(center * center, axis=-1, keepdims=True)
    return center * lax.rsqrt(spread + norm_eps) * gain_row + offset


def renew(weight, moment, average, gradient, decay_rate, step_rate):
    step_grad = gradient + decay_rate * weight
    moment_new = momentum_decay * moment + step_grad
    weight_new = weight - step_rate * (step_grad + momentum_decay * moment_new)
    average_new = average_decay * average + (1.0 - average_decay) * weight_new
    return (gradient, moment_new, weight_new, average_new)


def params(**kwargs):
    return pltpu.CompilerParams(vmem_limit_bytes=kernel_vmem, **kwargs)


def smem():
    return pl.BlockSpec(memory_space=pltpu.SMEM)


def whole_vmem():
    return pl.BlockSpec(memory_space=pltpu.VMEM)


def in_place():
    return pl.BlockSpec(memory_space=pl.ANY)


def attention_forward_kernel(tile, q_ref, k_ref, v_ref, query_seg, key_seg, valid_ref, *refs):
    o_ref, lse_ref = refs[-2:]
    rows = q_ref.shape[0]
    lane = lax.broadcasted_iota(jnp.int32, (1, 128), 1)
    k = k_ref[...]
    v = v_ref[...]
    v_and_ones = jnp.concatenate([v, jnp.ones_like(v)], axis=1)
    for start in range(0, rows, tile):
        part = pl.ds(start, tile)
        q = q_ref[part, :]
        same = query_seg[part, :] == key_seg[...]
        heads = []
        for head in range(2):
            mine = (lane // HEAD_DIM) == head
            scores = rows_by_rows(jnp.where(mine, q, jnp.zeros_like(q)), k)
            scores = jnp.where(same, scores, big_negative)
            top = jnp.max(scores, axis=1, keepdims=True)
            weights = jnp.exp(scores - top).astype(low)
            sums = rows_by_cols(weights, v_and_ones)
            total = sums[:, 128:]
            heads.append(sums[:, :128] / total)
            lse_ref[0, head : head + 1, part] = jnp.transpose(top + jnp.log(total))[:1, :]
        joined = jnp.where(lane < HEAD_DIM, heads[0], heads[1]) * valid_ref[part, :]
        o_ref[part, :] = joined.astype(low)


def attention_forward(q, k, v, query_seg, key_seg, valid, pairs, earlier=(), after=()):
    rows, width = q.shape
    keys = k.shape[0]
    column = lambda n: pl.BlockSpec((n, 128), lambda g: (0, pairs[0] + g))
    whole = lambda a: pl.BlockSpec(a.shape, lambda g: (0, 0))
    return pl.pallas_call(
        functools.partial(attention_forward_kernel, min(128, rows)),
        grid=(len(pairs),),
        in_specs=[
            column(rows),
            column(keys),
            column(keys),
            whole(query_seg),
            whole(key_seg),
            whole(valid),
        ]
        + [in_place()] * (len(earlier) + len(after)),
        out_specs=[
            column(rows),
            pl.BlockSpec((1, 2, rows), lambda g: (pairs[0] + g, 0, 0)),
        ],
        out_shape=[
            jax.ShapeDtypeStruct((rows, width), low),
            jax.ShapeDtypeStruct((width // 128, 2, rows), wide),
        ],
        input_output_aliases={6 + i: i for i in range(len(earlier))},
        compiler_params=params(),
        cost_estimate=cost(4 * len(pairs)),
        name="attention_forward",
    )(q, k, v, query_seg, key_seg, valid, *earlier, *after)


def attention_backward_pair(
    tile, q_ref, k_ref, v_ref, do_ref, lse_ref, delta_ref, query_seg, key_seg, sums
):
    dq, dk, dv = sums
    rows = q_ref.shape[0]
    lane = lax.broadcasted_iota(jnp.int32, (1, 128), 1)
    k = k_ref[...]
    v = v_ref[...]
    k_turned = jnp.transpose(k)
    q_turned = jnp.transpose(q_ref[...])
    do_turned = jnp.transpose(do_ref[...])
    for start in range(0, rows, tile):
        part = pl.ds(start, tile)
        q = q_ref[part, :]
        do = do_ref[part, :]
        same = key_seg[...] == query_seg[:, part]
        for head in range(2):
            mine = (lane // HEAD_DIM) == head
            features = slice(head * HEAD_DIM, (head + 1) * HEAD_DIM)
            scores = rows_by_rows(k, jnp.where(mine, q, jnp.zeros_like(q)))
            scores = jnp.where(same, scores, big_negative)
            probs = jnp.exp(scores - lse_ref[0, head : head + 1, part])
            grads = rows_by_rows(v, jnp.where(mine, do, jnp.zeros_like(do)))
            grads = (probs * (grads - delta_ref[0, head : head + 1, part])).astype(low)
            here = slice(start, start + tile)
            dv_term = rows_by_rows(do_turned[features, here], probs.astype(low))
            dk_term = rows_by_rows(q_turned[features, here], grads)
            dq[features, part] = score_scale * rows_by_cols(k_turned[features, :], grads)
            if start == 0:
                dk[features, :] = dk_term
                dv[features, :] = dv_term
            else:
                dk[features, :] += dk_term
                dv[features, :] += dv_term


def attention_backward_kernel(tile, *refs):
    dq_ref, dk_ref, dv_ref, dq, dk, dv = refs[-6:]
    attention_backward_pair(tile, *refs[:8], (dq, dk, dv))
    for out, total in zip((dq_ref, dk_ref, dv_ref), (dq, dk, dv)):
        out[...] = jnp.transpose(total[...].astype(low))


def attention_backward(q, k, v, do, lse, delta, query_seg, key_seg):
    rows, width = q.shape
    keys = k.shape[0]
    pairs = width // 128
    column = lambda n: pl.BlockSpec((n, 128), lambda g: (0, g))
    whole = lambda a: pl.BlockSpec(a.shape, lambda g: (0, 0))
    stat = pl.BlockSpec((1, 2, rows), lambda g: (g, 0, 0))
    return pl.pallas_call(
        functools.partial(attention_backward_kernel, min(256, rows)),
        grid=(pairs,),
        in_specs=[
            column(rows),
            column(keys),
            column(keys),
            column(rows),
            stat,
            stat,
            whole(query_seg),
            whole(key_seg),
        ],
        out_specs=[column(rows), column(keys), column(keys)],
        out_shape=[
            jax.ShapeDtypeStruct((rows, width), low),
            jax.ShapeDtypeStruct((keys, width), low),
            jax.ShapeDtypeStruct((keys, width), low),
        ],
        scratch_shapes=[
            pltpu.VMEM((128, rows), wide),
            pltpu.VMEM((128, keys), wide),
            pltpu.VMEM((128, keys), wide),
        ],
        compiler_params=params(),
        cost_estimate=cost(6 * pairs),
        name="attention_backward",
    )(q, k, v, do, lse, delta, query_seg, key_seg)


def attention_grads_kernel(tile, seqs, place, *refs):
    dt_ref, a_ref, o_ref = refs[8:11]
    dq_ref, dk_ref, dv_ref, even_ref, odd_ref, dq, dk, dv, dq_all, dk_all, dv_all, grads = refs[-12:]
    attention_backward_pair(tile, *refs[:8], (dq, dk, dv))
    pair = pl.program_id(0)
    band = pl.ds(pl.multiple_of(pair * 128, 128), 128)
    for out, total, group in zip(
        (dq_ref, dk_ref, dv_ref), (dq, dk, dv), (dq_all, dk_all, dv_all)
    ):
        rounded = total[...].astype(low)
        out[...] = jnp.transpose(rounded)
        group[band, :] = rounded

    @pl.when(pair == pl.num_programs(0) - 1)
    def _():
        grads[0] = rows_by_cols(dq_all[...], a_ref[...]).astype(low)
        grads[1] = rows_by_cols(dk_all[...], a_ref[...]).astype(low)
        grads[2] = rows_by_cols(dv_all[...], a_ref[...]).astype(low)
        grads[3] = cols_by_cols(dt_ref[...], o_ref[...]).astype(low)
        piece = even_ref.shape[2]
        for other in range(seqs):
            source = pl.ds(pl.multiple_of((place[1] ^ other) * piece, 16), piece)
            target = odd_ref if other % 2 else even_ref
            for matrix in range(4):
                target[other // 2, matrix ^ place[0]] = grads[matrix, source, :]


def attention_grads(
    place, seqs, q, k, v, do, lse, delta, query_seg, key_seg, dt, a, o, pairs, earlier=()
):
    rows, width = q.shape
    count = len(pairs)
    piece = count * 128 // seqs
    group = pairs[0] // count
    column = pl.BlockSpec((rows, 128), lambda g, p: (0, pairs[0] + g))
    fixed = lambda a: pl.BlockSpec(a.shape, lambda g, p: (0,) * len(a.shape))
    stat = pl.BlockSpec((1, 2, rows), lambda g, p: (pairs[0] + g, 0, 0))
    grad = jax.ShapeDtypeStruct((rows, width), low)
    result = jax.ShapeDtypeStruct((seqs // 2, 4, piece, width), low)
    return pl.pallas_call(
        functools.partial(attention_grads_kernel, min(256, rows), seqs),
        grid_spec=pltpu.PrefetchScalarGridSpec(
            num_scalar_prefetch=1,
            grid=(count,),
            in_specs=[column] * 4
            + [
                stat,
                stat,
                fixed(query_seg),
                fixed(key_seg),
                pl.BlockSpec((rows, count * 128), lambda g, p: (0, group)),
                fixed(a),
                fixed(o),
            ]
            + [in_place()] * len(earlier),
            out_specs=[column] * 3 + [fixed(result)] * 2,
            scratch_shapes=[pltpu.VMEM((128, rows), wide)] * 3
            + [pltpu.VMEM((count * 128, rows), low)] * 3
            + [pltpu.VMEM((4, count * 128, width), low)],
        ),
        out_shape=[grad] * 3 + [result] * 2,
        input_output_aliases={12 + i: i for i in range(len(earlier))},
        compiler_params=params(),
        cost_estimate=cost(7 * count),
        name="attention_backward",
    )(place, q, k, v, do, lse, delta, query_seg, key_seg, dt, a, o, *earlier)


def mlp_step(a, dy, up, down, bias):
    before = rows_by_rows(a, up) + bias
    grad_active = rows_by_rows(dy, down)
    density = 0.3989422804014327 * jnp.exp(-0.5 * before * before)
    below = 0.5 * (1.0 + lax.erf(before * 0.7071067811865476))
    active = (before * below).astype(low)
    grad_before = ((below + before * density) * grad_active).astype(low)
    bias_grad = jnp.sum(grad_before.astype(wide), axis=0, keepdims=True)
    up_grad = cols_by_cols(grad_before, a)
    down_grad = cols_by_cols(active, dy)
    return (
        rows_by_cols(active, down),
        rows_by_cols(grad_before, up),
        up_grad,
        down_grad,
        bias_grad,
    )


def add_up(step, steps, h_ref, vec_ref, out_ref, da_ref, out_sum, da_sum, out_term, da_term):
    @pl.when(step == 0)
    def _():
        out_sum[...] = out_term
        da_sum[...] = da_term

    @pl.when(step > 0)
    def _():
        out_sum[...] += out_term
        da_sum[...] += da_term

    @pl.when(step == steps - 1)
    def _():
        out_ref[...] = (h_ref[...] + out_sum[...] + vec_ref[7:8, :]).astype(low)
        da_ref[...] = da_sum[...]


def mlp_plain_kernel(
    a_ref,
    dy_ref,
    h_ref,
    vec_ref,
    up_ref,
    dn_ref,
    hb_ref,
    out_ref,
    da_ref,
    gup,
    gdn,
    ghb,
    out_sum,
    da_sum,
):
    out_term, da_term, up_grad, down_grad, bias_grad = mlp_step(
        a_ref[...], dy_ref[...], up_ref[...], dn_ref[...], hb_ref[0]
    )
    gup[...] = up_grad.astype(low)
    gdn[...] = down_grad.astype(low)
    ghb[0] = bias_grad
    step, steps = pl.program_id(0), pl.num_programs(0)
    add_up(step, steps, h_ref, vec_ref, out_ref, da_ref, out_sum, da_sum, out_term, da_term)


def mlp_plain(a, dy, h, vec, up, down, bias, step_width=768):
    rows, width = a.shape
    hidden = up.shape[0]
    steps = hidden // step_width
    whole = pl.BlockSpec((rows, width), lambda i: (0, 0))
    chunk = pl.BlockSpec((step_width, width), lambda i: (i, 0))
    strip = pl.BlockSpec((1, 1, step_width), lambda i: (i, 0, 0))
    return pl.pallas_call(
        mlp_plain_kernel,
        grid=(steps,),
        in_specs=[whole, whole, whole, pl.BlockSpec(vec.shape, lambda i: (0, 0))]
        + [chunk, chunk, strip],
        out_specs=[whole, whole, chunk, chunk, strip],
        out_shape=[
            jax.ShapeDtypeStruct((rows, width), low),
            jax.ShapeDtypeStruct((rows, width), wide),
        ]
        + [jax.ShapeDtypeStruct((hidden, width), low)] * 2
        + [jax.ShapeDtypeStruct((steps, 1, step_width), wide)],
        scratch_shapes=[pltpu.VMEM((rows, width), wide)] * 2,
        compiler_params=params(),
        name="mlp_both_ways",
    )(a, dy, h, vec, up, down, bias.reshape(steps, 1, step_width))


def norm_parts(rows):
    center = rows - jnp.mean(rows, axis=-1, keepdims=True)
    scale = lax.rsqrt(jnp.mean(center * center, axis=-1, keepdims=True) + norm_eps)
    return center * scale, scale


def norm_back(unit, scale, gain, grad):
    inner = grad * gain
    return scale * (
        inner
        - jnp.mean(inner, axis=-1, keepdims=True)
        - unit * jnp.mean(inner * unit, axis=-1, keepdims=True)
    )


def add_rows(ref, rows, first):
    total = [jnp.sum(row, axis=0, keepdims=True) for row in rows]
    total = jnp.concatenate(total + [jnp.zeros_like(total[0])] * (8 - len(total)), axis=0)

    @pl.when(first)
    def _():
        ref[...] = total

    @pl.when(jnp.logical_not(first))
    def _():
        ref[...] += total


def gather_rows(place, local_ref, piece_refs, out_ref):
    hid_index, seq_index = place[0], place[1]
    quarter = local_ref.shape[0]
    steps, _, rows, _ = piece_refs[0].shape
    out_ref[pl.ds(pl.multiple_of(hid_index * quarter, 16), quarter), :] = local_ref[...]
    for step in range(steps):
        for number, piece_ref in enumerate(piece_refs):
            for chunk, away in enumerate(((0, 4), (2, 6), (0, 2), (4, 6))[number // 2]):
                away += number % 2
                start = (hid_index ^ (step + 1)) * quarter + (seq_index ^ away) * (2 * rows)
                start += (number // 4) * rows
                target = pl.ds(pl.multiple_of(start, 16), rows)
                out_ref[target, :] = piece_ref[step, chunk]


def project_kernel(pieces, place, x_ref, vec_ref, *refs):
    if pieces:
        w_ref, a_ref, q_ref, k_ref, v_ref = refs[pieces:]

        @pl.when(pl.program_id(0) == 0)
        def _():
            gather_rows(place, refs[0], refs[1:pieces], w_ref)

    else:
        w_ref, a_ref, q_ref, k_ref, v_ref = refs
    width = x_ref.shape[1]
    unit, _ = norm_parts(x_ref[...].astype(wide))
    first = (unit * vec_ref[0:1, :] + vec_ref[1:2, :]).astype(low)
    a_ref[...] = first
    q = (rows_by_rows(first, w_ref[0:width, :]) + vec_ref[2:3, :]).astype(low)
    q_ref[...] = (q.astype(wide) * score_scale).astype(low)
    k_ref[...] = rows_by_rows(first, w_ref[width : 2 * width, :]).astype(low)
    v = rows_by_rows(first, w_ref[2 * width : 3 * width, :]) + vec_ref[3:4, :]
    v_ref[...] = v.astype(low)


def row_tile(rows):
    return min(256, rows)


def project(place, x, vec, pieces, whole):
    rows, width = x.shape
    tile = min(512, rows)
    strip = pl.BlockSpec((tile, width), lambda i, p: (i, 0))
    fixed = lambda a: pl.BlockSpec(a.shape, lambda i, p: (0,) * len(a.shape))
    arrays = pieces if whole is None else [whole]
    matrix = jax.ShapeDtypeStruct((4 * width, width), low)
    strips = [jax.ShapeDtypeStruct((rows, width), low)] * 4
    results = pl.pallas_call(
        functools.partial(project_kernel, len(pieces)),
        grid_spec=pltpu.PrefetchScalarGridSpec(
            num_scalar_prefetch=1,
            grid=(rows // tile,),
            in_specs=[strip, fixed(vec)] + [fixed(a) for a in arrays],
            out_specs=([fixed(matrix)] if whole is None else []) + [strip] * 4,
        ),
        out_shape=([matrix] if whole is None else []) + strips,
        compiler_params=params(),
        cost_estimate=cost(10),
        name="norm_and_project",
    )(place, x, vec, *arrays)
    return results if whole is None else [whole] + list(results)


def join_kernel(o_ref, x_ref, w_ref, vec_ref, h_ref, a_ref):
    joined = x_ref[...].astype(wide) + rows_by_rows(o_ref[...], w_ref[...]) + vec_ref[4:5, :]
    h_ref[...] = joined
    unit, _ = norm_parts(joined)
    a_ref[...] = (unit * vec_ref[5:6, :] + vec_ref[6:7, :]).astype(low)


def join(o, x, w, vec):
    rows, width = x.shape
    tile = min(512, rows)
    strip = pl.BlockSpec((tile, width), lambda i: (i, 0))
    return pl.pallas_call(
        join_kernel,
        grid=(rows // tile,),
        in_specs=[
            strip,
            strip,
            pl.BlockSpec((width, width), lambda i: (3, 0)),
            pl.BlockSpec(vec.shape, lambda i: (0, 0)),
        ],
        out_specs=[strip, strip],
        out_shape=[
            jax.ShapeDtypeStruct((rows, width), wide),
            jax.ShapeDtypeStruct((rows, width), low),
        ],
        compiler_params=params(),
        cost_estimate=cost(6),
        name="join_and_norm",
    )(o, x, w, vec)


def branch_back_rows(da, h, dy, o, valid, w, vec_ref):
    unit, scale = norm_parts(h)
    dy = dy.astype(wide)
    dh = dy + norm_back(unit, scale, vec_ref[5:6, :], da)
    dt = dh.astype(low)
    do = (rows_by_cols(dt, w) * valid).astype(low)
    product = do.astype(wide) * o.astype(wide)
    width = product.shape[1]
    lane = lax.broadcasted_iota(jnp.int32, (width, 128), 0)
    head = lax.broadcasted_iota(jnp.int32, (width, 128), 1)
    pick = (lane // HEAD_DIM == head).astype(low)
    high = product.astype(low)
    rest = (product - high.astype(wide)).astype(low)
    delta = jnp.transpose(rows_by_cols(high, pick) + rows_by_cols(rest, pick))
    return dh, dt, do, delta, [da * unit, da, dt.astype(wide), dy]


def branch_back_kernel(
    da_ref, h_ref, dy_ref, o_ref, valid_ref, w_ref, vec_ref, dh_ref, dt_ref, do_ref, delta_ref, sums
):
    dh, dt, do, delta, rows = branch_back_rows(
        da_ref[...], h_ref[...], dy_ref[...], o_ref[...], valid_ref[...], w_ref[...], vec_ref
    )
    dh_ref[...] = dh
    dt_ref[...] = dt
    do_ref[...] = do
    for pair in range(delta_ref.shape[0]):
        delta_ref[pair] = delta[2 * pair : 2 * pair + 2, :]
    add_rows(sums, rows, pl.program_id(0) == 0)


def branch_back(da, h, dy, o, valid, w, vec):
    rows, width = h.shape
    tile = row_tile(rows)
    pairs = width // 128
    strip = pl.BlockSpec((tile, width), lambda i: (i, 0))
    return pl.pallas_call(
        branch_back_kernel,
        grid=(rows // tile,),
        in_specs=[
            strip,
            strip,
            strip,
            strip,
            pl.BlockSpec((tile, 1), lambda i: (i, 0)),
            pl.BlockSpec((width, width), lambda i: (3, 0)),
            pl.BlockSpec(vec.shape, lambda i: (0, 0)),
        ],
        out_specs=[
            strip,
            strip,
            strip,
            pl.BlockSpec((pairs, 2, tile), lambda i: (0, 0, i)),
            pl.BlockSpec((8, width), lambda i: (0, 0)),
        ],
        out_shape=[
            jax.ShapeDtypeStruct((rows, width), wide),
            jax.ShapeDtypeStruct((rows, width), low),
            jax.ShapeDtypeStruct((rows, width), low),
            jax.ShapeDtypeStruct((pairs, 2, rows), wide),
            jax.ShapeDtypeStruct((8, width), wide),
        ],
        compiler_params=params(),
        cost_estimate=cost(11),
        name="branch_backward",
    )(da, h, dy, o, valid, w, vec)


def mlp_rows_kernel(count, steps, place, *refs):
    a_ref, dy_ref, h_ref, o_ref, valid_ref, wo_ref, vec_ref, hb_ref, local_ref = refs[:9]
    up_refs, down_refs = refs[9 : 9 + count], refs[9 + count : 9 + 2 * count]
    out_ref, dh_ref, dt_ref, do_ref, delta_ref, sums = refs[9 + 2 * count : 15 + 2 * count]
    even_grad, odd_grad, ghb, active, inner, up, down, a_turned, dy_turned = refs[
        15 + 2 * count : 24 + 2 * count
    ]
    local_done, piece_done = refs[24 + 2 * count :]
    step = pl.program_id(0)
    seq_index = place[1]
    piece = up_refs[0].shape[1]
    units = count * piece
    share = a_turned.shape[0] // count
    tile = h_ref.shape[0]

    def local_copies():
        return [
            pltpu.make_async_copy(
                local_ref.at[matrix], target.at[pl.ds(0, units), :], local_done.at[matrix]
            )
            for matrix, target in enumerate((up, down))
        ]

    def piece_copies(number):
        copies = []
        for other in range(count):
            start = pl.multiple_of(number * units + (seq_index ^ other) * piece, 16)
            for matrix, (sources, target) in enumerate(((up_refs, up), (down_refs, down))):
                copies.append(
                    pltpu.make_async_copy(
                        sources[other].at[number - 1],
                        target.at[pl.ds(start, piece), :],
                        piece_done.at[number - 1, matrix, other],
                    )
                )
        return copies

    @pl.when(step == 0)
    def _():
        for copy in local_copies():
            copy.start()
        for number in range(1, steps):
            for copy in piece_copies(number):
                copy.start()
        for source, target in ((a_ref, a_turned), (dy_ref, dy_turned)):
            turned = jnp.transpose(source[...])
            for owner in range(count):
                start = pl.multiple_of((seq_index ^ owner) * share, 16)
                target[pl.ds(start, share), :] = turned[owner * share : (owner + 1) * share, :]
        for copy in local_copies():
            copy.wait()

    for number in range(1, steps):

        @pl.when(step == number)
        def _(number=number):
            for copy in piece_copies(number):
                copy.wait()

    @pl.when(step < steps)
    def _():
        here = pl.ds(pl.multiple_of(step * units, 128), units)
        before = rows_by_rows(a_ref[...], up[here, :]) + hb_ref[0]
        grad_active = rows_by_rows(dy_ref[...], down[here, :])
        density = 0.3989422804014327 * jnp.exp(-0.5 * before * before)
        below = 0.5 * (1.0 + lax.erf(before * 0.7071067811865476))
        active_now = (before * below).astype(low)
        inner_now = ((below + before * density) * grad_active).astype(low)
        active[:, here] = active_now
        inner[:, here] = inner_now
        ghb[0] = jnp.sum(inner_now.astype(wide), axis=0, keepdims=True)
        up_grad = rows_by_cols(a_turned[...], inner_now).astype(low)
        down_grad = rows_by_cols(dy_turned[...], active_now).astype(low)
        for other in range(count):
            part = slice(other * share, (other + 1) * share)
            target = odd_grad if other % 2 else even_grad
            target[other // 2, 0, 0] = up_grad[part, :]
            target[other // 2, 0, 1] = down_grad[part, :]

    @pl.when(step >= steps)
    def _():
        rows = pl.ds(pl.multiple_of((step - steps) * tile, 16), tile)
        out = h_ref[...] + rows_by_cols(active[rows, :], down[...]) + vec_ref[7:8, :]
        out_ref[...] = out.astype(low)
        da = rows_by_cols(inner[rows, :], up[...])
        dh, dt, do, delta, row_sums = branch_back_rows(
            da, h_ref[...], dy_ref[rows, :], o_ref[...], valid_ref[...], wo_ref[...], vec_ref
        )
        dh_ref[...] = dh
        dt_ref[...] = dt
        do_ref[...] = do
        for pair in range(delta_ref.shape[0]):
            delta_ref[pair] = delta[2 * pair : 2 * pair + 2, :]
        add_rows(sums, row_sums, step == steps)


def mlp_rows(place, a, dy, h, o, valid, w, vec, local, bias, ups, downs):
    rows, width = a.shape
    steps, count, piece = bias.shape[0], len(ups), ups[0].shape[1]
    share = width // count
    tile = row_tile(rows)
    pairs = width // 128
    hidden = steps * count * piece
    once = dict(pipeline_mode=pl.Buffered(1))
    fixed = lambda a: pl.BlockSpec(a.shape, lambda i, p: (0,) * len(a.shape), **once)
    late = lambda i: jnp.maximum(i - steps, 0)
    early = lambda i: jnp.minimum(i, steps - 1)
    strip = pl.BlockSpec((tile, width), lambda i, p: (late(i), 0))
    units = count * piece
    bias_strip = pl.BlockSpec((1, 1, units), lambda i, p: (p[0] ^ early(i), 0, 0))
    grads = pl.BlockSpec((count // 2, 1, 2, share, units), lambda i, p: (0, early(i), 0, 0, 0))
    return pl.pallas_call(
        functools.partial(mlp_rows_kernel, count, steps),
        grid_spec=pltpu.PrefetchScalarGridSpec(
            num_scalar_prefetch=1,
            grid=(steps + rows // tile,),
            in_specs=[
                fixed(a),
                fixed(dy),
                strip,
                strip,
                pl.BlockSpec((tile, 1), lambda i, p: (late(i), 0)),
                pl.BlockSpec((width, width), lambda i, p: (3, 0), **once),
                fixed(vec),
                bias_strip,
            ]
            + [in_place()] * (1 + 2 * count),
            out_specs=[
                strip,
                strip,
                strip,
                strip,
                pl.BlockSpec((pairs, 2, tile), lambda i, p: (0, 0, late(i))),
                pl.BlockSpec((8, width), lambda i, p: (0, 0)),
                grads,
                grads,
                bias_strip,
            ],
            scratch_shapes=[pltpu.VMEM((rows, hidden), low)] * 2
            + [pltpu.VMEM((hidden, width), low)] * 2
            + [pltpu.VMEM((width, rows), low)] * 2
            + [pltpu.SemaphoreType.DMA((2,)), pltpu.SemaphoreType.DMA((steps - 1, 2, count))],
        ),
        out_shape=[
            jax.ShapeDtypeStruct((rows, width), low),
            jax.ShapeDtypeStruct((rows, width), wide),
            jax.ShapeDtypeStruct((rows, width), low),
            jax.ShapeDtypeStruct((rows, width), low),
            jax.ShapeDtypeStruct((pairs, 2, rows), wide),
            jax.ShapeDtypeStruct((8, width), wide),
        ]
        + [jax.ShapeDtypeStruct((count // 2, steps, 2, share, units), low)] * 2
        + [jax.ShapeDtypeStruct(bias.shape, wide)],
        compiler_params=params(),
        cost_estimate=cost(36),
        name="mlp_both_ways",
    )(place, a, dy, h, o, valid, w, vec, bias, local, *ups, *downs)


def input_back_kernel(dq_ref, dk_ref, dv_ref, w_ref, x_ref, dh_ref, vec_ref, out_ref, sums):
    width = x_ref.shape[1]
    da = rows_by_cols(dq_ref[...], w_ref[0:width, :])
    da += rows_by_cols(dk_ref[...], w_ref[width : 2 * width, :])
    da += rows_by_cols(dv_ref[...], w_ref[2 * width : 3 * width, :])
    unit, scale = norm_parts(x_ref[...].astype(wide))
    grad = dh_ref[...] + norm_back(unit, scale, vec_ref[0:1, :], da)
    out_ref[...] = grad.astype(low)
    rows = [da * unit, da, dq_ref[...].astype(wide), dv_ref[...].astype(wide)]
    add_rows(sums, rows, pl.program_id(0) == 0)


def input_back(dq, dk, dv, w, x, dh, vec):
    rows, width = x.shape
    tile = row_tile(rows)
    strip = pl.BlockSpec((tile, width), lambda i: (i, 0))
    return pl.pallas_call(
        input_back_kernel,
        grid=(rows // tile,),
        in_specs=[
            strip,
            strip,
            strip,
            pl.BlockSpec((3 * width, width), lambda i: (0, 0)),
            strip,
            strip,
            pl.BlockSpec(vec.shape, lambda i: (0, 0)),
        ],
        out_specs=[strip, pl.BlockSpec((8, width), lambda i: (0, 0))],
        out_shape=[
            jax.ShapeDtypeStruct((rows, width), low),
            jax.ShapeDtypeStruct((8, width), wide),
        ],
        compiler_params=params(),
        cost_estimate=cost(10),
        name="input_backward",
    )(dq, dk, dv, w, x, dh, vec)


def renew_kernel(count, parts, turned, place, *refs):
    pieces = refs[:count]
    weight, moment, average = refs[count : count + 3]
    outs, grads = refs[-5:-1], refs[-1]
    block = weight.shape[1]

    @pl.when(pl.program_id(0) == 0)
    def _():
        base = 0
        for start, rows in parts:
            for other, piece in enumerate(pieces):
                first = base + (place[1] ^ other) * rows
                target = pl.ds(pl.multiple_of(first, 16), rows)
                grads[:, target, :] = piece[:, start : start + rows, :]
            base += count * rows
        if turned:
            for matrix in range(grads.shape[0]):
                grads[matrix] = jnp.transpose(grads[matrix])

    here = pl.ds(pl.multiple_of(pl.program_id(0) * block, 16), block)
    results = renew(
        weight[...],
        moment[...],
        average[...],
        grads[:, here, :].astype(wide),
        weight_decay,
        matrix_rate,
    )
    for out, value in zip(outs, results):
        out[...] = value


def renew_pieces(
    place, pieces, parts, weight, moment, average, turned=False, only=None, earlier=()
):
    matrices, rows, width = weight.shape
    count, at = (matrices, 0) if only is None else (1, only)
    steps = 4
    block = pl.BlockSpec((count, rows // steps, width), lambda i, p: (at, i, 0))
    fixed = pl.BlockSpec((count,) + pieces[0].shape[1:], lambda i, p: (at, 0, 0))
    return pl.pallas_call(
        functools.partial(renew_kernel, len(pieces), parts, turned),
        grid_spec=pltpu.PrefetchScalarGridSpec(
            num_scalar_prefetch=1,
            grid=(steps,),
            in_specs=[fixed] * len(pieces) + [block] * 3 + [in_place()] * len(earlier),
            out_specs=[block] * 4,
            scratch_shapes=[pltpu.VMEM((count, rows, width), low)],
        ),
        out_shape=[jax.ShapeDtypeStruct(weight.shape, wide)] * 4,
        input_output_aliases={4 + len(pieces) + i: i for i in range(len(earlier))},
        compiler_params=params(),
        cost_estimate=cost(10),
        name="renew_matrices",
    )(place, *pieces, weight, moment, average, *earlier)


def add_low(a, b):
    return (a.astype(wide) + b.astype(wide)).astype(low)


def fold_mlp_kernel(even_ref, other_ref, up_keep, up_send, down_keep, down_send):
    for half in range(4):
        up = add_low(even_ref[half, 0, 0], other_ref[half, 0, 0])
        down = add_low(even_ref[half, 0, 1], other_ref[half, 0, 1])
        (up_send if half % 2 else up_keep)[half // 2, 0] = up
        (down_send if half // 2 else down_keep)[half % 2, 0] = down


def fold_mlp(evens, others):
    halves, steps, matrices, piece, width = evens.shape
    block = pl.BlockSpec((halves, 1, matrices, piece, width), lambda i: (0, i, 0, 0, 0))
    part = pl.BlockSpec((2, 1, piece, width), lambda i: (0, i, 0, 0))
    return pl.pallas_call(
        fold_mlp_kernel,
        grid=(steps,),
        in_specs=[block, block],
        out_specs=[part] * 4,
        out_shape=[jax.ShapeDtypeStruct((2, steps, piece, width), low)] * 4,
        compiler_params=params(),
        cost_estimate=cost(4),
        name="fold_cores",
    )(evens, others)


def fold_chips_kernel(up, up_other, down, down_other, up_keep, up_send, down_keep, down_send):
    up_keep[...] = add_low(up[0], up_other[0])
    up_send[...] = add_low(up[1], up_other[1])
    down_keep[...] = add_low(down[0], down_other[0])
    down_send[...] = add_low(down[1], down_other[1])


def fold_chips(up, up_other, down, down_other):
    _, steps, piece, width = up.shape
    return pl.pallas_call(
        fold_chips_kernel,
        in_specs=[whole_vmem()] * 4,
        out_specs=[whole_vmem()] * 4,
        out_shape=[jax.ShapeDtypeStruct((steps, piece, width), low)] * 4,
        compiler_params=params(),
        cost_estimate=cost(4),
        name="fold_chips",
    )(up, up_other, down, down_other)


def fold_last_kernel(up, up_other, down, down_other, *outs):
    for step, out in enumerate(outs):
        out[0] = add_low(up[step], up_other[step])
        out[1] = add_low(down[step], down_other[step])


def fold_last(up, up_other, down, down_other):
    steps, piece, width = up.shape
    return pl.pallas_call(
        fold_last_kernel,
        in_specs=[whole_vmem()] * 4,
        out_specs=[whole_vmem()] * steps,
        out_shape=[jax.ShapeDtypeStruct((2, piece, width), low)] * steps,
        compiler_params=params(),
        cost_estimate=cost(3),
        name="fold_last",
    )(up, up_other, down, down_other)


def fold_kernel(halves, groups, *refs):
    evens, others, outs = refs[:groups], refs[groups : 2 * groups], refs[2 * groups :]
    for half, out in enumerate(outs):
        at = 0
        for step in range(evens[0].shape[1]):
            for even_ref, other_ref in zip(evens, others):
                rows = pl.ds(at, even_ref.shape[2])
                out[rows, :] = add_low(even_ref[half, step], other_ref[half, step])
                at += even_ref.shape[2]


def fold_pairs(evens, others):
    halves, steps, _, width = evens[0].shape
    rows = steps * sum(array.shape[2] for array in evens)
    return pl.pallas_call(
        functools.partial(fold_kernel, halves, len(evens)),
        in_specs=[whole_vmem()] * (2 * len(evens)),
        out_specs=[whole_vmem()] * halves,
        out_shape=[jax.ShapeDtypeStruct((rows, width), low)] * halves,
        compiler_params=params(),
        cost_estimate=cost(4),
        name="fold_cores",
    )(*evens, *others)


def sum_all(values):
    values = [value.astype(wide) for value in values]
    while len(values) > 1:
        values = [values[i] + values[i + 1] for i in range(0, len(values), 2)]
    return values[0].astype(low)


def sum_steps_kernel(terms, *refs):
    extra, outs = refs[terms : terms + 2], refs[terms + 2 :]
    total = sum_all([ref[...] for ref in refs[:terms]])
    tail = jnp.concatenate([ref[...] for ref in extra], axis=0).astype(low)
    rows = total.shape[0] // len(outs)
    for step, out in enumerate(outs):
        out[pl.ds(0, rows), :] = total[step * rows : (step + 1) * rows]
        out[pl.ds(rows, tail.shape[0]), :] = tail


def sum_steps(terms, steps, *extra):
    rows, width = terms[0].shape
    rows = rows // steps + sum(array.shape[0] for array in extra)
    return pl.pallas_call(
        functools.partial(sum_steps_kernel, len(terms)),
        in_specs=[whole_vmem()] * (len(terms) + 2),
        out_specs=[whole_vmem()] * steps,
        out_shape=[jax.ShapeDtypeStruct((rows, width), low)] * steps,
        compiler_params=params(),
        cost_estimate=cost(2),
        name="sum_steps",
    )(*terms, *extra)


def solution(mesh):
    seqs = mesh.shape["seq"]
    hids = mesh.shape["hid"]

    def swap(value, axis, step):
        count = mesh.shape[axis]
        return lax.ppermute(value, axis, [(i, i ^ step) for i in range(count)])

    def after(value, *others):
        return lax.optimization_barrier((value, others))[0]

    def spread_chips(array):
        return [array] + [swap(array, "seq", other) for other in range(2, seqs, 2)]

    def spread_pairs(evens):
        pieces = []
        for even in evens:
            pieces += [even, swap(even, "seq", 1)]
        return pieces

    def tree_sum(values):
        while len(values) > 1:
            values = [values[i] + values[i + 1] for i in range(0, len(values), 2)]
        return values[0]

    def hid_terms(arrays):
        return [arrays[0]] + [swap(arrays[i], "hid", i) for i in range(1, hids)]

    def seq_terms(arrays):
        return [arrays[0]] + [swap(arrays[i], "seq", 2 * i) for i in range(1, seqs // 2)]

    def exchange(array, packs, rows):
        teams = [[r * packs + b for b in range(packs)] for r in range(seqs // packs)]
        array = array.reshape(packs, rows, array.shape[-1])
        return lax.all_to_all(array, "seq", 0, 0, axis_index_groups=teams)

    def image_parts(image_lengths, packs, rows):
        seq_index = lax.axis_index("seq")
        first = (seq_index // packs) * (packs * rows)
        positions = first + jnp.arange(packs * rows, dtype=jnp.int32)
        lengths = lax.dynamic_index_in_dim(image_lengths, seq_index % packs, 0, keepdims=False)
        ends = jnp.cumsum(lengths)
        query_seg = jnp.sum((ends[None, :] <= positions[:, None]).astype(jnp.int32), axis=1)
        return query_seg, (positions < ends[-1]).astype(wide)[:, None]

    def vector_rows(small):
        return jnp.concatenate([small[:4], small[10:11], small[8:10], small[11:16]], axis=0)

    def shards_general(
        tokens_in,
        image_lengths,
        attn_weight,
        attn_moment,
        attn_average,
        mlp_weight,
        mlp_moment,
        mlp_average,
        vector_params,
        vector_moment,
        vector_average,
        out_grad,
    ):
        packs, rows, width = tokens_in.shape
        share = seqs // packs

        def across_share(array):
            return [array] + [swap(array, "seq", packs * m) for m in range(1, share)]

        place = jnp.stack([lax.axis_index("hid"), lax.axis_index("seq")]).astype(jnp.int32)
        tokens = exchange(tokens_in, packs, rows).reshape(packs * rows, width)
        grad_low = exchange(out_grad, packs, rows).reshape(packs * rows, width)
        query_seg, valid = image_parts(image_lengths, packs, rows)
        key_seg = jnp.concatenate(across_share(query_seg))
        whole_attn = lax.all_gather(attn_weight.astype(low), "hid", axis=0, tiled=True)
        whole_mlp = lax.all_gather(mlp_weight.astype(low), "hid", axis=1, tiled=True)
        whole_attn, first_low, queries, keys, values = project(
            place, tokens, vector_params, [], whole_attn
        )
        keys = jnp.concatenate(across_share(keys))
        values = jnp.concatenate(across_share(values))
        pairs = range(width // 128)
        mixed, log_total = attention_forward(
            queries, keys, values, query_seg[:, None], key_seg[None, :], valid, pairs
        )
        residual, second_low = join(mixed, tokens, whole_attn, vector_params)
        hidden_bias = vector_params[8:].reshape(-1)
        mlp_out, second_grad, up_grad, down_grad, bias_grad = mlp_plain(
            second_low,
            grad_low,
            residual,
            vector_params,
            whole_mlp[0],
            whole_mlp[1],
            hidden_bias,
        )
        block_out = exchange(mlp_out, packs, rows).astype(wide)
        mlp_grad = lax.psum_scatter(
            jnp.stack([up_grad, down_grad]), "hid", scatter_dimension=1, tiled=True
        )
        mlp_grad = lax.psum(mlp_grad, "seq").astype(wide)
        residual_grad, branch_grad, mixed_grad, delta, branch_sums = branch_back(
            second_grad, residual, grad_low, mixed, valid, whole_attn, vector_params
        )
        query_grad, key_grad, value_grad = attention_backward(
            queries,
            keys,
            values,
            mixed_grad,
            log_total,
            delta,
            query_seg[None, :],
            key_seg[:, None],
        )
        count = queries.shape[0]

        def own_share(array):
            terms = [array[:count]]
            for m in range(1, share):
                terms.append(swap(array[m * count : (m + 1) * count], "seq", packs * m))
            return sum_all(terms)

        key_grad = own_share(key_grad)
        value_grad = own_share(value_grad)
        input_grad, input_sums = input_back(
            query_grad, key_grad, value_grad, whole_attn, tokens, residual_grad, vector_params
        )
        input_grad = exchange(input_grad, packs, rows).astype(wide)
        attn_grad = [
            cols_by_cols(query_grad, first_low),
            cols_by_cols(key_grad, first_low),
            cols_by_cols(value_grad, first_low),
            cols_by_cols(branch_grad, mixed),
        ]
        attn_grad = lax.psum_scatter(
            jnp.concatenate(attn_grad).astype(low), "hid", scatter_dimension=0, tiled=True
        )
        attn_grad = lax.psum(attn_grad, "seq").astype(wide)
        small = jnp.concatenate([input_sums, branch_sums[:4], bias_grad.reshape(-1, width)])
        copies = jnp.broadcast_to(small[None], (hids * seqs,) + small.shape)
        small = jnp.sum(lax.all_to_all(copies, ("hid", "seq"), 0, 0), axis=0)
        rates = (weight_decay, matrix_rate)
        return (
            block_out,
            input_grad,
            *renew(attn_weight, attn_moment, attn_average, attn_grad, *rates),
            *renew(mlp_weight, mlp_moment, mlp_average, mlp_grad, *rates),
            *renew(
                vector_params, vector_moment, vector_average, vector_rows(small), 0.0, vector_rate
            ),
        )

    def shards(
        tokens_in,
        image_lengths,
        attn_weight,
        attn_moment,
        attn_average,
        mlp_weight,
        mlp_moment,
        mlp_average,
        vector_params,
        vector_moment,
        vector_average,
        out_grad,
    ):
        packs, rows, width = tokens_in.shape
        seq_index = lax.axis_index("seq")
        hid_index = lax.axis_index("hid")
        place = jnp.stack([hid_index, seq_index]).astype(jnp.int32)
        attn_piece = attn_weight.shape[0] // seqs
        mlp_piece = mlp_weight.shape[1] // seqs
        pairs = range(width // 128)

        def own_row(matrix, piece, other=0):
            start = (seq_index ^ other) * piece
            return lax.dynamic_slice_in_dim(matrix, start, piece, 0).astype(low)

        attn_half = attn_piece // 2
        attn_own = [own_row(attn_weight, attn_piece, other)[:attn_half] for other in (0, 4)]
        attn_own += [own_row(attn_weight, attn_piece, other)[attn_half:] for other in (0, 2)]
        attn_steps = hid_terms([jnp.stack(attn_own)] * hids)[1:]
        tokens = exchange(tokens_in, packs, rows).reshape(packs * rows, width)
        attn_low = attn_weight.astype(low)
        up_own, down_own = [own_row(matrix, mlp_piece) for matrix in mlp_weight]
        attn_steps = after(attn_steps, attn_low, up_own, down_own, tokens)
        first_here = jnp.stack([step[:2] for step in attn_steps])
        last_here = jnp.stack([step[2:] for step in attn_steps])
        attn_chips = [first_here, swap(first_here, "seq", 2), last_here, swap(last_here, "seq", 4)]
        up_here = jnp.stack(hid_terms([after(up_own, first_here)] * hids)[1:])
        query_seg, valid = image_parts(image_lengths, packs, rows)
        mlp_low = mlp_weight.astype(low)
        bias_pieces = vector_params[8:].reshape(hids, 1, seqs * mlp_piece)
        query_seg_rows, key_seg_rows = query_seg[:, None], query_seg[None, :]
        ready = (up_here, mlp_low, bias_pieces, query_seg_rows, key_seg_rows, valid)
        attn_chips = after(attn_chips, *ready)
        pieces = [attn_low] + spread_pairs(attn_chips)
        grad_low = exchange(after(out_grad, first_here), packs, rows)
        grad_low = grad_low.reshape(packs * rows, width)
        down_steps = hid_terms([after(down_own, *attn_chips)] * hids)[1:]

        whole_attn, first_low, queries, keys, values = project(
            place, tokens, vector_params, pieces, None
        )
        up_here = after(up_here, queries)
        up_x, up_y = swap(up_here, "seq", 2), swap(up_here, "seq", 4)
        down_here = jnp.stack(after(down_steps, queries))
        down_x, down_y = swap(down_here, "seq", 2), swap(down_here, "seq", 4)
        queries = after(queries, down_here)
        attended = (queries, keys, values, query_seg_rows, key_seg_rows, valid)
        half = len(pairs) // 2
        part = attention_forward(*attended, pairs[:half])
        mixed, log_total = attention_forward(*attended, pairs[half:], part)
        up_far = swap(after(up_x, mixed), "seq", 4)
        down_far = swap(after(down_y, mixed), "seq", 2)
        residual, second_low = join(mixed, tokens, whole_attn, vector_params)
        ups = [up_here, up_x, up_y, up_far]
        downs = [down_here, down_x, down_y, down_far]
        ups = after(ups[:3], mixed) + after(ups[3:], second_low)
        downs = after(downs[:3], mixed) + after(downs[3:], second_low)
        mlp_out, residual_grad, branch_grad, mixed_grad, delta, branch_sums, *mlp_grads = mlp_rows(
            place,
            second_low,
            grad_low,
            residual,
            mixed,
            valid,
            whole_attn,
            vector_params,
            mlp_low,
            bias_pieces,
            spread_pairs(ups),
            spread_pairs(downs),
        )
        even_grad, odd_grad, bias_grad = mlp_grads

        other_grad = swap(odd_grad, "seq", 1)
        block_out = exchange(mlp_out, packs, rows)
        early_rows = jnp.concatenate([branch_sums[:4], bias_grad.reshape(-1, width)])
        attended = (queries, keys, values, mixed_grad, log_total, delta)
        attended += (key_seg_rows, query_seg_rows)
        attended += (branch_grad, first_low, mixed)
        *part, first_even, first_odd = attention_grads(place, seqs, *attended, pairs[:half])
        even_grad = after(even_grad, first_even, block_out)
        up_keep, up_send, down_keep, down_send = fold_mlp(even_grad, other_grad)
        up_other = swap(up_send, "seq", 2)
        down_other = swap(down_send, "seq", 4)
        first_other = swap(first_odd, "seq", 1)
        part = after(part, up_keep)
        *part, last_even, last_odd = attention_grads(place, seqs, *attended, pairs[half:], part)
        up_keep, up_send, down_keep, down_send = fold_chips(
            after(up_keep, last_even), up_other, down_keep, down_other
        )
        up_other = swap(up_send, "seq", 4)
        down_other = swap(down_send, "seq", 2)
        last_other = swap(last_odd, "seq", 1)
        attn_folded = fold_pairs(
            after([first_even, last_even], up_keep), [first_other, last_other]
        )
        attn_terms = seq_terms(attn_folded)
        query_grad, key_grad, value_grad = after(part, attn_folded[0])
        input_grad, input_sums = input_back(
            query_grad, key_grad, value_grad, whole_attn, tokens, residual_grad, vector_params
        )
        mlp_added = fold_last(after(up_keep, input_sums), up_other, down_keep, down_other)
        mlp_terms = hid_terms(mlp_added)
        extra = input_sums.shape[0] + early_rows.shape[0]
        attn_terms = after(attn_terms, *mlp_terms[:3])
        attn_added = sum_steps(attn_terms, hids, input_sums, early_rows)
        mlp_sums = sum_all(after(mlp_terms, attn_added[0]))
        mlp_chips = spread_chips(mlp_sums)
        attn_terms = hid_terms(attn_added)
        block_out = block_out.astype(wide)
        attn_sums = sum_all(after(attn_terms, block_out))
        attn_grad = spread_chips(attn_sums)
        mlp_grad = spread_pairs(after(mlp_chips, attn_sums))
        mlp_rest = ([(0, width // seqs)], mlp_weight, mlp_moment, mlp_average, True)
        mlp_new = renew_pieces(place, mlp_grad, *mlp_rest, 0)
        attn_grad = after(attn_grad, mlp_new[0])
        input_grad = exchange(after(input_grad, *attn_grad), packs, rows)
        mlp_grad = after(mlp_grad, *attn_grad)
        mlp_new = renew_pieces(place, mlp_grad, *mlp_rest, 1, mlp_new)
        attn_grad = after(attn_grad, mlp_new[0])
        attn_grad = spread_pairs(attn_grad)
        group_rows = attn_piece // 2
        attn_new = renew_pieces(
            place,
            [piece[None] for piece in attn_grad],
            [(group * group_rows, group_rows) for group in range(2)],
            attn_weight[None],
            attn_moment[None],
            attn_average[None],
        )
        own = slice(attn_piece, attn_piece + extra)
        small = tree_sum([piece[own].astype(wide) for piece in attn_grad])
        return (
            block_out,
            after(input_grad, attn_new[0]).astype(wide),
            *[array[0] for array in attn_new],
            *mlp_new,
            *renew(
                vector_params, vector_moment, vector_average, vector_rows(small), 0.0, vector_rate
            ),
        )

    def whole(*arrays):
        pieces = [arrays[2].shape[0] // seqs, arrays[5].shape[1] // seqs]
        fits = seqs == 8 and arrays[0].shape[0] == 8 and all(n % 96 == 0 for n in pieces)
        return (shards if fits else shards_general)(*arrays)

    return jax.shard_map(
        whole,
        mesh=mesh,
        in_specs=(
            P("hid", "seq", None),
            P("hid", None),
            P("hid", None),
            P("hid", None),
            P("hid", None),
            P(None, "hid", None),
            P(None, "hid", None),
            P(None, "hid", None),
            P(),
            P(),
            P(),
            P("hid", "seq", None),
        ),
        out_specs=(
            P("hid", "seq", None),
            P("hid", "seq", None),
            P("hid", None),
            P("hid", None),
            P("hid", None),
            P("hid", None),
            P(None, "hid", None),
            P(None, "hid", None),
            P(None, "hid", None),
            P(None, "hid", None),
            P(),
            P(),
            P(),
            P(),
        ),
        check_vma=False,
    )
```
